32 devices in a mesh: mon: 8 (over z, y), out: 4 (over x, core).
Axes of the slice: x: 2, y: 2, z: 4, core: 2. Of those that a mesh axis runs over, the one named last changes fastest.
Arguments:
- mon_flow: bfloat16 [3072, 128], P('mon'), may hold values from -2.5 to 2.5
- out_flow: bfloat16 [4, 4096, 128], P('out', 'mon'), may hold values from -2.5 to 2.5
- rating: float32 [3072], P('mon'), may hold values from 1 to 3
- weights: float32 [128], replicated, may hold values from 0.25 to 1
- lodf: bfloat16 [8, 4, 8, 128, 128], P('mon', 'out'), may hold values from -1 to 1
- tile_mon: int32 [8, 4, 8], P('mon', 'out'), may hold values from 0 to 2
- tile_out: int32 [8, 4, 8], P('mon', 'out'), may hold values from 0 to 31
- tile_count: int32 [8, 4], P('mon', 'out'), may hold values from 1 to 8, as said below
Outputs:
- grad_mon: float32 [3072, 128], P(('mon', 'out'))
- grad_out: float32 [4, 4096, 128], P('out', 'mon')
The draws below stay inside these ranges and needn't reach their ends.
Inputs may be any that keep to these rules, and one draw needn't show every extreme that they name: `tile_count`: each device has 1 to 8 live slots; some device has exactly 8 in every draw.
All inputs are finite; a program needn't handle non-finite values.
Results may differ from the reference program's by a relative error of at most 0.00085.
Values may be sent and summed in bfloat16 or wider, within the bound.
No kernel may reach another device: no remote copies, remote signals or barrier semaphores. Data moves between devices by JAX's collectives and lax.ppermute only.
A program may use at most 64 MiB of HBM per device.

```python
import math
import jax
import jax.numpy as jnp
from jax import lax

BLK = 128
S = 128
MB_DEV = 3
KB_DEV = 32
SLOTS = 8
M = 3072
KDEV = 4096
N_MON = 8
N_OUT = 4


def draw_tile_count(key, part):
    first = jax.random.fold_in(key, 11)
    second = jax.random.fold_in(key, 12)
    third = jax.random.fold_in(key, 13)
    base = jax.random.randint(first, (N_MON, N_OUT), 1, SLOTS // 2 + 1)
    heavy = jax.random.randint(second, (N_MON, N_OUT), 0, 8) == 0
    chosen = jax.random.randint(third, (), 0, N_MON * N_OUT)
    flat_ids = jnp.arange(N_MON * N_OUT, dtype=jnp.int32).reshape(N_MON, N_OUT)
    heavy = jnp.logical_or(heavy, flat_ids == chosen)
    return jnp.where(heavy, SLOTS, base).astype(jnp.int32)


def with_ends(entries, stream_key, smallest, top_value):
    place = [jax.random.randint(jax.random.fold_in(stream_key, axis), (), 0, length) for axis, length in enumerate(entries.shape)]
    widest = entries.shape.index(max(entries.shape))
    beside = place[:widest] + [(place[widest] + 1) % entries.shape[widest]] + place[widest + 1:]
    return entries.at[tuple(place)].set(smallest).at[tuple(beside)].set(top_value)


def block_scale(own_key, shape, shards, low, top_value):
    loudness = 1.0
    for dim, shards_of in shards:
        heights = jax.random.uniform(jax.random.fold_in(jax.random.fold_in(own_key, 6), dim), (shards_of,), jnp.float32, low / len(shards), top_value / len(shards))
        loudness = loudness * jnp.repeat(jnp.exp(heights), shape[dim] // shards_of).reshape((-1,) + (1,) * (len(shape) - 1 - dim))
    return loudness


def scatter_about(key, dims, spread, limit, shards=(), kind=jnp.bfloat16):
    level = block_scale(key, dims, shards, -0.22, 0.18) if shards else 1.0
    entries = jax.random.normal(key, dims, jnp.float32) * spread * level
    return jnp.minimum(jnp.maximum(entries, -limit), limit).astype(kind)


def setup_inputs(seed: int = 0) -> dict:
    key_of = jax.random.split(jax.random.key(seed), 9)
    mon_flow = scatter_about(key_of[0], (M, S), 0.5, 2.5, ((0, 8),))
    out_flow = scatter_about(key_of[1], (N_OUT, KDEV, S), 0.5, 2.5, ((0, 4), (1, 8)))
    rating = jnp.clip(jnp.exp(math.log(3.0) - 1.0986123 * jax.random.uniform(key_of[2], (M,), jnp.float32) ** block_scale(key_of[2], (M,), ((0, 8),), -0.2, 0.2)), 1.0, 3.0)
    weights = jnp.clip(jnp.exp(jax.random.uniform(key_of[3], (S,), jnp.float32, math.log(0.25), math.log(1.0))), 0.25, 1.0)
    lodf = scatter_about(key_of[4], (N_MON, N_OUT, SLOTS, BLK, BLK), 0.25, 1.0, ((0, 8), (1, 4)))
    tile_mon = with_ends(jax.random.randint(key_of[5], (N_MON, N_OUT, SLOTS), 0, MB_DEV), jax.random.fold_in(key_of[5], 1), 0, MB_DEV - 1).astype(jnp.int32)
    tile_out = with_ends(jax.random.randint(key_of[6], (N_MON, N_OUT, SLOTS), 0, KB_DEV), jax.random.fold_in(key_of[6], 1), 0, KB_DEV - 1).astype(jnp.int32)
    tile_count = draw_tile_count(jax.random.fold_in(key_of[8], 71), 0)
    return dict(mon_flow=mon_flow, out_flow=out_flow, rating=rating, weights=weights, lodf=lodf, tile_mon=tile_mon, tile_out=tile_out, tile_count=tile_count)


def tile_grads(lodf_tile, mon_block, out_block, rating_rows, weights):
    coupling = lodf_tile.astype(jnp.float32)
    post_flow = mon_block.astype(jnp.float32)[:, None, :] + coupling[:, :, None] * out_block.astype(jnp.float32)[None, :, :]
    inverse = 1.0 / (rating_rows * rating_rows)
    excess = post_flow * post_flow * inverse[:, None, None] - 1.0
    derivative = jax.nn.softplus(excess) * jax.nn.sigmoid(excess) * post_flow
    derivative = derivative * (4.0 / coupling.shape[0]) * inverse[:, None, None] * weights[None, None, :]
    return jnp.sum(derivative, axis=1), jnp.sum(coupling[:, :, None] * derivative, axis=0)


def reference(mon_flow, out_flow, rating, weights, lodf, tile_mon, tile_out, tile_count):
    width = lodf.shape[-1]
    scen = mon_flow.shape[1]
    mon_total = jnp.zeros(mon_flow.shape, jnp.float32)
    out_total = jnp.zeros(out_flow.shape, jnp.float32)

    def visit(totals, flat_index):
        mon_dev = flat_index // (N_OUT * SLOTS)
        remainder = flat_index % (N_OUT * SLOTS)
        out_dev = remainder // SLOTS
        slot_index = remainder % SLOTS
        live = slot_index < tile_count[mon_dev, out_dev]

        def work(inner):
            mon_part, out_part = inner
            start = ((mon_dev * MB_DEV + tile_mon[mon_dev, out_dev, slot_index]) * width).astype(jnp.int32)
            out_start = (tile_out[mon_dev, out_dev, slot_index] * width).astype(jnp.int32)
            mon_rows = lax.dynamic_slice_in_dim(mon_flow, start, width, 0)
            rating_rows = lax.dynamic_slice_in_dim(rating, start, width, 0)
            out_rows = lax.dynamic_slice(out_flow, (out_dev.astype(jnp.int32), out_start, jnp.int32(0)), (1, width, scen))[0]
            grad_m, grad_k = tile_grads(lodf[mon_dev, out_dev, slot_index], mon_rows, out_rows, rating_rows, weights)
            old_m = lax.dynamic_slice_in_dim(mon_part, start, width, 0)
            mon_part = lax.dynamic_update_slice_in_dim(mon_part, old_m + grad_m, start, 0)
            corner = (out_dev.astype(jnp.int32), out_start, jnp.int32(0))
            old_k = lax.dynamic_slice(out_part, corner, (1, width, scen))
            out_part = lax.dynamic_update_slice(out_part, old_k + grad_k[None], corner)
            return (mon_part, out_part)

        def skip(inner):
            return inner

        return lax.cond(live, work, skip, totals), None

    totals, unused = lax.scan(visit, (mon_total, out_total), jnp.arange(N_MON * N_OUT * SLOTS, dtype=jnp.int32))
    return totals[0], totals[1]
```

```python
import math

import jax
import jax.numpy as jnp
from jax import lax
from jax.experimental import pallas as pl
from jax.experimental.pallas import tpu as pltpu
from jax.sharding import PartitionSpec as P

LOG2E = 1.0 / math.log(2.0)
ROOT = math.sqrt(LOG2E)
GROUP = 8


def tiles_kernel(
    count_ref, mon_ref, out_ref, blocks_ref, lodf_ref, base_ref, inverse_ref, weight_ref,
    grad_mon_ref, grad_out_ref, ratio_ref, flow_ref
):
    width = lodf_ref.shape[-1]
    scen = base_ref.shape[-1]
    grad_mon_ref[...] = jnp.zeros_like(grad_mon_ref)
    grad_out_ref[...] = jnp.zeros_like(grad_out_ref)
    weight = weight_ref[...] * (4.0 / width / LOG2E)

    def one_tile(slot, unused):
        rows = pl.ds(pl.multiple_of(mon_ref[slot] * width, width), width)
        block = out_ref[slot]
        out_row = block * width
        ratio_ref[...] = lodf_ref[slot].astype(jnp.float32) * inverse_ref[rows, :]
        flow_ref[...] = blocks_ref[block].astype(jnp.float32)
        base = base_ref[rows, :]

        def one_group(group, total):
            first = pl.multiple_of(group * GROUP, GROUP)
            ratio = pltpu.roll(ratio_ref[...], lax.rem(width - first, width), axis=1)
            sums = []
            for c in range(GROUP):
                coupling = jnp.broadcast_to(ratio[:, c : c + 1], (width, scen))
                p = base + coupling * flow_ref[pl.ds(first + c, 1), :]
                t = jnp.exp2(p * p)
                z = t + math.e
                d = ((jnp.log(z) - 1.0) * p) * (t * pl.reciprocal(z, approx=True))
                total = total + d
                sums.append(jnp.sum(coupling * d, axis=0, keepdims=True))
            at = pl.ds(pl.multiple_of(out_row + first, GROUP), GROUP)
            grad_out_ref[at, :] += jnp.concatenate(sums, axis=0) * weight
            return total

        total = lax.fori_loop(0, width // GROUP, one_group, jnp.zeros((width, scen), jnp.float32))
        grad_mon_ref[rows, :] += total
        return unused

    lax.fori_loop(0, count_ref[0], one_tile, 0)
    grad_mon_ref[...] *= inverse_ref[...] * weight


def local(mon_flow, out_flow, rating, weights, lodf, tile_mon, tile_out, tile_count):
    width = lodf.shape[-1]
    scen = mon_flow.shape[1]
    gathered = lax.all_gather(out_flow, "mon", axis=1, tiled=True)[0]
    blocks = gathered.reshape(-1, width, scen)
    inverse = jnp.broadcast_to((ROOT / rating)[:, None], mon_flow.shape)
    base = mon_flow.astype(jnp.float32) * inverse
    vmem = pl.BlockSpec(memory_space=pltpu.VMEM)
    smem = pl.BlockSpec(memory_space=pltpu.SMEM)
    mon_part, out_part = pl.pallas_call(
        tiles_kernel,
        out_shape=(
            jax.ShapeDtypeStruct(mon_flow.shape, jnp.float32),
            jax.ShapeDtypeStruct(gathered.shape, jnp.float32),
        ),
        in_specs=[smem] * 3 + [vmem] * 5,
        out_specs=(vmem, vmem),
        scratch_shapes=[
            pltpu.VMEM((width, width), jnp.float32),
            pltpu.VMEM((width, scen), jnp.float32),
        ],
        compiler_params=pltpu.CompilerParams(vmem_limit_bytes=32 << 20),
        name="tiles",
    )(tile_count.reshape(-1), tile_mon.reshape(-1), tile_out.reshape(-1), blocks, lodf[0, 0], base,
      inverse, weights.reshape(1, -1))
    grad_out = lax.psum_scatter(
        out_part.reshape(1, -1, scen), "mon", scatter_dimension=1, tiled=True
    )
    grad_mon = lax.psum_scatter(mon_part, "out", scatter_dimension=0, tiled=True)
    return (grad_mon, grad_out)


def solution(mesh):
    in_specs = (
        P("mon", None),
        P("out", "mon", None),
        P("mon"),
        P(),
        P("mon", "out", None, None, None),
        P("mon", "out", None),
        P("mon", "out", None),
        P("mon", "out"),
    )
    out_specs = (P(("mon", "out"), None), P("out", "mon", None))
    return jax.shard_map(local, mesh=mesh, in_specs=in_specs, out_specs=out_specs, check_vma=False)
```

```python
import math

import jax
import jax.numpy as jnp
from jax import lax
from jax.experimental import pallas as pl
from jax.experimental.pallas import tpu as pltpu
from jax.sharding import PartitionSpec as P

LOG2E = 1.0 / math.log(2.0)
ROOT = math.sqrt(LOG2E)
GROUP = 8


def tiles_kernel(ny, nz, *refs):
    place_ref, count_ref, mon_ref, out_ref = refs[:4]
    shard_refs = refs[4 : 4 + ny * nz]
    lodf_ref, base_ref, inverse_ref, weight_ref = refs[4 + ny * nz : 8 + ny * nz]
    grad_mon_ref, grad_out_ref, ratio_ref, flow_ref, tile_buf, flow_buf, tile_sem, flow_sem = refs[
        8 + ny * nz :
    ]
    width = lodf_ref.shape[-1]
    scen = base_ref.shape[-1]
    per_shard = shard_refs[0].shape[0]
    count = count_ref[0]

    def where(slot):
        block = out_ref[slot]
        owner = block // per_shard
        rel_y = lax.rem(lax.rem(owner, ny) - place_ref[1] + ny, ny)
        rel_z = lax.rem(owner // ny - place_ref[0] + nz, nz)
        return rel_y * nz + rel_z, lax.rem(block, per_shard)

    def tile_copy(slot):
        return pltpu.make_async_copy(lodf_ref.at[slot], tile_buf.at[slot], tile_sem.at[slot])

    def fetch(slot, unused):
        tile_copy(slot).start()
        shard, block = where(slot)
        for index, ref in enumerate(shard_refs):

            @pl.when(shard == index)
            def start():
                pltpu.make_async_copy(ref.at[block], flow_buf.at[slot], flow_sem.at[slot]).start()

        return unused

    lax.fori_loop(0, count, fetch, 0)
    grad_mon_ref[...] = jnp.zeros_like(grad_mon_ref)
    grad_out_ref[...] = jnp.zeros_like(grad_out_ref)
    weight = weight_ref[...] * (4.0 / width / LOG2E)

    def one_tile(slot, unused):
        rows = pl.ds(pl.multiple_of(mon_ref[slot] * width, width), width)
        shard, block = where(slot)
        out_row = (shard * per_shard + block) * width
        tile_copy(slot).wait()
        pltpu.make_async_copy(
            shard_refs[0].at[0], flow_buf.at[slot], flow_sem.at[slot]
        ).wait()
        ratio_ref[...] = tile_buf[slot].astype(jnp.float32) * inverse_ref[rows, :]
        flow_ref[...] = flow_buf[slot].astype(jnp.float32)
        base = base_ref[rows, :]

        def one_group(group, total):
            first = pl.multiple_of(group * GROUP, GROUP)
            ratio = pltpu.roll(ratio_ref[...], lax.rem(width - first, width), axis=1)
            sums = []
            for c in range(GROUP):
                coupling = jnp.broadcast_to(ratio[:, c : c + 1], (width, scen))
                p = base + coupling * flow_ref[pl.ds(first + c, 1), :]
                t = jnp.exp2(p * p)
                z = t + math.e
                d = ((jnp.log(z) - 1.0) * p) * (t * pl.reciprocal(z, approx=True))
                total = total + d
                sums.append(jnp.sum(coupling * d, axis=0, keepdims=True))
            at = pl.ds(pl.multiple_of(out_row + first, GROUP), GROUP)
            grad_out_ref[at, :] += jnp.concatenate(sums, axis=0) * weight
            return total

        total = lax.fori_loop(0, width // GROUP, one_group, jnp.zeros((width, scen), jnp.float32))
        grad_mon_ref[rows, :] += total
        return unused

    lax.fori_loop(0, count, one_tile, 0)
    grad_mon_ref[...] *= inverse_ref[...] * weight


def run_tiles(shards, ny, nz, place, mon_flow, rating, weights, lodf, tile_mon, tile_out, tile_count):
    slots, width = lodf.shape[2], lodf.shape[-1]
    scen = mon_flow.shape[1]
    inverse = jnp.broadcast_to((ROOT / rating)[:, None], mon_flow.shape)
    base = mon_flow.astype(jnp.float32) * inverse
    vmem = pl.BlockSpec(memory_space=pltpu.VMEM)
    smem = pl.BlockSpec(memory_space=pltpu.SMEM)
    hbm = pl.BlockSpec(memory_space=pl.ANY)
    rows = len(shards) * shards[0].shape[0] * width

    def body(*refs):
        tiles_kernel(ny, nz, *refs)

    return pl.pallas_call(
        body,
        out_shape=(
            jax.ShapeDtypeStruct(mon_flow.shape, jnp.float32),
            jax.ShapeDtypeStruct((rows, scen), jnp.float32),
        ),
        in_specs=[smem] * 4 + [hbm] * (len(shards) + 1) + [vmem] * 3,
        out_specs=(vmem, vmem),
        scratch_shapes=[
            pltpu.VMEM((width, width), jnp.float32),
            pltpu.VMEM((width, scen), jnp.float32),
            pltpu.VMEM((slots, width, width), lodf.dtype),
            pltpu.VMEM((slots, width, scen), shards[0].dtype),
            pltpu.SemaphoreType.DMA((slots,)),
            pltpu.SemaphoreType.DMA((slots,)),
        ],
        compiler_params=pltpu.CompilerParams(vmem_limit_bytes=32 << 20),
        name="tiles",
    )(
        place, tile_count.reshape(-1), tile_mon.reshape(-1), tile_out.reshape(-1), *shards,
        lodf[0, 0], base, inverse, weights.reshape(1, -1)
    )


def shifted(n_mon, ny, dy, dz):
    nz = n_mon // ny
    return [
        (z * ny + y, (z + dz) % nz * ny + (y + dy) % ny) for z in range(nz) for y in range(ny)
    ]


def local_pairs(n_mon, n_out, *args):
    ny, nz = 2, n_mon // 2
    mon_flow, out_flow, rating, weights, lodf, tile_mon, tile_out, tile_count = args
    width = lodf.shape[-1]
    scen = mon_flow.shape[1]
    own = out_flow[0].reshape(-1, width, scen)
    column = [own] + [
        lax.ppermute(own, "mon", shifted(n_mon, ny, 0, nz - r)) for r in range(1, nz)
    ]
    across = [lax.ppermute(part, "mon", shifted(n_mon, ny, 1, 0)) for part in column]
    me = lax.axis_index("mon")
    place = jnp.stack([me // ny, me % ny]).astype(jnp.int32)
    mon_part, out_part = run_tiles(
        column + across, ny, nz, place, mon_flow, rating, weights, lodf, tile_mon, tile_out,
        tile_count
    )
    out_part = out_part.reshape(ny, nz, -1, scen)
    beside = lax.ppermute(out_part[1], "mon", shifted(n_mon, ny, 1, 0))
    summed = [out_part[0, r] + beside[r] for r in range(nz)]
    grad_out = summed[0]
    for r in range(1, nz):
        grad_out = grad_out + lax.ppermute(summed[r], "mon", shifted(n_mon, ny, 0, r))

    mine = lax.axis_index("out")
    pieces = mon_part.reshape(n_out, -1, scen)
    grad_mon = lax.dynamic_index_in_dim(pieces, mine, 0, keepdims=False)
    for r in range(1, n_out):
        piece = lax.dynamic_index_in_dim(pieces, (mine + r) % n_out, 0, keepdims=False)
        grad_mon = grad_mon + lax.ppermute(
            piece, "out", [(j, (j + r) % n_out) for j in range(n_out)]
        )
    return (grad_mon, grad_out[None])


def local_any(n_mon, n_out, *args):
    mon_flow, out_flow, rating, weights, lodf, tile_mon, tile_out, tile_count = args
    width = lodf.shape[-1]
    scen = mon_flow.shape[1]
    gathered = lax.all_gather(out_flow, "mon", axis=1, tiled=True)[0]
    blocks = gathered.reshape(-1, width, scen)
    place = jnp.zeros((2,), jnp.int32)
    mon_part, out_part = run_tiles(
        [blocks], 1, 1, place, mon_flow, rating, weights, lodf, tile_mon, tile_out, tile_count
    )
    grad_out = lax.psum_scatter(
        out_part.reshape(1, -1, scen), "mon", scatter_dimension=1, tiled=True
    )
    grad_mon = lax.psum_scatter(mon_part, "out", scatter_dimension=0, tiled=True)
    return (grad_mon, grad_out)


def solution(mesh):
    n_mon, n_out = mesh.shape["mon"], mesh.shape["out"]
    chosen = local_pairs if n_mon == 8 else local_any

    def local(*args):
        return chosen(n_mon, n_out, *args)

    in_specs = (
        P("mon", None),
        P("out", "mon", None),
        P("mon"),
        P(),
        P("mon", "out", None, None, None),
        P("mon", "out", None),
        P("mon", "out", None),
        P("mon", "out"),
    )
    out_specs = (P(("mon", "out"), None), P("out", "mon", None))
    return jax.shard_map(local, mesh=mesh, in_specs=in_specs, out_specs=out_specs, check_vma=False)
```

```python
import math

import jax
import jax.numpy as jnp
from jax import lax
from jax.experimental import pallas as pl
from jax.experimental.pallas import tpu as pltpu
from jax.sharding import PartitionSpec as P

GROUP = 8


def tiles_kernel(slots, sources, ny, nz, *refs):
    place_ref, info_ref = refs[:2]
    shard_refs = refs[2 : 2 + nz]
    refs = refs[2 + nz :]
    lodf_refs, mon_refs, rating_refs = (
        refs[sources * n : sources * (n + 1)] for n in range(3)
    )
    weight_ref, grad_mon_ref, grad_out_ref = refs[3 * sources : 3 * sources + 3]
    work_ref, ratio_ref, flow_ref, base_ref, inverse_ref, tile_buf, flow_buf, tile_sem, flow_sem = (
        refs[3 * sources + 3 :]
    )
    width = ratio_ref.shape[-1]
    scen = base_ref.shape[-1]
    per_shard = shard_refs[0].shape[0]
    blocks = mon_refs[0].shape[0] // width
    stride = 1 + 2 * slots

    def find(source, made):
        def look(slot, made):
            block = info_ref[source * stride + 1 + slots + slot]
            owner = block // per_shard
            here = lax.rem(owner, ny) == place_ref[1]

            @pl.when(here)
            def fetch():
                rel_z = lax.rem(owner // ny - place_ref[0] + nz, nz)
                inner = lax.rem(block, per_shard)
                work_ref[0, made] = source * blocks + info_ref[source * stride + 1 + slot]
                work_ref[1, made] = (rel_z * per_shard + inner) * width
                for index, ref in enumerate(lodf_refs):

                    @pl.when(source == index)
                    def start_tile():
                        pltpu.make_async_copy(
                            ref.at[slot], tile_buf.at[made], tile_sem.at[made]
                        ).start()

                for index, ref in enumerate(shard_refs):

                    @pl.when(rel_z == index)
                    def start_flow():
                        pltpu.make_async_copy(
                            ref.at[inner], flow_buf.at[made], flow_sem.at[made]
                        ).start()

            return made + here.astype(jnp.int32)

        return lax.fori_loop(0, info_ref[source * stride], look, made)

    count = lax.fori_loop(0, sources, find, jnp.int32(0))
    grad_mon_ref[...] = jnp.zeros_like(grad_mon_ref)
    grad_out_ref[...] = jnp.zeros_like(grad_out_ref)
    for source in range(sources):
        for block in range(blocks):
            row = 1.0 / rating_refs[source][block : block + 1, :]
            inverse = jnp.transpose(jnp.broadcast_to(row, (scen, width)))
            rows = mon_refs[source][block * width : (block + 1) * width, :]
            inverse_ref[source * blocks + block] = inverse
            base_ref[source * blocks + block] = rows.astype(jnp.float32) * inverse
    weight = weight_ref[...]

    def one_tile(item, unused):
        mon_block = work_ref[0, item]
        out_row = work_ref[1, item]
        pltpu.make_async_copy(lodf_refs[0].at[0], tile_buf.at[item], tile_sem.at[item]).wait()
        pltpu.make_async_copy(shard_refs[0].at[0], flow_buf.at[item], flow_sem.at[item]).wait()
        ratio_ref[...] = tile_buf[item].astype(jnp.float32) * inverse_ref[mon_block]
        flow_ref[...] = flow_buf[item].astype(jnp.float32)
        base = base_ref[mon_block]

        def one_group(group, total):
            first = pl.multiple_of(group * GROUP, GROUP)
            ratio = pltpu.roll(ratio_ref[...], lax.rem(width - first, width), axis=1)
            sums = []
            for c in range(GROUP):
                coupling = jnp.broadcast_to(ratio[:, c : c + 1], (width, scen))
                p = base + coupling * flow_ref[pl.ds(first + c, 1), :]
                square = p * p
                u = 1.0 + jnp.tanh(0.5 * square - 0.5)
                softplus = (square + (math.log(2.0) - 1.0)) - jnp.log(u)
                d = (u * p) * softplus
                total = total + d
                sums.append(jnp.sum(coupling * d, axis=0, keepdims=True))
            at = pl.ds(pl.multiple_of(out_row + first, GROUP), GROUP)
            grad_out_ref[at, :] += jnp.concatenate(sums, axis=0) * weight
            return total

        total = lax.fori_loop(0, width // GROUP, one_group, jnp.zeros((width, scen), jnp.float32))
        grad_mon_ref[mon_block] += total
        return unused

    lax.fori_loop(0, count, one_tile, 0)
    grad_mon_ref[...] *= inverse_ref[...] * weight


def run_tiles(place, info, shards, ny, lodfs, mon_flows, ratings, weights):
    sources, nz = len(lodfs), len(shards)
    slots, width, _ = lodfs[0].shape
    scen = mon_flows[0].shape[1]
    blocks = mon_flows[0].shape[0] // width
    vmem = pl.BlockSpec(memory_space=pltpu.VMEM)
    smem = pl.BlockSpec(memory_space=pltpu.SMEM)
    anywhere = pl.BlockSpec(memory_space=pl.ANY)
    hbm = pl.BlockSpec(memory_space=pltpu.HBM)
    items = sources * slots

    def body(*refs):
        tiles_kernel(slots, sources, ny, nz, *refs)

    return pl.pallas_call(
        body,
        out_shape=(
            jax.ShapeDtypeStruct((sources * blocks, width, scen), jnp.float32),
            jax.ShapeDtypeStruct((nz * shards[0].shape[0] * width, scen), jnp.float32),
        ),
        in_specs=[smem] * 2
        + [hbm] + [anywhere] * (nz - 1)
        + [hbm] + [anywhere] * (sources - 1)
        + [vmem] * (2 * sources + 1),
        out_specs=(vmem, vmem),
        scratch_shapes=[
            pltpu.SMEM((2, items), jnp.int32),
            pltpu.VMEM((width, width), jnp.float32),
            pltpu.VMEM((width, scen), jnp.float32),
            pltpu.VMEM((sources * blocks, width, scen), jnp.float32),
            pltpu.VMEM((sources * blocks, width, scen), jnp.float32),
            pltpu.VMEM((items, width, width), lodfs[0].dtype),
            pltpu.VMEM((items, width, scen), shards[0].dtype),
            pltpu.SemaphoreType.DMA((items,)),
            pltpu.SemaphoreType.DMA((items,)),
        ],
        compiler_params=pltpu.CompilerParams(vmem_limit_bytes=32 << 20),
        name="tiles",
    )(
        place, info, *shards, *lodfs, *mon_flows,
        *[r.reshape(blocks, width) for r in ratings],
        (weights * (2.0 / width)).reshape(1, -1)
    )


def pack_info(tile_mon, tile_out, tile_count):
    return jnp.concatenate([tile_count.reshape(-1), tile_mon.reshape(-1), tile_out.reshape(-1)])


def shifted(n_mon, ny, dy, dz):
    nz = n_mon // ny
    return [
        (z * ny + y, (z + dz) % nz * ny + (y + dy) % ny) for z in range(nz) for y in range(ny)
    ]


def local_pairs(n_mon, n_out, *args):
    ny, nz = 2, n_mon // 2
    mon_flow, out_flow, rating, weights, lodf, tile_mon, tile_out, tile_count = args
    width = lodf.shape[-1]
    scen = mon_flow.shape[1]
    beside = shifted(n_mon, ny, 1, 0)

    def across(part):
        return lax.ppermute(part, "mon", beside)

    own = out_flow[0].reshape(-1, width, scen)
    tiles = lodf[0, 0]
    column = [own] + [
        lax.ppermute(own, "mon", shifted(n_mon, ny, 0, nz - r)) for r in range(1, nz)
    ]
    info = pack_info(tile_mon, tile_out, tile_count)
    info = jnp.concatenate([info, across(info)])
    me = lax.axis_index("mon")
    place = jnp.stack([me // ny, me % ny]).astype(jnp.int32)
    mon_part, out_part = run_tiles(
        place, info, column, ny, [tiles, across(tiles)], [mon_flow, across(mon_flow)],
        [rating, across(rating)], weights
    )
    out_part = out_part.reshape(nz, -1, scen)
    grad_out = out_part[0]
    for r in range(1, nz):
        grad_out = grad_out + lax.ppermute(out_part[r], "mon", shifted(n_mon, ny, 0, r))

    mon_part = mon_part.reshape(2, n_out, -1, scen)
    pieces = mon_part[0] + across(mon_part[1])
    mine = lax.axis_index("out")
    grad_mon = lax.dynamic_index_in_dim(pieces, mine, 0, keepdims=False)
    for r in range(1, n_out):
        piece = lax.dynamic_index_in_dim(pieces, (mine + r) % n_out, 0, keepdims=False)
        grad_mon = grad_mon + lax.ppermute(
            piece, "out", [(j, (j + r) % n_out) for j in range(n_out)]
        )
    return (grad_mon, grad_out[None])


def local_any(n_mon, n_out, *args):
    mon_flow, out_flow, rating, weights, lodf, tile_mon, tile_out, tile_count = args
    width = lodf.shape[-1]
    scen = mon_flow.shape[1]
    gathered = lax.all_gather(out_flow, "mon", axis=1, tiled=True)[0]
    mon_part, out_part = run_tiles(
        jnp.zeros((2,), jnp.int32), pack_info(tile_mon, tile_out, tile_count),
        [gathered.reshape(-1, width, scen)], 1, [lodf[0, 0]], [mon_flow], [rating], weights
    )
    grad_out = lax.psum_scatter(
        out_part.reshape(1, -1, scen), "mon", scatter_dimension=1, tiled=True
    )
    grad_mon = lax.psum_scatter(
        mon_part.reshape(mon_flow.shape), "out", scatter_dimension=0, tiled=True
    )
    return (grad_mon, grad_out)


def solution(mesh):
    n_mon, n_out = mesh.shape["mon"], mesh.shape["out"]
    chosen = local_pairs if n_mon == 8 else local_any

    def local(*args):
        return chosen(n_mon, n_out, *args)

    in_specs = (
        P("mon", None),
        P("out", "mon", None),
        P("mon"),
        P(),
        P("mon", "out", None, None, None),
        P("mon", "out", None),
        P("mon", "out", None),
        P("mon", "out"),
    )
    out_specs = (P(("mon", "out"), None), P("out", "mon", None))
    return jax.shard_map(local, mesh=mesh, in_specs=in_specs, out_specs=out_specs, check_vma=False)
```

```python
import math

import jax
import jax.numpy as jnp
from jax import lax
from jax.experimental import pallas as pl
from jax.experimental.pallas import tpu as pltpu
from jax.sharding import PartitionSpec as P

LOG2E = 1.0 / math.log(2.0)
ROOT = math.sqrt(LOG2E)
GROUP = 16


def tiles_kernel(slots, sources, ny, nz, *refs):
    place_ref, info_ref = refs[:2]
    shard_refs = refs[2 : 2 + nz]
    refs = refs[2 + nz :]
    lodf_refs, mon_refs, rating_refs = (
        refs[sources * n : sources * (n + 1)] for n in range(3)
    )
    weight_ref, grad_mon_ref, grad_out_ref = refs[3 * sources : 3 * sources + 3]
    work_ref, pick_ref, ratio_ref, flow_ref, base_ref, inverse_ref, tile_buf, flow_buf = refs[
        3 * sources + 3 : -2
    ]
    tile_sem, flow_sem = refs[-2:]
    width = tile_buf.shape[-1]
    scen = base_ref.shape[-1]
    per_shard = shard_refs[0].shape[0]
    blocks = mon_refs[0].shape[0] // width
    stride = 1 + 2 * slots

    def find(source, made):
        def look(slot, made):
            block = info_ref[source * stride + 1 + slots + slot]
            owner = block // per_shard
            here = lax.rem(owner, ny) == place_ref[1]

            @pl.when(here)
            def fetch():
                rel_z = lax.rem(owner // ny - place_ref[0] + nz, nz)
                inner = lax.rem(block, per_shard)
                work_ref[0, made] = source * blocks + info_ref[source * stride + 1 + slot]
                work_ref[1, made] = (rel_z * per_shard + inner) * width
                for index, ref in enumerate(lodf_refs):

                    @pl.when(source == index)
                    def start_tile():
                        pltpu.make_async_copy(
                            ref.at[slot], tile_buf.at[made], tile_sem.at[made]
                        ).start()

                for index, ref in enumerate(shard_refs):

                    @pl.when(rel_z == index)
                    def start_flow():
                        pltpu.make_async_copy(
                            ref.at[inner], flow_buf.at[made], flow_sem.at[made]
                        ).start()

            return made + here.astype(jnp.int32)

        return lax.fori_loop(0, info_ref[source * stride], look, made)

    count = lax.fori_loop(0, sources, find, jnp.int32(0))
    grad_mon_ref[...] = jnp.zeros_like(grad_mon_ref)
    grad_out_ref[...] = jnp.zeros_like(grad_out_ref)
    for source in range(sources):
        for block in range(blocks):
            row = ROOT / rating_refs[source][block : block + 1, :]
            inverse = jnp.transpose(jnp.broadcast_to(row, (scen, width)))
            rows = mon_refs[source][block * width : (block + 1) * width, :]
            inverse_ref[source * blocks + block] = inverse
            base_ref[source * blocks + block] = rows.astype(jnp.float32) * inverse
    weight = weight_ref[...]
    row = lax.broadcasted_iota(jnp.int32, pick_ref.shape, 0) - (width - GROUP)
    column = lax.broadcasted_iota(jnp.int32, pick_ref.shape, 1)
    inside = jnp.logical_and(column >= row * scen, column < (row + 1) * scen)
    pick_ref[...] = inside.astype(jnp.float32).astype(pick_ref.dtype)

    def one_tile(item, unused):
        mon_block = work_ref[0, item]
        out_row = work_ref[1, item]
        pltpu.make_async_copy(lodf_refs[0].at[0], tile_buf.at[item], tile_sem.at[item]).wait()
        pltpu.make_async_copy(shard_refs[0].at[0], flow_buf.at[item], flow_sem.at[item]).wait()
        ratio = tile_buf[item].astype(jnp.float32) * inverse_ref[mon_block]
        high = ratio.astype(jnp.bfloat16)
        ratio_ref[:, :width] = high
        ratio_ref[:, width:] = (ratio - high.astype(jnp.float32)).astype(jnp.bfloat16)
        flow_ref[...] = flow_buf[item].astype(jnp.float32)
        base = base_ref[mon_block]

        def one_group(group, total):
            first = pl.multiple_of(group * GROUP, GROUP)
            picked = pl.ds(pl.multiple_of(width - GROUP - first, GROUP), width)
            sums = []
            for c in range(0, GROUP, 2):
                pick = pick_ref[picked, c * scen : (c + 2) * scen]
                pair = jnp.dot(
                    ratio_ref[...],
                    jnp.concatenate([pick, pick], axis=0),
                    preferred_element_type=jnp.float32,
                )
                for half in range(2):
                    coupling = pair[:, half * scen : (half + 1) * scen]
                    p = base + coupling * flow_ref[pl.ds(first + c + half, 1), :]
                    t = jnp.exp2(p * p)
                    z = t + math.e
                    d = ((jnp.log(z) - 1.0) * p) * (t * pl.reciprocal(z, approx=True))
                    total = total + d
                    sums.append(jnp.sum(coupling * d, axis=0, keepdims=True))
            at = pl.ds(pl.multiple_of(out_row + first, GROUP), GROUP)
            grad_out_ref[at, :] += jnp.concatenate(sums, axis=0) * weight
            return total

        total = lax.fori_loop(0, width // GROUP, one_group, jnp.zeros((width, scen), jnp.float32))
        grad_mon_ref[mon_block] += total
        return unused

    lax.fori_loop(0, count, one_tile, 0)
    grad_mon_ref[...] *= inverse_ref[...] * weight


def run_tiles(place, info, shards, ny, lodfs, mon_flows, ratings, weights):
    sources, nz = len(lodfs), len(shards)
    slots, width, _ = lodfs[0].shape
    scen = mon_flows[0].shape[1]
    blocks = mon_flows[0].shape[0] // width
    vmem = pl.BlockSpec(memory_space=pltpu.VMEM)
    smem = pl.BlockSpec(memory_space=pltpu.SMEM)
    anywhere = pl.BlockSpec(memory_space=pl.ANY)
    hbm = pl.BlockSpec(memory_space=pltpu.HBM)
    items = sources * slots

    def body(*refs):
        tiles_kernel(slots, sources, ny, nz, *refs)

    return pl.pallas_call(
        body,
        out_shape=(
            jax.ShapeDtypeStruct((sources * blocks, width, scen), jnp.float32),
            jax.ShapeDtypeStruct((nz * shards[0].shape[0] * width, scen), jnp.float32),
        ),
        in_specs=[smem] * 2
        + [hbm] + [anywhere] * (nz - 1)
        + [hbm] + [anywhere] * (sources - 1)
        + [vmem] * (2 * sources + 1),
        out_specs=(vmem, vmem),
        scratch_shapes=[
            pltpu.SMEM((2, items), jnp.int32),
            pltpu.VMEM((2 * width - GROUP, GROUP * scen), jnp.bfloat16),
            pltpu.VMEM((width, 2 * width), jnp.bfloat16),
            pltpu.VMEM((width, scen), jnp.float32),
            pltpu.VMEM((sources * blocks, width, scen), jnp.float32),
            pltpu.VMEM((sources * blocks, width, scen), jnp.float32),
            pltpu.VMEM((items, width, width), lodfs[0].dtype),
            pltpu.VMEM((items, width, scen), shards[0].dtype),
            pltpu.SemaphoreType.DMA((items,)),
            pltpu.SemaphoreType.DMA((items,)),
        ],
        compiler_params=pltpu.CompilerParams(vmem_limit_bytes=56 << 20),
        name="tiles",
    )(
        place, info, *shards, *lodfs, *mon_flows,
        *[r.reshape(blocks, width) for r in ratings],
        (weights * (4.0 / width / LOG2E)).reshape(1, -1)
    )


def pack_info(tile_mon, tile_out, tile_count):
    return jnp.concatenate([tile_count.reshape(-1), tile_mon.reshape(-1), tile_out.reshape(-1)])


def shifted(n_mon, ny, dy, dz):
    nz = n_mon // ny
    return [
        (z * ny + y, (z + dz) % nz * ny + (y + dy) % ny) for z in range(nz) for y in range(ny)
    ]


def local_pairs(n_mon, n_out, *args):
    ny, nz = 2, n_mon // 2
    mon_flow, out_flow, rating, weights, lodf, tile_mon, tile_out, tile_count = args
    width = lodf.shape[-1]
    scen = mon_flow.shape[1]
    beside = shifted(n_mon, ny, 1, 0)

    def across(part):
        return lax.ppermute(part, "mon", beside)

    own = out_flow[0].reshape(-1, width, scen)
    tiles = lodf[0, 0]
    column = [own] + [
        lax.ppermute(own, "mon", shifted(n_mon, ny, 0, nz - r)) for r in range(1, nz)
    ]
    info = pack_info(tile_mon, tile_out, tile_count)
    info = jnp.concatenate([info, across(info)])
    me = lax.axis_index("mon")
    place = jnp.stack([me // ny, me % ny]).astype(jnp.int32)
    mon_part, out_part = run_tiles(
        place, info, column, ny, [tiles, across(tiles)], [mon_flow, across(mon_flow)],
        [rating, across(rating)], weights
    )
    out_part = out_part.reshape(nz, -1, scen)
    grad_out = out_part[0]
    for r in range(1, nz):
        grad_out = grad_out + lax.ppermute(out_part[r], "mon", shifted(n_mon, ny, 0, r))

    mon_part = mon_part.reshape(2, n_out, -1, scen)
    pieces = mon_part[0] + across(mon_part[1])
    mine = lax.axis_index("out")
    grad_mon = lax.dynamic_index_in_dim(pieces, mine, 0, keepdims=False)
    for r in range(1, n_out):
        piece = lax.dynamic_index_in_dim(pieces, (mine + r) % n_out, 0, keepdims=False)
        grad_mon = grad_mon + lax.ppermute(
            piece, "out", [(j, (j + r) % n_out) for j in range(n_out)]
        )
    return (grad_mon, grad_out[None])


def local_any(n_mon, n_out, *args):
    mon_flow, out_flow, rating, weights, lodf, tile_mon, tile_out, tile_count = args
    width = lodf.shape[-1]
    scen = mon_flow.shape[1]
    gathered = lax.all_gather(out_flow, "mon", axis=1, tiled=True)[0]
    mon_part, out_part = run_tiles(
        jnp.zeros((2,), jnp.int32), pack_info(tile_mon, tile_out, tile_count),
        [gathered.reshape(-1, width, scen)], 1, [lodf[0, 0]], [mon_flow], [rating], weights
    )
    grad_out = lax.psum_scatter(
        out_part.reshape(1, -1, scen), "mon", scatter_dimension=1, tiled=True
    )
    grad_mon = lax.psum_scatter(
        mon_part.reshape(mon_flow.shape), "out", scatter_dimension=0, tiled=True
    )
    return (grad_mon, grad_out)


def solution(mesh):
    n_mon, n_out = mesh.shape["mon"], mesh.shape["out"]
    chosen = local_pairs if n_mon == 8 else local_any

    def local(*args):
        return chosen(n_mon, n_out, *args)

    in_specs = (
        P("mon", None),
        P("out", "mon", None),
        P("mon"),
        P(),
        P("mon", "out", None, None, None),
        P("mon", "out", None),
        P("mon", "out", None),
        P("mon", "out"),
    )
    out_specs = (P(("mon", "out"), None), P("out", "mon", None))
    return jax.shard_map(local, mesh=mesh, in_specs=in_specs, out_specs=out_specs, check_vma=False)
```

```python
import math

import jax
import jax.numpy as jnp
from jax import lax
from jax.experimental import pallas as pl
from jax.experimental.pallas import tpu as pltpu
from jax.sharding import PartitionSpec as P

GROUP = 16
VMEM = pl.BlockSpec(memory_space=pltpu.VMEM)
SMEM = pl.BlockSpec(memory_space=pltpu.SMEM)
ANY = pl.BlockSpec(memory_space=pl.ANY)
PARAMS = pltpu.CompilerParams(vmem_limit_bytes=32 << 20)


def scaled(mon_ref, rating_ref, base_ref, inverse_ref):
    blocks, width, scen = base_ref.shape
    for block in range(blocks):
        row = 1.0 / rating_ref[block : block + 1, :]
        inverse = jnp.transpose(jnp.broadcast_to(row, (scen, width)))
        rows = mon_ref[block * width : (block + 1) * width, :]
        inverse_ref[block] = inverse
        base_ref[block] = rows.astype(jnp.float32) * inverse


def prepare_kernel(
    mon_ref, rating_ref, lodf_ref, shard_ref,
    base_ref, inverse_ref, pick_ref, lodf_out_ref, shard_out_ref
):
    scaled(mon_ref, rating_ref, base_ref, inverse_ref)
    _, width, scen = base_ref.shape
    row = lax.broadcasted_iota(jnp.int32, pick_ref.shape, 0) - (width - GROUP)
    column = lax.broadcasted_iota(jnp.int32, pick_ref.shape, 1)
    inside = jnp.logical_and(column >= row * scen, column < (row + 1) * scen)
    pick_ref[...] = inside.astype(jnp.float32).astype(pick_ref.dtype)
    lodf_out_ref[...] = lodf_ref[...]
    shard_out_ref[...] = shard_ref[...]


def tiles_kernel(slots, sources, ny, nz, wanted, added, *refs):
    place_ref = refs[0]
    info_refs = refs[1 : 1 + sources]
    refs = refs[1 + sources :]
    shard_refs, refs = refs[:nz], refs[nz:]
    lodf_refs, refs = refs[:sources], refs[sources:]
    pick_ref, own_base_ref, own_inverse_ref, weight_ref = refs[:4]
    refs = refs[4:]
    other_refs, refs = refs[: 2 * (sources - 1)], refs[2 * (sources - 1) :]
    before_refs, refs = refs[:added], refs[added:]
    grad_mon_ref, grad_out_ref, work_ref, ratio_ref, flow_ref, base_ref, inverse_ref = refs[:7]
    tile_buf, flow_buf, tile_sem, flow_sem = refs[7:]
    width = tile_buf.shape[-1]
    scen = base_ref.shape[-1]
    per_shard = shard_refs[0].shape[0]
    blocks = own_base_ref.shape[0]

    def find(source, made):
        info_ref = info_refs[source]

        def look(slot, made):
            block = info_ref[1 + slots + slot]
            owner = block // per_shard
            rel_z = lax.rem(owner // ny - place_ref[0] + nz, nz)
            inner = lax.rem(block, per_shard)
            in_wanted = jnp.logical_and(rel_z >= wanted[0], rel_z <= wanted[-1])
            here = jnp.logical_and(lax.rem(owner, ny) == place_ref[1], in_wanted)

            @pl.when(here)
            def fetch():
                work_ref[0, made] = source * blocks + info_ref[1 + slot]
                work_ref[1, made] = ((rel_z - wanted[0]) * per_shard + inner) * width
                pltpu.make_async_copy(
                    lodf_refs[source].at[slot], tile_buf.at[made], tile_sem.at[made]
                ).start()
                for index in wanted:

                    @pl.when(rel_z == index)
                    def start_flow():
                        pltpu.make_async_copy(
                            shard_refs[index].at[inner], flow_buf.at[made], flow_sem.at[made]
                        ).start()

            return made + here.astype(jnp.int32)

        return lax.fori_loop(0, info_ref[0], look, made)

    count = jnp.int32(0)
    for source in range(sources):
        count = find(source, count)
    base_ref[:blocks] = own_base_ref[...]
    inverse_ref[:blocks] = own_inverse_ref[...]
    if sources > 1:
        scaled(*other_refs, base_ref.at[blocks:], inverse_ref.at[blocks:])
    grad_mon_ref[...] = before_refs[0][...] if added else jnp.zeros_like(grad_mon_ref)
    grad_out_ref[...] = jnp.zeros_like(grad_out_ref)
    weight = weight_ref[...]

    def one_tile(item, unused):
        mon_block = work_ref[0, item]
        out_row = work_ref[1, item]
        pltpu.make_async_copy(lodf_refs[0].at[0], tile_buf.at[item], tile_sem.at[item]).wait()
        pltpu.make_async_copy(shard_refs[0].at[0], flow_buf.at[item], flow_sem.at[item]).wait()
        ratio = tile_buf[item].astype(jnp.float32) * inverse_ref[mon_block]
        high = ratio.astype(jnp.bfloat16)
        ratio_ref[:, :width] = high
        ratio_ref[:, width:] = (ratio - high.astype(jnp.float32)).astype(jnp.bfloat16)
        flow_ref[...] = flow_buf[item].astype(jnp.float32)
        base = base_ref[mon_block]

        def one_group(group, total):
            first = pl.multiple_of(group * GROUP, GROUP)
            picked = pl.ds(pl.multiple_of(width - GROUP - first, GROUP), width)
            sums = []
            for c in range(0, GROUP, 2):
                pick = pick_ref[picked, c * scen : (c + 2) * scen]
                pair = jnp.dot(
                    ratio_ref[...],
                    jnp.concatenate([pick, pick], axis=0),
                    preferred_element_type=jnp.float32,
                )
                for half in range(2):
                    coupling = pair[:, half * scen : (half + 1) * scen]
                    p = base + coupling * flow_ref[pl.ds(first + c + half, 1), :]
                    square = p * p
                    u = 1.0 + jnp.tanh(0.5 * square - 0.5)
                    softplus = (square + (math.log(2.0) - 1.0)) - jnp.log(u)
                    d = (u * p) * softplus
                    total = total + d
                    sums.append(jnp.sum(coupling * d, axis=0, keepdims=True))
            at = pl.ds(pl.multiple_of(out_row + first, GROUP), GROUP)
            grad_out_ref[at, :] += jnp.concatenate(sums, axis=0) * weight
            return total

        total = lax.fori_loop(0, width // GROUP, one_group, jnp.zeros((width, scen), jnp.float32))
        grad_mon_ref[mon_block] += total * (inverse_ref[mon_block] * weight)
        return unused

    lax.fori_loop(0, count, one_tile, 0)


def prepare(mon_flow, rating, tiles, shard):
    width, scen = tiles.shape[-1], mon_flow.shape[1]
    blocks = mon_flow.shape[0] // width
    by_block = jax.ShapeDtypeStruct((blocks, width, scen), jnp.float32)
    return pl.pallas_call(
        prepare_kernel,
        out_shape=(
            by_block,
            by_block,
            jax.ShapeDtypeStruct((2 * width - GROUP, GROUP * scen), jnp.bfloat16),
            jax.ShapeDtypeStruct(tiles.shape, tiles.dtype),
            jax.ShapeDtypeStruct(shard.shape, shard.dtype),
        ),
        in_specs=[VMEM] * 4,
        out_specs=(VMEM,) * 5,
        compiler_params=PARAMS,
        cost_estimate=pl.CostEstimate(flops=1 << 22, bytes_accessed=4 << 20, transcendentals=0),
        name="prepare",
    )(mon_flow, rating.reshape(blocks, width), tiles, shard)


def run_tiles(place, infos, shards, ny, lodfs, prepared, weight, others, wanted, before=None):
    sources, nz = len(lodfs), len(shards)
    slots, width, _ = lodfs[0].shape
    base, inverse, pick = prepared
    blocks, _, scen = base.shape
    items = sources * slots
    added = [] if before is None else [before]
    elements = items // 2 * width * width * scen

    def body(*refs):
        tiles_kernel(slots, sources, ny, nz, wanted, len(added), *refs)

    return pl.pallas_call(
        body,
        out_shape=(
            jax.ShapeDtypeStruct((sources * blocks, width, scen), jnp.float32),
            jax.ShapeDtypeStruct((len(wanted) * shards[0].shape[0] * width, scen), jnp.float32),
        ),
        in_specs=[SMEM] * (1 + sources)
        + [ANY] * (nz + sources)
        + [VMEM] * (4 + len(others) + len(added)),
        out_specs=(VMEM, VMEM),
        scratch_shapes=[
            pltpu.SMEM((2, items), jnp.int32),
            pltpu.VMEM((width, 2 * width), jnp.bfloat16),
            pltpu.VMEM((width, scen), jnp.float32),
            pltpu.VMEM((sources * blocks, width, scen), jnp.float32),
            pltpu.VMEM((sources * blocks, width, scen), jnp.float32),
            pltpu.VMEM((items, width, width), lodfs[0].dtype),
            pltpu.VMEM((items, width, scen), shards[0].dtype),
            pltpu.SemaphoreType.DMA((items,)),
            pltpu.SemaphoreType.DMA((items,)),
        ],
        compiler_params=PARAMS,
        cost_estimate=pl.CostEstimate(
            flops=14 * elements, bytes_accessed=8 << 20, transcendentals=2 * elements
        ),
        name="tiles",
    )(place, *infos, *shards, *lodfs, pick, base, inverse, weight, *others, *added)


def pack_info(tile_mon, tile_out, tile_count):
    return jnp.concatenate([tile_count.reshape(-1), tile_mon.reshape(-1), tile_out.reshape(-1)])


def shifted(n_mon, ny, dy, dz):
    nz = n_mon // ny
    return [
        (z * ny + y, (z + dz) % nz * ny + (y + dy) % ny) for z in range(nz) for y in range(ny)
    ]


def local_pairs(n_mon, n_out, *args):
    ny, nz = 2, n_mon // 2
    mon_flow, out_flow, rating, weights, lodf, tile_mon, tile_out, tile_count = args
    width = lodf.shape[-1]
    rows, scen = mon_flow.shape
    beside = shifted(n_mon, ny, 1, 0)

    def across(part):
        return lax.ppermute(part, "mon", beside)

    own = out_flow[0].reshape(-1, width, scen)
    arrived = [lax.ppermute(own, "mon", shifted(n_mon, ny, 0, nz - r)) for r in range(1, nz)]
    info = pack_info(tile_mon, tile_out, tile_count)
    small = across(jnp.concatenate([rating, info.astype(jnp.float32)]))
    tiles = lodf[0, 0]
    other_tiles, other_mon = across(tiles), across(mon_flow)
    base, inverse, pick, tiles, own = prepare(mon_flow, rating, tiles, own)
    me = lax.axis_index("mon")
    place = jnp.stack([me // ny, me % ny]).astype(jnp.int32)
    common = (
        place, [info, small[rows:].astype(jnp.int32)], [own] + arrived, ny, [tiles, other_tiles],
        (base, inverse, pick), (weights * (2.0 / width)).reshape(1, -1),
        [other_mon, small[:rows].reshape(-1, width)]
    )
    mon_part, far = run_tiles(*common, tuple(range(1, nz)))
    far = far.reshape(nz - 1, -1, scen)
    come = [lax.ppermute(far[r - 1], "mon", shifted(n_mon, ny, 0, r)) for r in range(1, nz)]
    mon_part, near = run_tiles(*common, (0,), mon_part)
    grad_out = near
    for part in come:
        grad_out = grad_out + part

    mon_part = mon_part.reshape(2, n_out, -1, scen)
    pieces = mon_part[0] + across(mon_part[1])
    mine = lax.axis_index("out")
    grad_mon = lax.dynamic_index_in_dim(pieces, mine, 0, keepdims=False)
    for r in range(1, n_out):
        piece = lax.dynamic_index_in_dim(pieces, (mine + r) % n_out, 0, keepdims=False)
        grad_mon = grad_mon + lax.ppermute(
            piece, "out", [(j, (j + r) % n_out) for j in range(n_out)]
        )
    return (grad_mon, grad_out[None])


def local_any(n_mon, n_out, *args):
    mon_flow, out_flow, rating, weights, lodf, tile_mon, tile_out, tile_count = args
    width = lodf.shape[-1]
    scen = mon_flow.shape[1]
    gathered = lax.all_gather(out_flow, "mon", axis=1, tiled=True)[0]
    shard = out_flow[0].reshape(-1, scen)
    base, inverse, pick, tiles, _ = prepare(mon_flow, rating, lodf[0, 0], shard)
    mon_part, out_part = run_tiles(
        jnp.zeros((2,), jnp.int32), [pack_info(tile_mon, tile_out, tile_count)],
        [gathered.reshape(-1, width, scen)], 1, [tiles], (base, inverse, pick),
        (weights * (2.0 / width)).reshape(1, -1), [], (0,)
    )
    grad_out = lax.psum_scatter(
        out_part.reshape(1, -1, scen), "mon", scatter_dimension=1, tiled=True
    )
    grad_mon = lax.psum_scatter(
        mon_part.reshape(mon_flow.shape), "out", scatter_dimension=0, tiled=True
    )
    return (grad_mon, grad_out)


def solution(mesh):
    n_mon, n_out = mesh.shape["mon"], mesh.shape["out"]
    chosen = local_pairs if n_mon == 8 else local_any

    def local(*args):
        return chosen(n_mon, n_out, *args)

    in_specs = (
        P("mon", None),
        P("out", "mon", None),
        P("mon"),
        P(),
        P("mon", "out", None, None, None),
        P("mon", "out", None),
        P("mon", "out", None),
        P("mon", "out"),
    )
    out_specs = (P(("mon", "out"), None), P("out", "mon", None))
    return jax.shard_map(local, mesh=mesh, in_specs=in_specs, out_specs=out_specs, check_vma=False)
```

```python
import math

import jax
import jax.numpy as jnp
from jax import lax
from jax.experimental import pallas as pl
from jax.experimental.pallas import tpu as pltpu
from jax.sharding import PartitionSpec as P

GROUP = 16
VMEM = pl.BlockSpec(memory_space=pltpu.VMEM)
SMEM = pl.BlockSpec(memory_space=pltpu.SMEM)
ANY = pl.BlockSpec(memory_space=pl.ANY)
PARAMS = pltpu.CompilerParams(vmem_limit_bytes=32 << 20)


def scaled(mon_ref, rating, base_ref, inverse_ref):
    blocks, width, scen = base_ref.shape
    for block in range(blocks):
        row = 1.0 / rating[block : block + 1, :]
        inverse = jnp.transpose(jnp.broadcast_to(row, (scen, width)))
        rows = mon_ref[block * width : (block + 1) * width, :]
        inverse_ref[block] = inverse
        base_ref[block] = rows.astype(jnp.float32) * inverse


def prepare_kernel(
    mon_ref, rating_ref, lodf_ref, shard_ref,
    base_ref, inverse_ref, pick_ref, lodf_out_ref, shard_out_ref
):
    scaled(mon_ref, rating_ref[...], base_ref, inverse_ref)
    _, width, scen = base_ref.shape
    row = lax.broadcasted_iota(jnp.int32, pick_ref.shape, 0) - (width - GROUP)
    column = lax.broadcasted_iota(jnp.int32, pick_ref.shape, 1)
    inside = jnp.logical_and(column >= row * scen, column < (row + 1) * scen)
    pick_ref[...] = inside.astype(jnp.float32).astype(pick_ref.dtype)
    lodf_out_ref[...] = lodf_ref[...]
    shard_out_ref[...] = shard_ref[...]


def tiles_kernel(slots, sources, ny, nz, wanted, added, *refs):
    place_ref = refs[0]
    info_refs = refs[1 : 1 + sources]
    refs = refs[1 + sources :]
    shard_refs, refs = refs[:nz], refs[nz:]
    lodf_refs, refs = refs[:sources], refs[sources:]
    pick_ref, own_base_ref, own_inverse_ref, weight_ref = refs[:4]
    refs = refs[4:]
    other_refs, refs = refs[: sources - 1], refs[sources - 1 :]
    before_refs, refs = refs[:added], refs[added:]
    grad_mon_ref, grad_out_ref, work_ref, ratio_ref, exact_ref, flow_ref, base_ref = refs[:7]
    inverse_ref, tile_buf, flow_buf, tile_sem, flow_sem = refs[7:]
    width = tile_buf.shape[-1]
    scen = base_ref.shape[-1]
    per_shard = shard_refs[0].shape[0]
    blocks = own_base_ref.shape[0]

    def find(source, made):
        info_ref = info_refs[source]

        def look(slot, made):
            block = info_ref[1 + slots + slot]
            owner = block // per_shard
            rel_z = lax.rem(owner // ny - place_ref[0] + nz, nz)
            inner = lax.rem(block, per_shard)
            in_wanted = jnp.logical_and(rel_z >= wanted[0], rel_z <= wanted[-1])
            here = jnp.logical_and(lax.rem(owner, ny) == place_ref[1], in_wanted)

            @pl.when(here)
            def fetch():
                work_ref[0, made] = source * blocks + info_ref[1 + slot]
                work_ref[1, made] = ((rel_z - wanted[0]) * per_shard + inner) * width
                pltpu.make_async_copy(
                    lodf_refs[source].at[slot], tile_buf.at[made], tile_sem.at[made]
                ).start()
                for index in wanted:

                    @pl.when(rel_z == index)
                    def start_flow():
                        pltpu.make_async_copy(
                            shard_refs[index].at[inner], flow_buf.at[made], flow_sem.at[made]
                        ).start()

            return made + here.astype(jnp.int32)

        return lax.fori_loop(0, info_ref[0], look, made)

    count = jnp.int32(0)
    for source in range(sources):
        count = find(source, count)
    base_ref[:blocks] = own_base_ref[...]
    inverse_ref[:blocks] = own_inverse_ref[...]
    if sources > 1:
        other_ref = other_refs[0]
        parts = other_ref[blocks * width : blocks * width + 16, :].astype(jnp.float32)
        rating = parts[:blocks] + parts[blocks : 2 * blocks] + parts[2 * blocks : 3 * blocks]
        scaled(other_ref, rating, base_ref.at[blocks:], inverse_ref.at[blocks:])
    grad_mon_ref[...] = before_refs[0][...] if added else jnp.zeros_like(grad_mon_ref)
    grad_out_ref[...] = jnp.zeros_like(grad_out_ref)
    weight = weight_ref[...]

    def one_tile(item, unused):
        mon_block = work_ref[0, item]
        out_row = work_ref[1, item]
        pltpu.make_async_copy(lodf_refs[0].at[0], tile_buf.at[item], tile_sem.at[item]).wait()
        pltpu.make_async_copy(shard_refs[0].at[0], flow_buf.at[item], flow_sem.at[item]).wait()
        ratio = tile_buf[item].astype(jnp.float32) * inverse_ref[mon_block]
        exact_ref[...] = ratio
        high = ratio.astype(jnp.bfloat16)
        ratio_ref[:, :width] = high
        ratio_ref[:, width:] = (ratio - high.astype(jnp.float32)).astype(jnp.bfloat16)
        flow_ref[...] = flow_buf[item].astype(jnp.float32)
        base = base_ref[mon_block]

        def one_group(group, total):
            first = pl.multiple_of(group * GROUP, GROUP)
            picked = pl.ds(pl.multiple_of(width - GROUP - first, GROUP), width)
            turned = pltpu.roll(exact_ref[...], lax.rem(width - first, width), axis=1)
            sums = []
            for c in range(0, GROUP, 2):
                if c % 4 == 0:
                    pick = pick_ref[picked, c * scen : (c + 2) * scen]
                    pair = jnp.dot(
                        ratio_ref[...],
                        jnp.concatenate([pick, pick], axis=0),
                        preferred_element_type=jnp.float32,
                    )
                for half in range(2):
                    if c % 4 == 0:
                        coupling = pair[:, half * scen : (half + 1) * scen]
                    else:
                        lane = turned[:, c + half : c + half + 1]
                        coupling = jnp.broadcast_to(lane, (width, scen))
                    p = base + coupling * flow_ref[pl.ds(first + c + half, 1), :]
                    square = p * p
                    u = 1.0 + jnp.tanh(0.5 * square - 0.5)
                    softplus = (square + (math.log(2.0) - 1.0)) - jnp.log(u)
                    d = (u * p) * softplus
                    total = total + d
                    sums.append(jnp.sum(coupling * d, axis=0, keepdims=True))
            at = pl.ds(pl.multiple_of(out_row + first, GROUP), GROUP)
            grad_out_ref[at, :] += jnp.concatenate(sums, axis=0) * weight
            return total

        total = lax.fori_loop(0, width // GROUP, one_group, jnp.zeros((width, scen), jnp.float32))
        grad_mon_ref[mon_block] += total * (inverse_ref[mon_block] * weight)
        return unused

    lax.fori_loop(0, count, one_tile, 0)


def prepare(mon_flow, rating, tiles, shard):
    width, scen = tiles.shape[-1], mon_flow.shape[1]
    blocks = mon_flow.shape[0] // width
    by_block = jax.ShapeDtypeStruct((blocks, width, scen), jnp.float32)
    return pl.pallas_call(
        prepare_kernel,
        out_shape=(
            by_block,
            by_block,
            jax.ShapeDtypeStruct((2 * width - GROUP, GROUP * scen), jnp.bfloat16),
            jax.ShapeDtypeStruct(tiles.shape, tiles.dtype),
            jax.ShapeDtypeStruct(shard.shape, shard.dtype),
        ),
        in_specs=[VMEM] * 4,
        out_specs=(VMEM,) * 5,
        compiler_params=PARAMS,
        cost_estimate=pl.CostEstimate(flops=1 << 22, bytes_accessed=4 << 20, transcendentals=0),
        name="prepare",
    )(mon_flow, rating.reshape(blocks, width), tiles, shard)


def run_tiles(place, infos, shards, ny, lodfs, prepared, weight, others, wanted, before=None):
    sources, nz = len(lodfs), len(shards)
    slots, width, _ = lodfs[0].shape
    base, inverse, pick = prepared
    blocks, _, scen = base.shape
    items = sources * slots
    added = [] if before is None else [before]
    elements = items // 2 * width * width * scen

    def body(*refs):
        tiles_kernel(slots, sources, ny, nz, wanted, len(added), *refs)

    return pl.pallas_call(
        body,
        out_shape=(
            jax.ShapeDtypeStruct((sources * blocks, width, scen), jnp.float32),
            jax.ShapeDtypeStruct((len(wanted) * shards[0].shape[0] * width, scen), jnp.float32),
        ),
        in_specs=[SMEM] * (1 + sources)
        + [ANY] * (nz + sources)
        + [VMEM] * (4 + len(others) + len(added)),
        out_specs=(VMEM, VMEM),
        scratch_shapes=[
            pltpu.SMEM((2, items), jnp.int32),
            pltpu.VMEM((width, 2 * width), jnp.bfloat16),
            pltpu.VMEM((width, width), jnp.float32),
            pltpu.VMEM((width, scen), jnp.float32),
            pltpu.VMEM((sources * blocks, width, scen), jnp.float32),
            pltpu.VMEM((sources * blocks, width, scen), jnp.float32),
            pltpu.VMEM((items, width, width), lodfs[0].dtype),
            pltpu.VMEM((items, width, scen), shards[0].dtype),
            pltpu.SemaphoreType.DMA((items,)),
            pltpu.SemaphoreType.DMA((items,)),
        ],
        compiler_params=PARAMS,
        cost_estimate=pl.CostEstimate(
            flops=14 * elements, bytes_accessed=64 << 20, transcendentals=2 * elements
        ),
        name="tiles",
    )(place, *infos, *shards, *lodfs, pick, base, inverse, weight, *others, *added)


def pack_info(tile_mon, tile_out, tile_count):
    return jnp.concatenate([tile_count.reshape(-1), tile_mon.reshape(-1), tile_out.reshape(-1)])


def pack_rows(mon_flow, rating, info, width):
    parts, rest = [], rating.reshape(-1, width)
    for _ in range(3):
        part = lax.reduce_precision(rest, 8, 7)
        parts.append(part)
        rest = rest - part
    parts.append(jnp.pad(info.astype(jnp.float32), (0, width - info.shape[0]))[None])
    tail = jnp.concatenate(parts).astype(mon_flow.dtype)
    tail = jnp.pad(tail, ((0, 16 - tail.shape[0]), (0, 0)))
    return jnp.concatenate([mon_flow, tail])


def shifted(n_mon, ny, dy, dz):
    nz = n_mon // ny
    return [
        (z * ny + y, (z + dz) % nz * ny + (y + dy) % ny) for z in range(nz) for y in range(ny)
    ]


def local_pairs(n_mon, n_out, *args):
    ny, nz = 2, n_mon // 2
    mon_flow, out_flow, rating, weights, lodf, tile_mon, tile_out, tile_count = args
    width = lodf.shape[-1]
    rows, scen = mon_flow.shape
    beside = shifted(n_mon, ny, 1, 0)

    def across(part):
        return lax.ppermute(part, "mon", beside)

    own = out_flow[0].reshape(-1, width, scen)
    arrived = [lax.ppermute(own, "mon", shifted(n_mon, ny, 0, nz - r)) for r in range(1, nz)]
    info = pack_info(tile_mon, tile_out, tile_count)
    tiles = lodf[0, 0]
    other_tiles = across(tiles)
    other = across(pack_rows(mon_flow, rating, info, width))
    other_info = other[rows + 3 * (rows // width), : info.shape[0]].astype(jnp.int32)
    base, inverse, pick, tiles, own = prepare(mon_flow, rating, tiles, own)
    me = lax.axis_index("mon")
    place = jnp.stack([me // ny, me % ny]).astype(jnp.int32)
    common = (
        place, [info, other_info], [own] + arrived, ny, [tiles, other_tiles],
        (base, inverse, pick), (weights * (2.0 / width)).reshape(1, -1), [other]
    )
    mon_part, far = run_tiles(*common, tuple(range(1, nz)))
    far = far.reshape(nz - 1, -1, scen)
    come = [lax.ppermute(far[r - 1], "mon", shifted(n_mon, ny, 0, r)) for r in range(1, nz)]
    mon_part, near = run_tiles(*common, (0,), mon_part)
    grad_out = near
    for part in come:
        grad_out = grad_out + part

    mon_part = mon_part.reshape(2, n_out, -1, scen)
    mine = lax.axis_index("out")
    grad_mon = lax.dynamic_index_in_dim(mon_part[0], mine, 0, keepdims=False)
    grad_mon, grad_out = lax.optimization_barrier((grad_mon, grad_out))
    for dy, r in [(dy, r) for dy in range(ny) for r in range(n_out) if dy or r]:
        piece = lax.dynamic_index_in_dim(mon_part[dy], (mine + r) % n_out, 0, keepdims=False)
        pairs = [
            (i * n_out + j, k * n_out + (j + r) % n_out)
            for i, k in shifted(n_mon, ny, dy, 0)
            for j in range(n_out)
        ]
        grad_mon = grad_mon + lax.ppermute(piece, ("mon", "out"), pairs)
    return (grad_mon, grad_out[None])


def local_any(n_mon, n_out, *args):
    mon_flow, out_flow, rating, weights, lodf, tile_mon, tile_out, tile_count = args
    width = lodf.shape[-1]
    scen = mon_flow.shape[1]
    gathered = lax.all_gather(out_flow, "mon", axis=1, tiled=True)[0]
    shard = out_flow[0].reshape(-1, scen)
    base, inverse, pick, tiles, _ = prepare(mon_flow, rating, lodf[0, 0], shard)
    mon_part, out_part = run_tiles(
        jnp.zeros((2,), jnp.int32), [pack_info(tile_mon, tile_out, tile_count)],
        [gathered.reshape(-1, width, scen)], 1, [tiles], (base, inverse, pick),
        (weights * (2.0 / width)).reshape(1, -1), [], (0,)
    )
    grad_out = lax.psum_scatter(
        out_part.reshape(1, -1, scen), "mon", scatter_dimension=1, tiled=True
    )
    grad_mon = lax.psum_scatter(
        mon_part.reshape(mon_flow.shape), "out", scatter_dimension=0, tiled=True
    )
    return (grad_mon, grad_out)


def solution(mesh):
    n_mon, n_out = mesh.shape["mon"], mesh.shape["out"]
    chosen = local_pairs if n_mon == 8 else local_any

    def local(*args):
        return chosen(n_mon, n_out, *args)

    in_specs = (
        P("mon", None),
        P("out", "mon", None),
        P("mon"),
        P(),
        P("mon", "out", None, None, None),
        P("mon", "out", None),
        P("mon", "out", None),
        P("mon", "out"),
    )
    out_specs = (P(("mon", "out"), None), P("out", "mon", None))
    return jax.shard_map(local, mesh=mesh, in_specs=in_specs, out_specs=out_specs, check_vma=False)
```

```python
import math

import jax
import jax.numpy as jnp
from jax import lax
from jax.experimental import pallas as pl
from jax.experimental.pallas import tpu as pltpu
from jax.sharding import PartitionSpec as P

CHUNK = 32
VMEM = pl.BlockSpec(memory_space=pltpu.VMEM)
SMEM = pl.BlockSpec(memory_space=pltpu.SMEM)
ANY = pl.BlockSpec(memory_space=pl.ANY)
PARAMS = pltpu.CompilerParams(vmem_limit_bytes=32 << 20)


def scaled(mon_ref, rating, base_ref, inverse_ref):
    blocks, width, scen = base_ref.shape
    for block in range(blocks):
        row = 1.0 / rating[block : block + 1, :]
        inverse = jnp.transpose(jnp.broadcast_to(row, (scen, width)))
        rows = mon_ref[block * width : (block + 1) * width, :]
        inverse_ref[block] = inverse
        base_ref[block] = rows.astype(jnp.float32) * inverse


def prepare_kernel(
    mon_ref, rating_ref, lodf_ref, shard_ref,
    base_ref, inverse_ref, lodf_out_ref, shard_out_ref
):
    scaled(mon_ref, rating_ref[...], base_ref, inverse_ref)
    lodf_out_ref[...] = lodf_ref[...]
    shard_out_ref[...] = shard_ref[...]


def tiles_kernel(slots, sources, ny, nz, wanted, added, *refs):
    place_ref = refs[0]
    info_refs = refs[1 : 1 + sources]
    refs = refs[1 + sources :]
    shard_refs, refs = refs[:nz], refs[nz:]
    lodf_refs, refs = refs[:sources], refs[sources:]
    own_base_ref, own_inverse_ref, weight_ref = refs[:3]
    refs = refs[3:]
    other_refs, refs = refs[: sources - 1], refs[sources - 1 :]
    before_refs, refs = refs[:added], refs[added:]
    grad_mon_ref, grad_out_ref, work_ref, ratio_ref, sums_ref, flow_ref, base_ref = refs[:7]
    inverse_ref, tile_buf, flow_buf, tile_sem, flow_sem = refs[7:]
    width = tile_buf.shape[-1]
    scen = base_ref.shape[-1]
    per_shard = shard_refs[0].shape[0]
    blocks = own_base_ref.shape[0]

    def find(source, made):
        info_ref = info_refs[source]

        def look(slot, made):
            block = info_ref[1 + slots + slot]
            owner = block // per_shard
            rel_z = lax.rem(owner // ny - place_ref[0] + nz, nz)
            inner = lax.rem(block, per_shard)
            in_wanted = jnp.logical_and(rel_z >= wanted[0], rel_z <= wanted[-1])
            here = jnp.logical_and(lax.rem(owner, ny) == place_ref[1], in_wanted)

            @pl.when(here)
            def fetch():
                work_ref[0, made] = source * blocks + info_ref[1 + slot]
                work_ref[1, made] = ((rel_z - wanted[0]) * per_shard + inner) * width
                pltpu.make_async_copy(
                    lodf_refs[source].at[slot], tile_buf.at[made], tile_sem.at[made]
                ).start()
                for index in wanted:

                    @pl.when(rel_z == index)
                    def start_flow():
                        pltpu.make_async_copy(
                            shard_refs[index].at[inner], flow_buf.at[made], flow_sem.at[made]
                        ).start()

            return made + here.astype(jnp.int32)

        return lax.fori_loop(0, info_ref[0], look, made)

    count = jnp.int32(0)
    for source in range(sources):
        count = find(source, count)
    base_ref[:blocks] = own_base_ref[...]
    inverse_ref[:blocks] = own_inverse_ref[...]
    if sources > 1:
        other_ref = other_refs[0]
        parts = other_ref[blocks * width : blocks * width + 16, :].astype(jnp.float32)
        rating = parts[:blocks] + parts[blocks : 2 * blocks] + parts[2 * blocks : 3 * blocks]
        scaled(other_ref, rating, base_ref.at[blocks:], inverse_ref.at[blocks:])
    grad_mon_ref[...] = before_refs[0][...] if added else jnp.zeros_like(grad_mon_ref)
    grad_out_ref[...] = jnp.zeros_like(grad_out_ref)
    weight = weight_ref[...]

    def one_tile(item, unused):
        mon_block = work_ref[0, item]
        out_row = work_ref[1, item]
        pltpu.make_async_copy(lodf_refs[0].at[0], tile_buf.at[item], tile_sem.at[item]).wait()
        pltpu.make_async_copy(shard_refs[0].at[0], flow_buf.at[item], flow_sem.at[item]).wait()
        ratio_ref[...] = tile_buf[item].astype(jnp.float32) * inverse_ref[mon_block]
        flow_ref[...] = flow_buf[item].astype(jnp.float32)
        sums_ref[...] = jnp.zeros_like(sums_ref)

        def one_chunk(chunk, unused):
            rows = pl.ds(pl.multiple_of(chunk * CHUNK, CHUNK), CHUNK)
            ratio = ratio_ref[rows, :]
            base = base_ref[mon_block, rows, :]
            total = jnp.zeros_like(base)
            for k in range(width):
                coupling = jnp.broadcast_to(ratio[:, k : k + 1], (CHUNK, scen))
                p = base + coupling * flow_ref[k : k + 1, :]
                square = p * p
                u = 1.0 + jnp.tanh(0.5 * square - 0.5)
                softplus = (square + (math.log(2.0) - 1.0)) - jnp.log(u)
                d = (u * p) * softplus
                total = total + d
                part = jnp.sum((coupling * d).reshape(CHUNK // 8, 8, scen), axis=0)
                sums_ref[8 * k : 8 * k + 8, :] += part
            scale = inverse_ref[mon_block, rows, :] * weight
            grad_mon_ref[mon_block, rows, :] += total * scale
            return unused

        lax.fori_loop(0, width // CHUNK, one_chunk, 0)
        gradient = sums_ref[pl.ds(0, width, stride=8), :]
        for row in range(1, 8):
            gradient = gradient + sums_ref[pl.ds(row, width, stride=8), :]
        at = pl.ds(pl.multiple_of(out_row, width), width)
        grad_out_ref[at, :] += gradient * weight
        return unused

    lax.fori_loop(0, count, one_tile, 0)


def prepare(mon_flow, rating, tiles, shard):
    width, scen = tiles.shape[-1], mon_flow.shape[1]
    blocks = mon_flow.shape[0] // width
    by_block = jax.ShapeDtypeStruct((blocks, width, scen), jnp.float32)
    return pl.pallas_call(
        prepare_kernel,
        out_shape=(
            by_block,
            by_block,
            jax.ShapeDtypeStruct(tiles.shape, tiles.dtype),
            jax.ShapeDtypeStruct(shard.shape, shard.dtype),
        ),
        in_specs=[VMEM] * 4,
        out_specs=(VMEM,) * 4,
        compiler_params=PARAMS,
        cost_estimate=pl.CostEstimate(flops=1 << 22, bytes_accessed=4 << 20, transcendentals=0),
        name="prepare",
    )(mon_flow, rating.reshape(blocks, width), tiles, shard)


def run_tiles(place, infos, shards, ny, lodfs, prepared, weight, others, wanted, before=None):
    sources, nz = len(lodfs), len(shards)
    slots, width, _ = lodfs[0].shape
    base, inverse = prepared
    blocks, _, scen = base.shape
    items = sources * slots
    added = [] if before is None else [before]
    elements = items // 2 * width * width * scen

    def body(*refs):
        tiles_kernel(slots, sources, ny, nz, wanted, len(added), *refs)

    return pl.pallas_call(
        body,
        out_shape=(
            jax.ShapeDtypeStruct((sources * blocks, width, scen), jnp.float32),
            jax.ShapeDtypeStruct((len(wanted) * shards[0].shape[0] * width, scen), jnp.float32),
        ),
        in_specs=[SMEM] * (1 + sources)
        + [ANY] * (nz + sources)
        + [VMEM] * (3 + len(others) + len(added)),
        out_specs=(VMEM, VMEM),
        scratch_shapes=[
            pltpu.SMEM((2, items), jnp.int32),
            pltpu.VMEM((width, width), jnp.float32),
            pltpu.VMEM((8 * width, scen), jnp.float32),
            pltpu.VMEM((width, scen), jnp.float32),
            pltpu.VMEM((sources * blocks, width, scen), jnp.float32),
            pltpu.VMEM((sources * blocks, width, scen), jnp.float32),
            pltpu.VMEM((items, width, width), lodfs[0].dtype),
            pltpu.VMEM((items, width, scen), shards[0].dtype),
            pltpu.SemaphoreType.DMA((items,)),
            pltpu.SemaphoreType.DMA((items,)),
        ],
        compiler_params=PARAMS,
        cost_estimate=pl.CostEstimate(
            flops=14 * elements, bytes_accessed=64 << 20, transcendentals=2 * elements
        ),
        name="tiles",
    )(place, *infos, *shards, *lodfs, base, inverse, weight, *others, *added)


def pack_info(tile_mon, tile_out, tile_count):
    return jnp.concatenate([tile_count.reshape(-1), tile_mon.reshape(-1), tile_out.reshape(-1)])


def pack_rows(mon_flow, rating, info, width):
    parts, rest = [], rating.reshape(-1, width)
    for _ in range(3):
        part = lax.reduce_precision(rest, 8, 7)
        parts.append(part)
        rest = rest - part
    parts.append(jnp.pad(info.astype(jnp.float32), (0, width - info.shape[0]))[None])
    tail = jnp.concatenate(parts).astype(mon_flow.dtype)
    tail = jnp.pad(tail, ((0, 16 - tail.shape[0]), (0, 0)))
    return jnp.concatenate([mon_flow, tail])


def shifted(n_mon, ny, dy, dz):
    nz = n_mon // ny
    return [
        (z * ny + y, (z + dz) % nz * ny + (y + dy) % ny) for z in range(nz) for y in range(ny)
    ]


def local_pairs(n_mon, n_out, *args):
    ny, nz = 2, n_mon // 2
    mon_flow, out_flow, rating, weights, lodf, tile_mon, tile_out, tile_count = args
    width = lodf.shape[-1]
    rows, scen = mon_flow.shape
    beside = shifted(n_mon, ny, 1, 0)

    def across(part):
        return lax.ppermute(part, "mon", beside)

    own = out_flow[0].reshape(-1, width, scen)
    arrived = [lax.ppermute(own, "mon", shifted(n_mon, ny, 0, nz - r)) for r in range(1, nz)]
    info = pack_info(tile_mon, tile_out, tile_count)
    tiles = lodf[0, 0]
    other_tiles = across(tiles)
    other = across(pack_rows(mon_flow, rating, info, width))
    other_info = other[rows + 3 * (rows // width), : info.shape[0]].astype(jnp.int32)
    base, inverse, tiles, own = prepare(mon_flow, rating, tiles, own)
    me = lax.axis_index("mon")
    place = jnp.stack([me // ny, me % ny]).astype(jnp.int32)
    common = (
        place, [info, other_info], [own] + arrived, ny, [tiles, other_tiles],
        (base, inverse), (weights * (2.0 / width)).reshape(1, -1), [other]
    )
    mon_part, far = run_tiles(*common, tuple(range(1, nz)))
    far = far.reshape(nz - 1, -1, scen)
    come = [lax.ppermute(far[r - 1], "mon", shifted(n_mon, ny, 0, r)) for r in range(1, nz)]
    mon_part, near = run_tiles(*common, (0,), mon_part)
    grad_out = near
    for part in come:
        grad_out = grad_out + part

    mon_part = mon_part.reshape(2, n_out, -1, scen)
    mine = lax.axis_index("out")
    grad_mon = lax.dynamic_index_in_dim(mon_part[0], mine, 0, keepdims=False)
    grad_mon, grad_out = lax.optimization_barrier((grad_mon, grad_out))
    for dy, r in [(dy, r) for dy in range(ny) for r in range(n_out) if dy or r]:
        piece = lax.dynamic_index_in_dim(mon_part[dy], (mine + r) % n_out, 0, keepdims=False)
        pairs = [
            (i * n_out + j, k * n_out + (j + r) % n_out)
            for i, k in shifted(n_mon, ny, dy, 0)
            for j in range(n_out)
        ]
        grad_mon = grad_mon + lax.ppermute(piece, ("mon", "out"), pairs)
    return (grad_mon, grad_out[None])


def local_any(n_mon, n_out, *args):
    mon_flow, out_flow, rating, weights, lodf, tile_mon, tile_out, tile_count = args
    width = lodf.shape[-1]
    scen = mon_flow.shape[1]
    gathered = lax.all_gather(out_flow, "mon", axis=1, tiled=True)[0]
    shard = out_flow[0].reshape(-1, scen)
    base, inverse, tiles, _ = prepare(mon_flow, rating, lodf[0, 0], shard)
    mon_part, out_part = run_tiles(
        jnp.zeros((2,), jnp.int32), [pack_info(tile_mon, tile_out, tile_count)],
        [gathered.reshape(-1, width, scen)], 1, [tiles], (base, inverse),
        (weights * (2.0 / width)).reshape(1, -1), [], (0,)
    )
    grad_out = lax.psum_scatter(
        out_part.reshape(1, -1, scen), "mon", scatter_dimension=1, tiled=True
    )
    grad_mon = lax.psum_scatter(
        mon_part.reshape(mon_flow.shape), "out", scatter_dimension=0, tiled=True
    )
    return (grad_mon, grad_out)


def solution(mesh):
    n_mon, n_out = mesh.shape["mon"], mesh.shape["out"]
    chosen = local_pairs if n_mon == 8 else local_any

    def local(*args):
        return chosen(n_mon, n_out, *args)

    in_specs = (
        P("mon", None),
        P("out", "mon", None),
        P("mon"),
        P(),
        P("mon", "out", None, None, None),
        P("mon", "out", None),
        P("mon", "out", None),
        P("mon", "out"),
    )
    out_specs = (P(("mon", "out"), None), P("out", "mon", None))
    return jax.shard_map(local, mesh=mesh, in_specs=in_specs, out_specs=out_specs, check_vma=False)
```

```python
import math

import jax
import jax.numpy as jnp
from jax import lax
from jax.experimental import pallas as pl
from jax.experimental.pallas import tpu as pltpu
from jax.sharding import PartitionSpec as P

LOG2E = 1.0 / math.log(2.0)
ROOT = math.sqrt(LOG2E)
CHUNK = 32
VMEM = pl.BlockSpec(memory_space=pltpu.VMEM)
SMEM = pl.BlockSpec(memory_space=pltpu.SMEM)
ANY = pl.BlockSpec(memory_space=pl.ANY)
PARAMS = pltpu.CompilerParams(vmem_limit_bytes=32 << 20)


def scaled(mon_ref, rating, base_ref, inverse_ref):
    blocks, width, scen = base_ref.shape
    for block in range(blocks):
        row = ROOT / rating[block : block + 1, :]
        inverse = jnp.transpose(jnp.broadcast_to(row, (scen, width)))
        rows = mon_ref[block * width : (block + 1) * width, :]
        inverse_ref[block] = inverse
        base_ref[block] = rows.astype(jnp.float32) * inverse


def prepare_kernel(
    mon_ref, rating_ref, lodf_ref, shard_ref,
    base_ref, inverse_ref, lodf_out_ref, shard_out_ref
):
    scaled(mon_ref, rating_ref[...], base_ref, inverse_ref)
    lodf_out_ref[...] = lodf_ref[...]
    shard_out_ref[...] = shard_ref[...]


def tiles_kernel(slots, sources, ny, nz, wanted, added, *refs):
    place_ref = refs[0]
    info_refs = refs[1 : 1 + sources]
    refs = refs[1 + sources :]
    shard_refs, refs = refs[:nz], refs[nz:]
    lodf_refs, refs = refs[:sources], refs[sources:]
    own_base_ref, own_inverse_ref, weight_ref = refs[:3]
    refs = refs[3:]
    other_refs, refs = refs[: sources - 1], refs[sources - 1 :]
    before_refs, refs = refs[:added], refs[added:]
    grad_mon_ref, grad_out_ref, work_ref, ratio_ref, sums_ref, flow_ref, base_ref = refs[:7]
    inverse_ref, tile_buf, flow_buf, tile_sem, flow_sem = refs[7:]
    width = tile_buf.shape[-1]
    scen = base_ref.shape[-1]
    per_shard = shard_refs[0].shape[0]
    blocks = own_base_ref.shape[0]

    def find(source, made):
        info_ref = info_refs[source]

        def look(slot, made):
            block = info_ref[1 + slots + slot]
            owner = block // per_shard
            rel_z = lax.rem(owner // ny - place_ref[0] + nz, nz)
            inner = lax.rem(block, per_shard)
            in_wanted = jnp.logical_and(rel_z >= wanted[0], rel_z <= wanted[-1])
            here = jnp.logical_and(lax.rem(owner, ny) == place_ref[1], in_wanted)

            @pl.when(here)
            def fetch():
                work_ref[0, made] = source * blocks + info_ref[1 + slot]
                work_ref[1, made] = ((rel_z - wanted[0]) * per_shard + inner) * width
                pltpu.make_async_copy(
                    lodf_refs[source].at[slot], tile_buf.at[made], tile_sem.at[made]
                ).start()
                for index in wanted:

                    @pl.when(rel_z == index)
                    def start_flow():
                        pltpu.make_async_copy(
                            shard_refs[index].at[inner], flow_buf.at[made], flow_sem.at[made]
                        ).start()

            return made + here.astype(jnp.int32)

        return lax.fori_loop(0, info_ref[0], look, made)

    count = jnp.int32(0)
    for source in range(sources):
        count = find(source, count)
    base_ref[:blocks] = own_base_ref[...]
    inverse_ref[:blocks] = own_inverse_ref[...]
    if sources > 1:
        other_ref = other_refs[0]
        parts = other_ref[blocks * width : blocks * width + 16, :].astype(jnp.float32)
        rating = parts[:blocks] + parts[blocks : 2 * blocks] + parts[2 * blocks : 3 * blocks]
        scaled(other_ref, rating, base_ref.at[blocks:], inverse_ref.at[blocks:])
    grad_mon_ref[...] = before_refs[0][...] if added else jnp.zeros_like(grad_mon_ref)
    grad_out_ref[...] = jnp.zeros_like(grad_out_ref)
    weight = weight_ref[...]

    def one_tile(item, unused):
        mon_block = work_ref[0, item]
        out_row = work_ref[1, item]
        pltpu.make_async_copy(lodf_refs[0].at[0], tile_buf.at[item], tile_sem.at[item]).wait()
        pltpu.make_async_copy(shard_refs[0].at[0], flow_buf.at[item], flow_sem.at[item]).wait()
        ratio_ref[...] = tile_buf[item].astype(jnp.float32) * inverse_ref[mon_block]
        flow_ref[...] = flow_buf[item].astype(jnp.float32)
        sums_ref[...] = jnp.zeros_like(sums_ref)

        def one_chunk(chunk, unused):
            rows = pl.ds(pl.multiple_of(chunk * CHUNK, CHUNK), CHUNK)
            ratio = ratio_ref[rows, :]
            base = base_ref[mon_block, rows, :]
            total = jnp.zeros_like(base)
            for k in range(width):
                coupling = jnp.broadcast_to(ratio[:, k : k + 1], (CHUNK, scen))
                p = base + coupling * flow_ref[k : k + 1, :]
                t = jnp.exp2(p * p)
                z = t + math.e
                d = ((jnp.log(z) - 1.0) * p) * (t * pl.reciprocal(z, approx=True))
                total = total + d
                part = jnp.sum((coupling * d).reshape(CHUNK // 8, 8, scen), axis=0)
                sums_ref[8 * k : 8 * k + 8, :] += part
            scale = inverse_ref[mon_block, rows, :] * weight
            grad_mon_ref[mon_block, rows, :] += total * scale
            return unused

        lax.fori_loop(0, width // CHUNK, one_chunk, 0)
        gradient = sums_ref[pl.ds(0, width, stride=8), :]
        for row in range(1, 8):
            gradient = gradient + sums_ref[pl.ds(row, width, stride=8), :]
        at = pl.ds(pl.multiple_of(out_row, width), width)
        grad_out_ref[at, :] += gradient * weight
        return unused

    lax.fori_loop(0, count, one_tile, 0)


def prepare(mon_flow, rating, tiles, shard):
    width, scen = tiles.shape[-1], mon_flow.shape[1]
    blocks = mon_flow.shape[0] // width
    by_block = jax.ShapeDtypeStruct((blocks, width, scen), jnp.float32)
    return pl.pallas_call(
        prepare_kernel,
        out_shape=(
            by_block,
            by_block,
            jax.ShapeDtypeStruct(tiles.shape, tiles.dtype),
            jax.ShapeDtypeStruct(shard.shape, shard.dtype),
        ),
        in_specs=[VMEM] * 4,
        out_specs=(VMEM,) * 4,
        compiler_params=PARAMS,
        cost_estimate=pl.CostEstimate(flops=1 << 22, bytes_accessed=4 << 20, transcendentals=0),
        name="prepare",
    )(mon_flow, rating.reshape(blocks, width), tiles, shard)


def run_tiles(place, infos, shards, ny, lodfs, prepared, weight, others, wanted, before=None):
    sources, nz = len(lodfs), len(shards)
    slots, width, _ = lodfs[0].shape
    base, inverse = prepared
    blocks, _, scen = base.shape
    items = sources * slots
    added = [] if before is None else [before]
    elements = items // 2 * width * width * scen

    def body(*refs):
        tiles_kernel(slots, sources, ny, nz, wanted, len(added), *refs)

    return pl.pallas_call(
        body,
        out_shape=(
            jax.ShapeDtypeStruct((sources * blocks, width, scen), jnp.float32),
            jax.ShapeDtypeStruct((len(wanted) * shards[0].shape[0] * width, scen), jnp.float32),
        ),
        in_specs=[SMEM] * (1 + sources)
        + [ANY] * (nz + sources)
        + [VMEM] * (3 + len(others) + len(added)),
        out_specs=(VMEM, VMEM),
        scratch_shapes=[
            pltpu.SMEM((2, items), jnp.int32),
            pltpu.VMEM((width, width), jnp.float32),
            pltpu.VMEM((8 * width, scen), jnp.float32),
            pltpu.VMEM((width, scen), jnp.float32),
            pltpu.VMEM((sources * blocks, width, scen), jnp.float32),
            pltpu.VMEM((sources * blocks, width, scen), jnp.float32),
            pltpu.VMEM((items, width, width), lodfs[0].dtype),
            pltpu.VMEM((items, width, scen), shards[0].dtype),
            pltpu.SemaphoreType.DMA((items,)),
            pltpu.SemaphoreType.DMA((items,)),
        ],
        compiler_params=PARAMS,
        cost_estimate=pl.CostEstimate(
            flops=14 * elements, bytes_accessed=64 << 20, transcendentals=2 * elements
        ),
        name="tiles",
    )(place, *infos, *shards, *lodfs, base, inverse, weight, *others, *added)


def pack_info(tile_mon, tile_out, tile_count):
    return jnp.concatenate([tile_count.reshape(-1), tile_mon.reshape(-1), tile_out.reshape(-1)])


def pack_rows(mon_flow, rating, info, width):
    parts, rest = [], rating.reshape(-1, width)
    for _ in range(3):
        part = lax.reduce_precision(rest, 8, 7)
        parts.append(part)
        rest = rest - part
    parts.append(jnp.pad(info.astype(jnp.float32), (0, width - info.shape[0]))[None])
    tail = jnp.concatenate(parts).astype(mon_flow.dtype)
    tail = jnp.pad(tail, ((0, 16 - tail.shape[0]), (0, 0)))
    return jnp.concatenate([mon_flow, tail])


def shifted(n_mon, ny, dy, dz):
    nz = n_mon // ny
    return [
        (z * ny + y, (z + dz) % nz * ny + (y + dy) % ny) for z in range(nz) for y in range(ny)
    ]


def local_pairs(n_mon, n_out, *args):
    ny, nz = 2, n_mon // 2
    mon_flow, out_flow, rating, weights, lodf, tile_mon, tile_out, tile_count = args
    width = lodf.shape[-1]
    rows, scen = mon_flow.shape
    beside = shifted(n_mon, ny, 1, 0)

    def across(part):
        return lax.ppermute(part, "mon", beside)

    own = out_flow[0].reshape(-1, width, scen)
    arrived = [lax.ppermute(own, "mon", shifted(n_mon, ny, 0, nz - r)) for r in range(1, nz)]
    info = pack_info(tile_mon, tile_out, tile_count)
    tiles = lodf[0, 0]
    other_tiles = across(tiles)
    other = across(pack_rows(mon_flow, rating, info, width))
    other_info = other[rows + 3 * (rows // width), : info.shape[0]].astype(jnp.int32)
    base, inverse, tiles, own = prepare(mon_flow, rating, tiles, own)
    me = lax.axis_index("mon")
    place = jnp.stack([me // ny, me % ny]).astype(jnp.int32)
    common = (
        place, [info, other_info], [own] + arrived, ny, [tiles, other_tiles],
        (base, inverse), (weights * (4.0 / width / LOG2E)).reshape(1, -1), [other]
    )
    mon_part, far = run_tiles(*common, tuple(range(1, nz)))
    far = far.reshape(nz - 1, -1, scen)
    come = [lax.ppermute(far[r - 1], "mon", shifted(n_mon, ny, 0, r)) for r in range(1, nz)]
    mon_part, near = run_tiles(*common, (0,), mon_part)
    grad_out = near
    for part in come:
        grad_out = grad_out + part

    mon_part = mon_part.reshape(2, n_out, -1, scen)
    mine = lax.axis_index("out")
    grad_mon = lax.dynamic_index_in_dim(mon_part[0], mine, 0, keepdims=False)
    grad_mon, grad_out = lax.optimization_barrier((grad_mon, grad_out))
    for dy, r in [(dy, r) for dy in range(ny) for r in range(n_out) if dy or r]:
        piece = lax.dynamic_index_in_dim(mon_part[dy], (mine + r) % n_out, 0, keepdims=False)
        pairs = [
            (i * n_out + j, k * n_out + (j + r) % n_out)
            for i, k in shifted(n_mon, ny, dy, 0)
            for j in range(n_out)
        ]
        grad_mon = grad_mon + lax.ppermute(piece, ("mon", "out"), pairs)
    return (grad_mon, grad_out[None])


def local_any(n_mon, n_out, *args):
    mon_flow, out_flow, rating, weights, lodf, tile_mon, tile_out, tile_count = args
    width = lodf.shape[-1]
    scen = mon_flow.shape[1]
    gathered = lax.all_gather(out_flow, "mon", axis=1, tiled=True)[0]
    shard = out_flow[0].reshape(-1, scen)
    base, inverse, tiles, _ = prepare(mon_flow, rating, lodf[0, 0], shard)
    mon_part, out_part = run_tiles(
        jnp.zeros((2,), jnp.int32), [pack_info(tile_mon, tile_out, tile_count)],
        [gathered.reshape(-1, width, scen)], 1, [tiles], (base, inverse),
        (weights * (4.0 / width / LOG2E)).reshape(1, -1), [], (0,)
    )
    grad_out = lax.psum_scatter(
        out_part.reshape(1, -1, scen), "mon", scatter_dimension=1, tiled=True
    )
    grad_mon = lax.psum_scatter(
        mon_part.reshape(mon_flow.shape), "out", scatter_dimension=0, tiled=True
    )
    return (grad_mon, grad_out)


def solution(mesh):
    n_mon, n_out = mesh.shape["mon"], mesh.shape["out"]
    chosen = local_pairs if n_mon == 8 else local_any

    def local(*args):
        return chosen(n_mon, n_out, *args)

    in_specs = (
        P("mon", None),
        P("out", "mon", None),
        P("mon"),
        P(),
        P("mon", "out", None, None, None),
        P("mon", "out", None),
        P("mon", "out", None),
        P("mon", "out"),
    )
    out_specs = (P(("mon", "out"), None), P("out", "mon", None))
    return jax.shard_map(local, mesh=mesh, in_specs=in_specs, out_specs=out_specs, check_vma=False)
```

```python
import math

import jax
import jax.numpy as jnp
from jax import lax
from jax.experimental import pallas as pl
from jax.experimental.pallas import tpu as pltpu
from jax.sharding import PartitionSpec as P

LOG2E = 1.0 / math.log(2.0)
ROOT = math.sqrt(LOG2E)
CHUNK = 32
VMEM = pl.BlockSpec(memory_space=pltpu.VMEM)
SMEM = pl.BlockSpec(memory_space=pltpu.SMEM)
ANY = pl.BlockSpec(memory_space=pl.ANY)
PARAMS = pltpu.CompilerParams(vmem_limit_bytes=32 << 20)


def scaled(mon_ref, rating, base_ref, inverse_ref):
    blocks, width, scen = base_ref.shape
    for block in range(blocks):
        row = ROOT / rating[block : block + 1, :]
        inverse_ref[block] = jnp.transpose(jnp.broadcast_to(row * row, (scen, width)))
        rows = mon_ref[block * width : (block + 1) * width, :]
        base_ref[block] = rows.astype(jnp.float32)


def prepare_kernel(
    mon_ref, rating_ref, lodf_ref, shard_ref,
    base_ref, inverse_ref, lodf_out_ref, shard_out_ref
):
    scaled(mon_ref, rating_ref[...], base_ref, inverse_ref)
    lodf_out_ref[...] = lodf_ref[...]
    shard_out_ref[...] = shard_ref[...]


def tiles_kernel(slots, sources, ny, nz, wanted, added, *refs):
    place_ref = refs[0]
    info_refs = refs[1 : 1 + sources]
    refs = refs[1 + sources :]
    shard_refs, refs = refs[:nz], refs[nz:]
    lodf_refs, refs = refs[:sources], refs[sources:]
    own_base_ref, own_inverse_ref, weight_ref = refs[:3]
    refs = refs[3:]
    other_refs, refs = refs[: sources - 1], refs[sources - 1 :]
    before_refs, refs = refs[:added], refs[added:]
    grad_mon_ref, grad_out_ref, work_ref, sums_ref, flow_ref, base_ref, inverse_ref = refs[:7]
    tile_buf, flow_buf, tile_sem, flow_sem = refs[7:]
    width = tile_buf.shape[-1]
    scen = base_ref.shape[-1]
    per_shard = shard_refs[0].shape[0]
    blocks = own_base_ref.shape[0]

    def find(source, made):
        info_ref = info_refs[source]

        def look(slot, made):
            block = info_ref[1 + slots + slot]
            owner = block // per_shard
            rel_z = lax.rem(owner // ny - place_ref[0] + nz, nz)
            inner = lax.rem(block, per_shard)
            in_wanted = jnp.logical_and(rel_z >= wanted[0], rel_z <= wanted[-1])
            here = jnp.logical_and(lax.rem(owner, ny) == place_ref[1], in_wanted)

            @pl.when(here)
            def fetch():
                work_ref[0, made] = source * blocks + info_ref[1 + slot]
                work_ref[1, made] = ((rel_z - wanted[0]) * per_shard + inner) * width
                pltpu.make_async_copy(
                    lodf_refs[source].at[slot], tile_buf.at[made], tile_sem.at[made]
                ).start()
                for index in wanted:

                    @pl.when(rel_z == index)
                    def start_flow():
                        pltpu.make_async_copy(
                            shard_refs[index].at[inner], flow_buf.at[made], flow_sem.at[made]
                        ).start()

            return made + here.astype(jnp.int32)

        return lax.fori_loop(0, info_ref[0], look, made)

    count = jnp.int32(0)
    for source in range(sources):
        count = find(source, count)
    base_ref[:blocks] = own_base_ref[...]
    inverse_ref[:blocks] = own_inverse_ref[...]
    if sources > 1:
        other_ref = other_refs[0]
        parts = other_ref[blocks * width : blocks * width + 16, :].astype(jnp.float32)
        rating = parts[:blocks] + parts[blocks : 2 * blocks] + parts[2 * blocks : 3 * blocks]
        scaled(other_ref, rating, base_ref.at[blocks:], inverse_ref.at[blocks:])
    grad_mon_ref[...] = before_refs[0][...] if added else jnp.zeros_like(grad_mon_ref)
    grad_out_ref[...] = jnp.zeros_like(grad_out_ref)
    weight = weight_ref[...]

    def one_tile(item, unused):
        mon_block = work_ref[0, item]
        out_row = work_ref[1, item]
        pltpu.make_async_copy(lodf_refs[0].at[0], tile_buf.at[item], tile_sem.at[item]).wait()
        pltpu.make_async_copy(shard_refs[0].at[0], flow_buf.at[item], flow_sem.at[item]).wait()
        flow_ref[...] = flow_buf[item].astype(jnp.float32)
        sums_ref[...] = jnp.zeros_like(sums_ref)

        def one_chunk(chunk, unused):
            rows = pl.ds(pl.multiple_of(chunk * CHUNK, CHUNK), CHUNK)
            lanes = tile_buf[item, rows, :]
            base = base_ref[mon_block, rows, :]
            inverse = inverse_ref[mon_block, rows, :]
            total = jnp.zeros_like(base)
            for k in range(width):
                coupling = jnp.broadcast_to(lanes[:, k : k + 1], (CHUNK, scen)).astype(jnp.float32)
                post = base + coupling * flow_ref[k : k + 1, :]
                w = post * inverse
                t = jnp.exp2(post * w)
                z = t + math.e
                d = ((jnp.log(z) - 1.0) * w) * (t * pl.reciprocal(z, approx=True))
                total = total + d
                part = jnp.sum((coupling * d).reshape(CHUNK // 8, 8, scen), axis=0)
                sums_ref[8 * k : 8 * k + 8, :] += part
            grad_mon_ref[mon_block, rows, :] += total * weight
            return unused

        lax.fori_loop(0, width // CHUNK, one_chunk, 0)
        gradient = sums_ref[pl.ds(0, width, stride=8), :]
        for row in range(1, 8):
            gradient = gradient + sums_ref[pl.ds(row, width, stride=8), :]
        at = pl.ds(pl.multiple_of(out_row, width), width)
        grad_out_ref[at, :] += gradient * weight
        return unused

    lax.fori_loop(0, count, one_tile, 0)


def prepare(mon_flow, rating, tiles, shard):
    width, scen = tiles.shape[-1], mon_flow.shape[1]
    blocks = mon_flow.shape[0] // width
    by_block = jax.ShapeDtypeStruct((blocks, width, scen), jnp.float32)
    return pl.pallas_call(
        prepare_kernel,
        out_shape=(
            by_block,
            by_block,
            jax.ShapeDtypeStruct(tiles.shape, tiles.dtype),
            jax.ShapeDtypeStruct(shard.shape, shard.dtype),
        ),
        in_specs=[VMEM] * 4,
        out_specs=(VMEM,) * 4,
        compiler_params=PARAMS,
        cost_estimate=pl.CostEstimate(flops=1 << 22, bytes_accessed=4 << 20, transcendentals=0),
        name="prepare",
    )(mon_flow, rating.reshape(blocks, width), tiles, shard)


def run_tiles(place, infos, shards, ny, lodfs, prepared, weight, others, wanted, before=None):
    sources, nz = len(lodfs), len(shards)
    slots, width, _ = lodfs[0].shape
    base, inverse = prepared
    blocks, _, scen = base.shape
    items = sources * slots
    added = [] if before is None else [before]
    elements = items // 2 * width * width * scen

    def body(*refs):
        tiles_kernel(slots, sources, ny, nz, wanted, len(added), *refs)

    return pl.pallas_call(
        body,
        out_shape=(
            jax.ShapeDtypeStruct((sources * blocks, width, scen), jnp.float32),
            jax.ShapeDtypeStruct((len(wanted) * shards[0].shape[0] * width, scen), jnp.float32),
        ),
        in_specs=[SMEM] * (1 + sources)
        + [ANY] * (nz + sources)
        + [VMEM] * (3 + len(others) + len(added)),
        out_specs=(VMEM, VMEM),
        scratch_shapes=[
            pltpu.SMEM((2, items), jnp.int32),
            pltpu.VMEM((8 * width, scen), jnp.float32),
            pltpu.VMEM((width, scen), jnp.float32),
            pltpu.VMEM((sources * blocks, width, scen), jnp.float32),
            pltpu.VMEM((sources * blocks, width, scen), jnp.float32),
            pltpu.VMEM((items, width, width), lodfs[0].dtype),
            pltpu.VMEM((items, width, scen), shards[0].dtype),
            pltpu.SemaphoreType.DMA((items,)),
            pltpu.SemaphoreType.DMA((items,)),
        ],
        compiler_params=PARAMS,
        cost_estimate=pl.CostEstimate(
            flops=14 * elements, bytes_accessed=64 << 20, transcendentals=2 * elements
        ),
        name="tiles",
    )(place, *infos, *shards, *lodfs, base, inverse, weight, *others, *added)


def pack_info(tile_mon, tile_out, tile_count):
    return jnp.concatenate([tile_count.reshape(-1), tile_mon.reshape(-1), tile_out.reshape(-1)])


def pack_rows(mon_flow, rating, info, width):
    parts, rest = [], rating.reshape(-1, width)
    for _ in range(3):
        part = lax.reduce_precision(rest, 8, 7)
        parts.append(part)
        rest = rest - part
    parts.append(jnp.pad(info.astype(jnp.float32), (0, width - info.shape[0]))[None])
    tail = jnp.concatenate(parts).astype(mon_flow.dtype)
    tail = jnp.pad(tail, ((0, 16 - tail.shape[0]), (0, 0)))
    return jnp.concatenate([mon_flow, tail])


def shifted(n_mon, ny, dy, dz):
    nz = n_mon // ny
    return [
        (z * ny + y, (z + dz) % nz * ny + (y + dy) % ny) for z in range(nz) for y in range(ny)
    ]


def local_pairs(n_mon, n_out, *args):
    ny, nz = 2, n_mon // 2
    mon_flow, out_flow, rating, weights, lodf, tile_mon, tile_out, tile_count = args
    width = lodf.shape[-1]
    rows, scen = mon_flow.shape
    beside = shifted(n_mon, ny, 1, 0)

    def across(part):
        return lax.ppermute(part, "mon", beside)

    own = out_flow[0].reshape(-1, width, scen)
    arrived = [lax.ppermute(own, "mon", shifted(n_mon, ny, 0, nz - r)) for r in range(1, nz)]
    info = pack_info(tile_mon, tile_out, tile_count)
    tiles = lodf[0, 0]
    other_tiles = across(tiles)
    other = across(pack_rows(mon_flow, rating, info, width))
    other_info = other[rows + 3 * (rows // width), : info.shape[0]].astype(jnp.int32)
    base, inverse, tiles, own = prepare(mon_flow, rating, tiles, own)
    me = lax.axis_index("mon")
    place = jnp.stack([me // ny, me % ny]).astype(jnp.int32)
    common = (
        place, [info, other_info], [own] + arrived, ny, [tiles, other_tiles],
        (base, inverse), (weights * (4.0 / width / LOG2E)).reshape(1, -1), [other]
    )
    mon_part, far = run_tiles(*common, tuple(range(1, nz)))
    far = far.reshape(nz - 1, -1, scen)
    come = [lax.ppermute(far[r - 1], "mon", shifted(n_mon, ny, 0, r)) for r in range(1, nz)]
    mon_part, near = run_tiles(*common, (0,), mon_part)
    grad_out = near
    for part in come:
        grad_out = grad_out + part

    mon_part = mon_part.reshape(2, n_out, -1, scen)
    mine = lax.axis_index("out")
    grad_mon = lax.dynamic_index_in_dim(mon_part[0], mine, 0, keepdims=False)
    grad_mon, grad_out = lax.optimization_barrier((grad_mon, grad_out))
    for dy, r in [(dy, r) for dy in range(ny) for r in range(n_out) if dy or r]:
        piece = lax.dynamic_index_in_dim(mon_part[dy], (mine + r) % n_out, 0, keepdims=False)
        pairs = [
            (i * n_out + j, k * n_out + (j + r) % n_out)
            for i, k in shifted(n_mon, ny, dy, 0)
            for j in range(n_out)
        ]
        grad_mon = grad_mon + lax.ppermute(piece, ("mon", "out"), pairs)
    return (grad_mon, grad_out[None])


def local_any(n_mon, n_out, *args):
    mon_flow, out_flow, rating, weights, lodf, tile_mon, tile_out, tile_count = args
    width = lodf.shape[-1]
    scen = mon_flow.shape[1]
    gathered = lax.all_gather(out_flow, "mon", axis=1, tiled=True)[0]
    shard = out_flow[0].reshape(-1, scen)
    base, inverse, tiles, _ = prepare(mon_flow, rating, lodf[0, 0], shard)
    mon_part, out_part = run_tiles(
        jnp.zeros((2,), jnp.int32), [pack_info(tile_mon, tile_out, tile_count)],
        [gathered.reshape(-1, width, scen)], 1, [tiles], (base, inverse),
        (weights * (4.0 / width / LOG2E)).reshape(1, -1), [], (0,)
    )
    grad_out = lax.psum_scatter(
        out_part.reshape(1, -1, scen), "mon", scatter_dimension=1, tiled=True
    )
    grad_mon = lax.psum_scatter(
        mon_part.reshape(mon_flow.shape), "out", scatter_dimension=0, tiled=True
    )
    return (grad_mon, grad_out)


def solution(mesh):
    n_mon, n_out = mesh.shape["mon"], mesh.shape["out"]
    chosen = local_pairs if n_mon == 8 else local_any

    def local(*args):
        return chosen(n_mon, n_out, *args)

    in_specs = (
        P("mon", None),
        P("out", "mon", None),
        P("mon"),
        P(),
        P("mon", "out", None, None, None),
        P("mon", "out", None),
        P("mon", "out", None),
        P("mon", "out"),
    )
    out_specs = (P(("mon", "out"), None), P("out", "mon", None))
    return jax.shard_map(local, mesh=mesh, in_specs=in_specs, out_specs=out_specs, check_vma=False)
```

```python
import math

import jax
import jax.numpy as jnp
from jax import lax
from jax.experimental import pallas as pl
from jax.experimental.pallas import tpu as pltpu
from jax.sharding import PartitionSpec as P

LOG2E = 1.0 / math.log(2.0)
ROOT = math.sqrt(LOG2E)
CHUNK = 32
TAIL = 16
VMEM = pl.BlockSpec(memory_space=pltpu.VMEM)
SMEM = pl.BlockSpec(memory_space=pltpu.SMEM)
ANY = pl.BlockSpec(memory_space=pl.ANY)
PARAMS = pltpu.CompilerParams(vmem_limit_bytes=32 << 20)


def prepare_kernel(parts, position_ref, lodf_ref, info_ref, mon_ref, rating_ref, *out_refs):
    part_refs, mon_out_ref, turned_ref = out_refs[:parts], out_refs[parts], out_refs[parts + 1]
    slots, width, _ = lodf_ref.shape
    depth = width // parts
    for slot in range(slots):
        turned_ref[...] = jnp.transpose(lodf_ref[slot].astype(jnp.float32))
        for r in range(parts):
            part = lax.rem(position_ref[0] + r, parts)
            rows = turned_ref[pl.ds(pl.multiple_of(part * depth, depth), depth), :]
            part_refs[r][slot * depth : (slot + 1) * depth, :] = rows.astype(jnp.bfloat16)
    info = jnp.broadcast_to(info_ref[...], (TAIL, width)).astype(jnp.bfloat16)
    for r in range(parts):
        part_refs[r][slots * depth :, :] = info
    rows, _ = mon_ref.shape
    mon_out_ref[:rows, :] = mon_ref[...]
    rest = rating_ref[...]
    pieces = []
    for _ in range(3):
        piece = rest.astype(jnp.bfloat16).astype(jnp.float32)
        pieces.append(piece)
        rest = rest - piece
    blank = jnp.zeros((TAIL - 3 * rest.shape[0], width), jnp.float32)
    mon_out_ref[rows:, :] = jnp.concatenate(pieces + [blank], axis=0).astype(jnp.bfloat16)


def prepare(parts, position, tiles, info, mon_flow, rating):
    slots, width, _ = tiles.shape
    rows, scen = mon_flow.shape
    part = jax.ShapeDtypeStruct((slots * width // parts + TAIL, width), tiles.dtype)
    info = jnp.pad(info.astype(jnp.float32), (0, width - info.shape[0]))

    def body(*refs):
        prepare_kernel(parts, *refs)

    out = pl.pallas_call(
        body,
        out_shape=(part,) * parts + (jax.ShapeDtypeStruct((rows + TAIL, scen), mon_flow.dtype),),
        in_specs=[SMEM] + [VMEM] * 4,
        out_specs=(VMEM,) * (parts + 1),
        scratch_shapes=[pltpu.VMEM((width, width), jnp.float32)],
        compiler_params=PARAMS,
        cost_estimate=pl.CostEstimate(flops=1 << 22, bytes_accessed=4 << 20, transcendentals=0),
        name="prepare",
    )(position.reshape(1), tiles, info[None], mon_flow, rating.reshape(-1, width))
    return list(out[:parts]), out[parts]


def tiles_kernel(dims, wanted, added, *refs):
    sources, parts, slots, blocks, ny, nz = dims
    place_ref, refs = refs[0], refs[1:]
    info_refs, refs = refs[:sources], refs[sources:]
    shard_refs, refs = refs[:nz], refs[nz:]
    bundle_refs, refs = refs[:sources], refs[sources:]
    weight_ref, refs = refs[0], refs[1:]
    mon_refs, refs = refs[:sources], refs[sources:]
    before_refs, refs = refs[:added], refs[added:]
    grad_mon_ref, grad_out_ref, work_ref, turn_ref, ratio_ref, sums_ref, flow_ref = refs[:7]
    base_ref, inverse_ref, tile_buf, flow_buf, tile_sem, flow_sem = refs[7:]
    _, depth, width = tile_buf.shape
    scen = base_ref.shape[-1]
    per_shard = shard_refs[0].shape[1]
    stride = 1 + 2 * slots
    segment = slots * depth + TAIL

    def find(source, made):
        info_ref = info_refs[source]

        def of_part(r, made):
            def look(slot, made):
                block = info_ref[r * stride + 1 + slots + slot]
                owner = block // per_shard
                rel_z = lax.rem(owner // ny - place_ref[0] + nz, nz)
                inner = lax.rem(block, per_shard)
                in_wanted = jnp.logical_and(rel_z >= wanted[0], rel_z <= wanted[-1])
                here = jnp.logical_and(lax.rem(owner, ny) == place_ref[1], in_wanted)

                @pl.when(here)
                def fetch():
                    work_ref[0, made] = source * blocks + info_ref[r * stride + 1 + slot]
                    work_ref[1, made] = (
                        ((rel_z - wanted[0]) * parts + r) * per_shard + inner
                    ) * depth
                    row = pl.multiple_of(r * segment + slot * depth, TAIL)
                    pltpu.make_async_copy(
                        bundle_refs[source].at[pl.ds(row, depth), :],
                        tile_buf.at[made],
                        tile_sem.at[made],
                    ).start()
                    for index in wanted:

                        @pl.when(rel_z == index)
                        def start_flow():
                            pltpu.make_async_copy(
                                shard_refs[index].at[r, inner],
                                flow_buf.at[made],
                                flow_sem.at[made],
                            ).start()

                return made + here.astype(jnp.int32)

            return lax.fori_loop(0, info_ref[r * stride], look, made)

        return lax.fori_loop(0, parts, of_part, made)

    count = jnp.int32(0)
    for source in range(sources):
        count = find(source, count)
    for source in range(sources):
        mon_ref = mon_refs[source]
        tail = mon_ref[blocks * width : blocks * width + TAIL, :].astype(jnp.float32)
        rating = tail[:blocks] + tail[blocks : 2 * blocks] + tail[2 * blocks : 3 * blocks]
        for block in range(blocks):
            row = ROOT / rating[block : block + 1, :]
            inverse = jnp.transpose(jnp.broadcast_to(row, (scen, width)))
            rows = mon_ref[block * width : (block + 1) * width, :]
            inverse_ref[source * blocks + block] = inverse
            base_ref[source * blocks + block] = rows.astype(jnp.float32) * inverse
    grad_mon_ref[...] = before_refs[0][...] if added else jnp.zeros_like(grad_mon_ref)
    grad_out_ref[...] = jnp.zeros_like(grad_out_ref)
    turn_ref[...] = jnp.zeros_like(turn_ref)
    weight = weight_ref[...]

    def one_tile(item, unused):
        mon_block = work_ref[0, item]
        out_row = work_ref[1, item]
        pltpu.make_async_copy(
            bundle_refs[0].at[pl.ds(0, depth), :], tile_buf.at[item], tile_sem.at[item]
        ).wait()
        pltpu.make_async_copy(shard_refs[0].at[0, 0], flow_buf.at[item], flow_sem.at[item]).wait()
        turn_ref[:depth, :] = tile_buf[item].astype(jnp.float32)
        ratio_ref[...] = jnp.transpose(turn_ref[...]) * inverse_ref[mon_block]
        flow_ref[...] = flow_buf[item].astype(jnp.float32)
        for chunk in range(width // CHUNK):
            rows = slice(chunk * CHUNK, (chunk + 1) * CHUNK)
            ratio = ratio_ref[rows, :]
            base = base_ref[mon_block, rows, :]
            total = jnp.zeros_like(base)
            for k in range(depth):
                coupling = jnp.broadcast_to(ratio[:, k : k + 1], (CHUNK, scen))
                p = base + coupling * flow_ref[k : k + 1, :]
                t = jnp.exp2(p * p)
                z = t + math.e
                d = ((jnp.log(z) - 1.0) * p) * (t * pl.reciprocal(z, approx=True))
                total = total + d
                part = jnp.sum((coupling * d).reshape(CHUNK // 8, 8, scen), axis=0)
                at = slice(8 * k, 8 * k + 8)
                sums_ref[at, :] = part if chunk == 0 else sums_ref[at, :] + part
            scale = inverse_ref[mon_block, rows, :] * weight
            grad_mon_ref[mon_block, rows, :] += total * scale
        gradient = sums_ref[pl.ds(0, depth, stride=8), :]
        for row in range(1, 8):
            gradient = gradient + sums_ref[pl.ds(row, depth, stride=8), :]
        at = pl.ds(pl.multiple_of(out_row, depth), depth)
        grad_out_ref[at, :] += gradient * weight
        return unused

    lax.fori_loop(0, count, one_tile, 0)


def run_tiles(slots, ny, place, infos, shards, bundles, mons, weight, wanted, before=None):
    sources, nz = len(bundles), len(shards)
    parts, per_shard, depth, scen = shards[0].shape
    width = bundles[0].shape[-1]
    blocks = (mons[0].shape[0] - TAIL) // width
    items = sources * parts * slots
    added = [] if before is None else [before]
    dims = sources, parts, slots, blocks, ny, nz
    elements = items // 2 * depth * width * scen

    def body(*refs):
        tiles_kernel(dims, wanted, len(added), *refs)

    by_block = (sources * blocks, width, scen)
    return pl.pallas_call(
        body,
        out_shape=(
            jax.ShapeDtypeStruct(by_block, jnp.float32),
            jax.ShapeDtypeStruct((len(wanted) * parts * per_shard * depth, scen), jnp.float32),
        ),
        in_specs=[SMEM] * (1 + sources)
        + [ANY] * (nz + sources)
        + [VMEM] * (1 + sources + len(added)),
        out_specs=(VMEM, VMEM),
        scratch_shapes=[
            pltpu.SMEM((2, items), jnp.int32),
            pltpu.VMEM((width, width), jnp.float32),
            pltpu.VMEM((width, width), jnp.float32),
            pltpu.VMEM((8 * depth, scen), jnp.float32),
            pltpu.VMEM((depth, scen), jnp.float32),
            pltpu.VMEM(by_block, jnp.float32),
            pltpu.VMEM(by_block, jnp.float32),
            pltpu.VMEM((items, depth, width), bundles[0].dtype),
            pltpu.VMEM((items, depth, scen), shards[0].dtype),
            pltpu.SemaphoreType.DMA((items,)),
            pltpu.SemaphoreType.DMA((items,)),
        ],
        compiler_params=PARAMS,
        cost_estimate=pl.CostEstimate(
            flops=14 * elements, bytes_accessed=64 << 20, transcendentals=3 * elements
        ),
        name="tiles",
    )(place, *infos, *shards, *bundles, weight, *mons, *added)


def pack_info(tile_mon, tile_out, tile_count):
    return jnp.concatenate([tile_count.reshape(-1), tile_mon.reshape(-1), tile_out.reshape(-1)])


def unpack_info(bundle, parts, depth, slots):
    segment = slots * depth + TAIL
    rows = bundle[: parts * segment].reshape(parts, segment, -1)
    return rows[:, slots * depth, : 1 + 2 * slots].astype(jnp.int32).reshape(-1)


def shifted(n_mon, ny, dy, dz):
    nz = n_mon // ny
    return [
        (z * ny + y, (z + dz) % nz * ny + (y + dy) % ny) for z in range(nz) for y in range(ny)
    ]


def local_pairs(parts, n_mon, n_out, *args):
    ny, nz = 2, n_mon // 2
    mon_flow, out_flow, rating, weights, lodf, tile_mon, tile_out, tile_count = args
    tiles = lodf[0, 0]
    slots, width, _ = tiles.shape
    rows, scen = mon_flow.shape
    depth = width // parts
    me, mine = lax.axis_index("mon"), lax.axis_index("out")
    position = lax.rem(mine, parts).astype(jnp.int32)

    def along(part, r):
        pairs = [(j, j - j % parts + (j + r) % parts) for j in range(n_out)]
        return lax.ppermute(part, "out", pairs)

    def exchanged(send):
        return [send[0]] + [along(send[parts - r], parts - r) for r in range(1, parts)]

    own = out_flow[0].reshape(-1, parts, depth, scen)
    pieces = [
        lax.dynamic_index_in_dim(own, lax.rem(position + r, parts), 1, keepdims=False)
        for r in range(parts)
    ]
    shard = jnp.stack(exchanged(pieces))
    shards = [shard] + [
        lax.ppermute(shard, "mon", shifted(n_mon, ny, 0, nz - r)) for r in range(1, nz)
    ]
    info = pack_info(tile_mon, tile_out, tile_count)
    sent, mon = prepare(parts, position, tiles, info, mon_flow, rating)
    bundle = jnp.concatenate(exchanged(sent) + [mon])
    other = lax.ppermute(bundle, "mon", shifted(n_mon, ny, 1, 0))
    bundles = [bundle, other]
    common = (
        slots, ny, jnp.stack([me // ny, me % ny]).astype(jnp.int32),
        [unpack_info(b, parts, depth, slots) for b in bundles], shards, bundles,
        [mon, other[-(rows + TAIL) :]], (weights * (4.0 / width / LOG2E)).reshape(1, -1)
    )
    mon_part, far = run_tiles(*common, tuple(range(1, nz)))
    far = far.reshape(nz - 1, -1, scen)
    come = [lax.ppermute(far[r - 1], "mon", shifted(n_mon, ny, 0, r)) for r in range(1, nz)]
    mon_part, near = run_tiles(*common, (0,), mon_part)
    for part in come:
        near = near + part
    near = near.reshape(parts, -1, depth, scen)
    back = exchanged([near[r] for r in range(parts)])
    grad_out = jnp.stack(
        [
            lax.select_n(lax.rem(p - position + parts, parts), *back) if parts > 1 else back[0]
            for p in range(parts)
        ],
        axis=1,
    ).reshape(1, -1, scen)

    mon_part = mon_part.reshape(2, n_out, -1, scen)
    grad_mon = lax.dynamic_index_in_dim(mon_part[0], mine, 0, keepdims=False)
    grad_mon, grad_out = lax.optimization_barrier((grad_mon, grad_out))
    for dy, r in [(dy, r) for dy in range(ny) for r in range(n_out) if dy or r]:
        piece = lax.dynamic_index_in_dim(mon_part[dy], (mine + r) % n_out, 0, keepdims=False)
        pairs = [
            (i * n_out + j, k * n_out + (j + r) % n_out)
            for i, k in shifted(n_mon, ny, dy, 0)
            for j in range(n_out)
        ]
        grad_mon = grad_mon + lax.ppermute(piece, ("mon", "out"), pairs)
    return (grad_mon, grad_out)


def local_any(n_mon, n_out, *args):
    mon_flow, out_flow, rating, weights, lodf, tile_mon, tile_out, tile_count = args
    slots, width = lodf.shape[2], lodf.shape[-1]
    scen = mon_flow.shape[1]
    gathered = lax.all_gather(out_flow, "mon", axis=1, tiled=True)[0]
    info = pack_info(tile_mon, tile_out, tile_count)
    sent, mon = prepare(1, jnp.int32(0), lodf[0, 0], info, mon_flow, rating)
    mon_part, out_part = run_tiles(
        slots, 1, jnp.zeros((2,), jnp.int32), [info], [gathered.reshape(1, -1, width, scen)],
        sent, [mon], (weights * (4.0 / width / LOG2E)).reshape(1, -1), (0,)
    )
    grad_out = lax.psum_scatter(
        out_part.reshape(1, -1, scen), "mon", scatter_dimension=1, tiled=True
    )
    grad_mon = lax.psum_scatter(
        mon_part.reshape(mon_flow.shape), "out", scatter_dimension=0, tiled=True
    )
    return (grad_mon, grad_out)


def solution(mesh):
    n_mon, n_out = mesh.shape["mon"], mesh.shape["out"]

    def local(*args):
        if n_mon == 8:
            return local_pairs(4, n_mon, n_out, *args)
        return local_any(n_mon, n_out, *args)

    in_specs = (
        P("mon", None),
        P("out", "mon", None),
        P("mon"),
        P(),
        P("mon", "out", None, None, None),
        P("mon", "out", None),
        P("mon", "out", None),
        P("mon", "out"),
    )
    out_specs = (P(("mon", "out"), None), P("out", "mon", None))
    return jax.shard_map(local, mesh=mesh, in_specs=in_specs, out_specs=out_specs, check_vma=False)
```

```python
import math

import jax
import jax.numpy as jnp
from jax import lax
from jax.experimental import pallas as pl
from jax.experimental.pallas import tpu as pltpu
from jax.sharding import PartitionSpec as P

LOG2E = 1.0 / math.log(2.0)
ROOT = math.sqrt(LOG2E)
CHUNK = 32
TAIL = 16
VMEM = pl.BlockSpec(memory_space=pltpu.VMEM)
SMEM = pl.BlockSpec(memory_space=pltpu.SMEM)
ANY = pl.BlockSpec(memory_space=pl.ANY)
PARAMS = pltpu.CompilerParams(vmem_limit_bytes=32 << 20)


def prepare_kernel(parts, position_ref, lodf_ref, info_ref, mon_ref, rating_ref, *out_refs):
    part_refs, (mon_out_ref, tail_ref, turned_ref) = out_refs[:parts], out_refs[parts:]
    slots, width, _ = lodf_ref.shape
    depth = width // parts
    for slot in range(slots):
        turned_ref[...] = jnp.transpose(lodf_ref[slot].astype(jnp.float32))
        for r in range(parts):
            part = lax.rem(position_ref[0] + r, parts)
            rows = turned_ref[pl.ds(pl.multiple_of(part * depth, depth), depth), :]
            part_refs[r][slot * depth : (slot + 1) * depth, :] = rows.astype(jnp.bfloat16)
    info = jnp.broadcast_to(info_ref[...], (TAIL, width)).astype(jnp.bfloat16)
    for r in range(parts):
        part_refs[r][slots * depth :, :] = info
    mon_out_ref[...] = mon_ref[...]
    rest = rating_ref[...]
    pieces = []
    for _ in range(3):
        piece = rest.astype(jnp.bfloat16).astype(jnp.float32)
        pieces.append(piece)
        rest = rest - piece
    blank = jnp.zeros((TAIL - 3 * rest.shape[0], width), jnp.float32)
    tail_ref[...] = jnp.concatenate(pieces + [blank], axis=0).astype(jnp.bfloat16)


def prepare(parts, position, tiles, info, mon_flow, rating):
    slots, width, _ = tiles.shape
    part = jax.ShapeDtypeStruct((slots * width // parts + TAIL, width), tiles.dtype)
    info = jnp.pad(info.astype(jnp.float32), (0, width - info.shape[0]))

    def body(*refs):
        prepare_kernel(parts, *refs)

    out = pl.pallas_call(
        body,
        out_shape=(part,) * parts
        + (
            jax.ShapeDtypeStruct(mon_flow.shape, mon_flow.dtype),
            jax.ShapeDtypeStruct((TAIL, width), tiles.dtype),
        ),
        in_specs=[SMEM] + [VMEM] * 4,
        out_specs=(VMEM,) * (parts + 2),
        scratch_shapes=[pltpu.VMEM((width, width), jnp.float32)],
        compiler_params=PARAMS,
        cost_estimate=pl.CostEstimate(flops=1 << 22, bytes_accessed=4 << 20, transcendentals=0),
        name="prepare",
    )(position.reshape(1), tiles, info[None], mon_flow, rating.reshape(-1, width))
    return list(out[:parts]), *out[parts:]


def tiles_kernel(dims, wanted, added, *refs):
    sources, parts, slots, blocks, ny, nz = dims
    place_ref, refs = refs[0], refs[1:]
    info_refs, refs = refs[:sources], refs[sources:]
    shard_refs, refs = refs[:nz], refs[nz:]
    bundle_refs, refs = refs[:sources], refs[sources:]
    weight_ref, refs = refs[0], refs[1:]
    mon_refs, refs = refs[:sources], refs[sources:]
    tail_refs, refs = refs[:sources], refs[sources:]
    before_refs, refs = refs[:added], refs[added:]
    grad_mon_ref, grad_out_ref, work_ref, turn_ref, ratio_ref, sums_ref, flow_ref = refs[:7]
    base_ref, inverse_ref, tile_buf, flow_buf, tile_sem, flow_sem = refs[7:]
    _, depth, width = tile_buf.shape
    scen = base_ref.shape[-1]
    per_shard = shard_refs[0].shape[1]
    stride = 1 + 2 * slots
    segment = slots * depth + TAIL

    def find(source, made):
        info_ref = info_refs[source]

        def of_part(r, made):
            def look(slot, made):
                block = info_ref[r * stride + 1 + slots + slot]
                owner = block // per_shard
                rel_z = lax.rem(owner // ny - place_ref[0] + nz, nz)
                inner = lax.rem(block, per_shard)
                in_wanted = jnp.logical_and(rel_z >= wanted[0], rel_z <= wanted[-1])
                here = jnp.logical_and(lax.rem(owner, ny) == place_ref[1], in_wanted)

                @pl.when(here)
                def fetch():
                    work_ref[0, made] = source * blocks + info_ref[r * stride + 1 + slot]
                    work_ref[1, made] = (
                        ((rel_z - wanted[0]) * parts + r) * per_shard + inner
                    ) * depth
                    row = pl.multiple_of(r * segment + slot * depth, TAIL)
                    pltpu.make_async_copy(
                        bundle_refs[source].at[pl.ds(row, depth), :],
                        tile_buf.at[made],
                        tile_sem.at[made],
                    ).start()
                    for index in wanted:

                        @pl.when(rel_z == index)
                        def start_flow():
                            pltpu.make_async_copy(
                                shard_refs[index].at[r, inner],
                                flow_buf.at[made],
                                flow_sem.at[made],
                            ).start()

                return made + here.astype(jnp.int32)

            return lax.fori_loop(0, info_ref[r * stride], look, made)

        return lax.fori_loop(0, parts, of_part, made)

    count = jnp.int32(0)
    for source in range(sources):
        count = find(source, count)
    for source in range(sources):
        mon_ref = mon_refs[source]
        tail = tail_refs[source][...].astype(jnp.float32)
        rating = tail[:blocks] + tail[blocks : 2 * blocks] + tail[2 * blocks : 3 * blocks]
        for block in range(blocks):
            row = ROOT / rating[block : block + 1, :]
            inverse = jnp.transpose(jnp.broadcast_to(row, (scen, width)))
            rows = mon_ref[block * width : (block + 1) * width, :]
            inverse_ref[source * blocks + block] = inverse
            base_ref[source * blocks + block] = rows.astype(jnp.float32) * inverse
    grad_mon_ref[...] = before_refs[0][...] if added else jnp.zeros_like(grad_mon_ref)
    grad_out_ref[...] = jnp.zeros_like(grad_out_ref)
    turn_ref[...] = jnp.zeros_like(turn_ref)
    weight = weight_ref[...]

    def one_tile(item, unused):
        mon_block = work_ref[0, item]
        out_row = work_ref[1, item]
        pltpu.make_async_copy(
            bundle_refs[0].at[pl.ds(0, depth), :], tile_buf.at[item], tile_sem.at[item]
        ).wait()
        pltpu.make_async_copy(shard_refs[0].at[0, 0], flow_buf.at[item], flow_sem.at[item]).wait()
        turn_ref[:depth, :] = tile_buf[item].astype(jnp.float32)
        ratio_ref[...] = jnp.transpose(turn_ref[...]) * inverse_ref[mon_block]
        flow_ref[...] = flow_buf[item].astype(jnp.float32)
        for chunk in range(width // CHUNK):
            rows = slice(chunk * CHUNK, (chunk + 1) * CHUNK)
            ratio = ratio_ref[rows, :]
            base = base_ref[mon_block, rows, :]
            total = jnp.zeros_like(base)
            for k in range(depth):
                coupling = jnp.broadcast_to(ratio[:, k : k + 1], (CHUNK, scen))
                p = base + coupling * flow_ref[k : k + 1, :]
                t = jnp.exp2(p * p)
                z = t + math.e
                d = ((jnp.log(z) - 1.0) * p) * (t * pl.reciprocal(z, approx=True))
                total = total + d
                part = jnp.sum((coupling * d).reshape(CHUNK // 8, 8, scen), axis=0)
                at = slice(8 * k, 8 * k + 8)
                sums_ref[at, :] = part if chunk == 0 else sums_ref[at, :] + part
            scale = inverse_ref[mon_block, rows, :] * weight
            grad_mon_ref[mon_block, rows, :] += total * scale
        gradient = sums_ref[pl.ds(0, depth, stride=8), :]
        for row in range(1, 8):
            gradient = gradient + sums_ref[pl.ds(row, depth, stride=8), :]
        at = pl.ds(pl.multiple_of(out_row, depth), depth)
        grad_out_ref[at, :] += gradient * weight
        return unused

    lax.fori_loop(0, count, one_tile, 0)


def run_tiles(slots, ny, place, infos, shards, bundles, mons, tails, weight, wanted, before=None):
    sources, nz = len(bundles), len(shards)
    parts, per_shard, depth, scen = shards[0].shape
    width = bundles[0].shape[-1]
    blocks = mons[0].shape[0] // width
    items = sources * parts * slots
    added = [] if before is None else [before]
    dims = sources, parts, slots, blocks, ny, nz
    elements = items // 2 * depth * width * scen

    def body(*refs):
        tiles_kernel(dims, wanted, len(added), *refs)

    by_block = (sources * blocks, width, scen)
    return pl.pallas_call(
        body,
        out_shape=(
            jax.ShapeDtypeStruct(by_block, jnp.float32),
            jax.ShapeDtypeStruct((len(wanted) * parts * per_shard * depth, scen), jnp.float32),
        ),
        in_specs=[SMEM] * (1 + sources)
        + [ANY] * (nz + sources)
        + [VMEM] * (1 + 2 * sources + len(added)),
        out_specs=(VMEM, VMEM),
        scratch_shapes=[
            pltpu.SMEM((2, items), jnp.int32),
            pltpu.VMEM((width, width), jnp.float32),
            pltpu.VMEM((width, width), jnp.float32),
            pltpu.VMEM((8 * depth, scen), jnp.float32),
            pltpu.VMEM((depth, scen), jnp.float32),
            pltpu.VMEM(by_block, jnp.float32),
            pltpu.VMEM(by_block, jnp.float32),
            pltpu.VMEM((items, depth, width), bundles[0].dtype),
            pltpu.VMEM((items, depth, scen), shards[0].dtype),
            pltpu.SemaphoreType.DMA((items,)),
            pltpu.SemaphoreType.DMA((items,)),
        ],
        compiler_params=PARAMS,
        cost_estimate=pl.CostEstimate(
            flops=14 * elements, bytes_accessed=64 << 20, transcendentals=3 * elements
        ),
        name="tiles",
    )(place, *infos, *shards, *bundles, weight, *mons, *tails, *added)


def pack_info(tile_mon, tile_out, tile_count):
    return jnp.concatenate([tile_count.reshape(-1), tile_mon.reshape(-1), tile_out.reshape(-1)])


def unpack_info(bundle, parts, depth, slots):
    segment = slots * depth + TAIL
    rows = bundle[: parts * segment].reshape(parts, segment, -1)
    return rows[:, slots * depth, : 1 + 2 * slots].astype(jnp.int32).reshape(-1)


def shifted(n_mon, ny, dy, dz):
    nz = n_mon // ny
    return [
        (z * ny + y, (z + dz) % nz * ny + (y + dy) % ny) for z in range(nz) for y in range(ny)
    ]


def local_pairs(parts, n_mon, n_out, *args):
    ny, nz = 2, n_mon // 2
    mon_flow, out_flow, rating, weights, lodf, tile_mon, tile_out, tile_count = args
    tiles = lodf[0, 0]
    slots, width, _ = tiles.shape
    scen = mon_flow.shape[1]
    depth = width // parts
    me, mine = lax.axis_index("mon"), lax.axis_index("out")
    position = lax.rem(mine, parts).astype(jnp.int32)

    def along(part, r):
        pairs = [(j, j - j % parts + (j + r) % parts) for j in range(n_out)]
        return lax.ppermute(part, "out", pairs)

    def exchanged(send):
        return [send[0]] + [along(send[parts - r], parts - r) for r in range(1, parts)]

    own = out_flow[0].reshape(-1, parts, depth, scen)
    pieces = [
        lax.dynamic_index_in_dim(own, lax.rem(position + r, parts), 1, keepdims=False)
        for r in range(parts)
    ]
    shard = jnp.stack(exchanged(pieces))
    shards = [shard] + [
        lax.ppermute(shard, "mon", shifted(n_mon, ny, 0, nz - r)) for r in range(1, nz)
    ]
    info = pack_info(tile_mon, tile_out, tile_count)
    sent, mon, tail = prepare(parts, position, tiles, info, mon_flow, rating)
    bundle = jnp.concatenate(exchanged(sent) + [tail])
    other = lax.ppermute(bundle, "mon", shifted(n_mon, ny, 1, 0))
    other_mon = lax.ppermute(mon_flow, "mon", shifted(n_mon, ny, 1, 0))
    bundles = [bundle, other]
    common = (
        slots, ny, jnp.stack([me // ny, me % ny]).astype(jnp.int32),
        [unpack_info(b, parts, depth, slots) for b in bundles], shards, bundles,
        [mon, other_mon], [tail, other[-TAIL:]], (weights * (4.0 / width / LOG2E)).reshape(1, -1)
    )
    mon_part, out_part = run_tiles(*common, tuple(range(nz)))
    out_part = out_part.reshape(nz, -1, scen)
    come = [lax.ppermute(out_part[r], "mon", shifted(n_mon, ny, 0, r)) for r in range(1, nz)]
    mon_part = mon_part.reshape(2, n_out, -1, scen)
    pieces = mon_part[0] + lax.ppermute(mon_part[1], "mon", shifted(n_mon, ny, 1, 0))
    near = out_part[0]
    for part in come:
        near = near + part
    near, pieces = lax.optimization_barrier((near, pieces))
    near = near.reshape(parts, -1, depth, scen)
    back = exchanged([near[r] for r in range(parts)])
    place = lax.rem(jnp.arange(parts).reshape(1, parts, 1, 1) - position + parts, parts)
    grad_out = jnp.broadcast_to(back[0][:, None], (back[0].shape[0], parts, depth, scen))
    for r in range(1, parts):
        grad_out = jnp.where(place == r, back[r][:, None], grad_out)
    grad_out = grad_out.reshape(1, -1, scen)

    grad_mon = lax.dynamic_index_in_dim(pieces, mine, 0, keepdims=False)
    for r in range(1, n_out):
        piece = lax.dynamic_index_in_dim(pieces, (mine + r) % n_out, 0, keepdims=False)
        grad_mon = grad_mon + lax.ppermute(
            piece, "out", [(j, (j + r) % n_out) for j in range(n_out)]
        )
    return (grad_mon, grad_out)


def local_any(n_mon, n_out, *args):
    mon_flow, out_flow, rating, weights, lodf, tile_mon, tile_out, tile_count = args
    slots, width = lodf.shape[2], lodf.shape[-1]
    scen = mon_flow.shape[1]
    gathered = lax.all_gather(out_flow, "mon", axis=1, tiled=True)[0]
    info = pack_info(tile_mon, tile_out, tile_count)
    sent, mon, tail = prepare(1, jnp.int32(0), lodf[0, 0], info, mon_flow, rating)
    mon_part, out_part = run_tiles(
        slots, 1, jnp.zeros((2,), jnp.int32), [info], [gathered.reshape(1, -1, width, scen)],
        sent, [mon], [tail], (weights * (4.0 / width / LOG2E)).reshape(1, -1), (0,)
    )
    grad_out = lax.psum_scatter(
        out_part.reshape(1, -1, scen), "mon", scatter_dimension=1, tiled=True
    )
    grad_mon = lax.psum_scatter(
        mon_part.reshape(mon_flow.shape), "out", scatter_dimension=0, tiled=True
    )
    return (grad_mon, grad_out)


def solution(mesh):
    n_mon, n_out = mesh.shape["mon"], mesh.shape["out"]

    def local(*args):
        if n_mon == 8:
            return local_pairs(4, n_mon, n_out, *args)
        return local_any(n_mon, n_out, *args)

    in_specs = (
        P("mon", None),
        P("out", "mon", None),
        P("mon"),
        P(),
        P("mon", "out", None, None, None),
        P("mon", "out", None),
        P("mon", "out", None),
        P("mon", "out"),
    )
    out_specs = (P(("mon", "out"), None), P("out", "mon", None))
    return jax.shard_map(local, mesh=mesh, in_specs=in_specs, out_specs=out_specs, check_vma=False)
```

```python
import math

import jax
import jax.numpy as jnp
from jax import lax
from jax.experimental import pallas as pl
from jax.experimental.pallas import tpu as pltpu
from jax.sharding import PartitionSpec as P

LOG2E = 1.0 / math.log(2.0)
ROOT = math.sqrt(LOG2E)
CHUNK = 32
VMEM = pl.BlockSpec(memory_space=pltpu.VMEM)
SMEM = pl.BlockSpec(memory_space=pltpu.SMEM)
ANY = pl.BlockSpec(memory_space=pl.ANY)
PARAMS = pltpu.CompilerParams(vmem_limit_bytes=32 << 20)


def scaled(mon_ref, rating, base_ref, inverse_ref):
    blocks, width, scen = base_ref.shape
    for block in range(blocks):
        row = ROOT / rating[block : block + 1, :]
        inverse = jnp.transpose(jnp.broadcast_to(row, (scen, width)))
        rows = mon_ref[block * width : (block + 1) * width, :]
        inverse_ref[block] = inverse
        base_ref[block] = rows.astype(jnp.float32) * inverse


def prepare_kernel(
    mon_ref, rating_ref, lodf_ref, shard_ref,
    base_ref, inverse_ref, lodf_out_ref, shard_out_ref
):
    scaled(mon_ref, rating_ref[...], base_ref, inverse_ref)
    lodf_out_ref[...] = lodf_ref[...]
    shard_out_ref[...] = shard_ref[...]


def tiles_kernel(slots, sources, ny, nz, wanted, added, *refs):
    place_ref = refs[0]
    info_refs = refs[1 : 1 + sources]
    refs = refs[1 + sources :]
    shard_refs, refs = refs[:nz], refs[nz:]
    lodf_refs, refs = refs[:sources], refs[sources:]
    own_base_ref, own_inverse_ref, weight_ref = refs[:3]
    refs = refs[3:]
    other_refs, refs = refs[: sources - 1], refs[sources - 1 :]
    before_refs, refs = refs[:added], refs[added:]
    grad_mon_ref, grad_out_ref, work_ref, ratio_ref, sums_ref, flow_ref, base_ref = refs[:7]
    inverse_ref, tile_buf, flow_buf, tile_sem, flow_sem = refs[7:]
    width = tile_buf.shape[-1]
    scen = base_ref.shape[-1]
    per_shard = shard_refs[0].shape[0]
    blocks = own_base_ref.shape[0]

    def find(source, made):
        info_ref = info_refs[source]

        def look(slot, made):
            block = info_ref[1 + slots + slot]
            owner = block // per_shard
            rel_z = lax.rem(owner // ny - place_ref[0] + nz, nz)
            inner = lax.rem(block, per_shard)
            in_wanted = jnp.logical_and(rel_z >= wanted[0], rel_z <= wanted[-1])
            here = jnp.logical_and(lax.rem(owner, ny) == place_ref[1], in_wanted)

            @pl.when(here)
            def fetch():
                work_ref[0, made] = source * blocks + info_ref[1 + slot]
                work_ref[1, made] = ((rel_z - wanted[0]) * per_shard + inner) * width
                pltpu.make_async_copy(
                    lodf_refs[source].at[slot], tile_buf.at[made], tile_sem.at[made]
                ).start()
                for index in wanted:

                    @pl.when(rel_z == index)
                    def start_flow():
                        pltpu.make_async_copy(
                            shard_refs[index].at[inner], flow_buf.at[made], flow_sem.at[made]
                        ).start()

            return made + here.astype(jnp.int32)

        return lax.fori_loop(0, info_ref[0], look, made)

    count = jnp.int32(0)
    for source in range(sources):
        count = find(source, count)
    base_ref[:blocks] = own_base_ref[...]
    inverse_ref[:blocks] = own_inverse_ref[...]
    if sources > 1:
        other_ref = other_refs[0]
        parts = other_ref[blocks * width : blocks * width + 16, :].astype(jnp.float32)
        rating = parts[:blocks] + parts[blocks : 2 * blocks] + parts[2 * blocks : 3 * blocks]
        scaled(other_ref, rating, base_ref.at[blocks:], inverse_ref.at[blocks:])
    grad_mon_ref[...] = before_refs[0][...] if added else jnp.zeros_like(grad_mon_ref)
    grad_out_ref[...] = jnp.zeros_like(grad_out_ref)
    weight = weight_ref[...]

    def one_tile(item, unused):
        mon_block = work_ref[0, item]
        out_row = work_ref[1, item]
        pltpu.make_async_copy(lodf_refs[0].at[0], tile_buf.at[item], tile_sem.at[item]).wait()
        pltpu.make_async_copy(shard_refs[0].at[0], flow_buf.at[item], flow_sem.at[item]).wait()
        ratio_ref[...] = tile_buf[item].astype(jnp.float32) * inverse_ref[mon_block]
        flow_ref[...] = flow_buf[item].astype(jnp.float32)
        sums_ref[...] = jnp.zeros_like(sums_ref)

        def one_chunk(chunk, unused):
            rows = pl.ds(pl.multiple_of(chunk * CHUNK, CHUNK), CHUNK)
            ratio = ratio_ref[rows, :]
            base = base_ref[mon_block, rows, :]
            total = jnp.zeros_like(base)
            for k in range(width):
                coupling = jnp.broadcast_to(ratio[:, k : k + 1], (CHUNK, scen))
                p = base + coupling * flow_ref[k : k + 1, :]
                t = jnp.exp2(p * p)
                z = t + math.e
                d = ((jnp.log(z) - 1.0) * p) * (t * pl.reciprocal(z, approx=True))
                total = total + d
                part = jnp.sum((coupling * d).reshape(CHUNK // 8, 8, scen), axis=0)
                sums_ref[8 * k : 8 * k + 8, :] += part
            scale = inverse_ref[mon_block, rows, :] * weight
            grad_mon_ref[mon_block, rows, :] += total * scale
            return unused

        lax.fori_loop(0, width // CHUNK, one_chunk, 0)
        gradient = sums_ref[pl.ds(0, width, stride=8), :]
        for row in range(1, 8):
            gradient = gradient + sums_ref[pl.ds(row, width, stride=8), :]
        at = pl.ds(pl.multiple_of(out_row, width), width)
        grad_out_ref[at, :] += gradient * weight
        return unused

    lax.fori_loop(0, count, one_tile, 0)


def prepare(mon_flow, rating, tiles, shard):
    width, scen = tiles.shape[-1], mon_flow.shape[1]
    blocks = mon_flow.shape[0] // width
    by_block = jax.ShapeDtypeStruct((blocks, width, scen), jnp.float32)
    return pl.pallas_call(
        prepare_kernel,
        out_shape=(
            by_block,
            by_block,
            jax.ShapeDtypeStruct(tiles.shape, tiles.dtype),
            jax.ShapeDtypeStruct(shard.shape, shard.dtype),
        ),
        in_specs=[VMEM] * 4,
        out_specs=(VMEM,) * 4,
        compiler_params=PARAMS,
        cost_estimate=pl.CostEstimate(flops=1 << 22, bytes_accessed=4 << 20, transcendentals=0),
        name="prepare",
    )(mon_flow, rating.reshape(blocks, width), tiles, shard)


def run_tiles(place, infos, shards, ny, lodfs, prepared, weight, others, wanted, before=None):
    sources, nz = len(lodfs), len(shards)
    slots, width, _ = lodfs[0].shape
    base, inverse = prepared
    blocks, _, scen = base.shape
    items = sources * slots
    added = [] if before is None else [before]
    elements = items // 2 * width * width * scen

    def body(*refs):
        tiles_kernel(slots, sources, ny, nz, wanted, len(added), *refs)

    return pl.pallas_call(
        body,
        out_shape=(
            jax.ShapeDtypeStruct((sources * blocks, width, scen), jnp.float32),
            jax.ShapeDtypeStruct((len(wanted) * shards[0].shape[0] * width, scen), jnp.float32),
        ),
        in_specs=[SMEM] * (1 + sources)
        + [ANY] * (nz + sources)
        + [VMEM] * (3 + len(others) + len(added)),
        out_specs=(VMEM, VMEM),
        scratch_shapes=[
            pltpu.SMEM((2, items), jnp.int32),
            pltpu.VMEM((width, width), jnp.float32),
            pltpu.VMEM((8 * width, scen), jnp.float32),
            pltpu.VMEM((width, scen), jnp.float32),
            pltpu.VMEM((sources * blocks, width, scen), jnp.float32),
            pltpu.VMEM((sources * blocks, width, scen), jnp.float32),
            pltpu.VMEM((items, width, width), lodfs[0].dtype),
            pltpu.VMEM((items, width, scen), shards[0].dtype),
            pltpu.SemaphoreType.DMA((items,)),
            pltpu.SemaphoreType.DMA((items,)),
        ],
        compiler_params=PARAMS,
        cost_estimate=pl.CostEstimate(
            flops=14 * elements, bytes_accessed=64 << 20, transcendentals=2 * elements
        ),
        name="tiles",
    )(place, *infos, *shards, *lodfs, base, inverse, weight, *others, *added)


def pack_info(tile_mon, tile_out, tile_count):
    return jnp.concatenate([tile_count.reshape(-1), tile_mon.reshape(-1), tile_out.reshape(-1)])


def pack_rows(mon_flow, rating, info, width):
    parts, rest = [], rating.reshape(-1, width)
    for _ in range(3):
        part = lax.reduce_precision(rest, 8, 7)
        parts.append(part)
        rest = rest - part
    parts.append(jnp.pad(info.astype(jnp.float32), (0, width - info.shape[0]))[None])
    tail = jnp.concatenate(parts).astype(mon_flow.dtype)
    tail = jnp.pad(tail, ((0, 16 - tail.shape[0]), (0, 0)))
    return jnp.concatenate([mon_flow, tail])


def shifted(n_mon, ny, dy, dz):
    nz = n_mon // ny
    return [
        (z * ny + y, (z + dz) % nz * ny + (y + dy) % ny) for z in range(nz) for y in range(ny)
    ]


def local_pairs(n_mon, n_out, *args):
    ny, nz = 2, n_mon // 2
    mon_flow, out_flow, rating, weights, lodf, tile_mon, tile_out, tile_count = args
    width = lodf.shape[-1]
    rows, scen = mon_flow.shape
    beside = shifted(n_mon, ny, 1, 0)

    def across(part):
        return lax.ppermute(part, "mon", beside)

    own = out_flow[0].reshape(-1, width, scen)
    arrived = [lax.ppermute(own, "mon", shifted(n_mon, ny, 0, nz - r)) for r in range(1, nz)]
    info = pack_info(tile_mon, tile_out, tile_count)
    tiles = lodf[0, 0]
    other_tiles = across(tiles)
    other = across(pack_rows(mon_flow, rating, info, width))
    other_info = other[rows + 3 * (rows // width), : info.shape[0]].astype(jnp.int32)
    base, inverse, tiles, own = prepare(mon_flow, rating, tiles, own)
    me = lax.axis_index("mon")
    place = jnp.stack([me // ny, me % ny]).astype(jnp.int32)
    common = (
        place, [info, other_info], [own] + arrived, ny, [tiles, other_tiles],
        (base, inverse), (weights * (4.0 / width / LOG2E)).reshape(1, -1), [other]
    )
    mon_part, out_part = run_tiles(*common, tuple(range(nz)))
    out_part = out_part.reshape(nz, -1, scen)
    come = [lax.ppermute(out_part[r], "mon", shifted(n_mon, ny, 0, r)) for r in range(1, nz)]
    mon_part = mon_part.reshape(2, n_out, -1, scen)
    pieces = mon_part[0] + across(mon_part[1])
    mine = lax.axis_index("out")
    grad_mon = lax.dynamic_index_in_dim(pieces, mine, 0, keepdims=False)
    grad_out = out_part[0]
    for part in come:
        grad_out = grad_out + part
    grad_mon, grad_out = lax.optimization_barrier((grad_mon, grad_out))
    for r in range(1, n_out):
        piece = lax.dynamic_index_in_dim(pieces, (mine + r) % n_out, 0, keepdims=False)
        grad_mon = grad_mon + lax.ppermute(
            piece, "out", [(j, (j + r) % n_out) for j in range(n_out)]
        )
    return (grad_mon, grad_out[None])


def local_any(n_mon, n_out, *args):
    mon_flow, out_flow, rating, weights, lodf, tile_mon, tile_out, tile_count = args
    width = lodf.shape[-1]
    scen = mon_flow.shape[1]
    gathered = lax.all_gather(out_flow, "mon", axis=1, tiled=True)[0]
    shard = out_flow[0].reshape(-1, scen)
    base, inverse, tiles, _ = prepare(mon_flow, rating, lodf[0, 0], shard)
    mon_part, out_part = run_tiles(
        jnp.zeros((2,), jnp.int32), [pack_info(tile_mon, tile_out, tile_count)],
        [gathered.reshape(-1, width, scen)], 1, [tiles], (base, inverse),
        (weights * (4.0 / width / LOG2E)).reshape(1, -1), [], (0,)
    )
    grad_out = lax.psum_scatter(
        out_part.reshape(1, -1, scen), "mon", scatter_dimension=1, tiled=True
    )
    grad_mon = lax.psum_scatter(
        mon_part.reshape(mon_flow.shape), "out", scatter_dimension=0, tiled=True
    )
    return (grad_mon, grad_out)


def solution(mesh):
    n_mon, n_out = mesh.shape["mon"], mesh.shape["out"]
    chosen = local_pairs if n_mon == 8 else local_any

    def local(*args):
        return chosen(n_mon, n_out, *args)

    in_specs = (
        P("mon", None),
        P("out", "mon", None),
        P("mon"),
        P(),
        P("mon", "out", None, None, None),
        P("mon", "out", None),
        P("mon", "out", None),
        P("mon", "out"),
    )
    out_specs = (P(("mon", "out"), None), P("out", "mon", None))
    return jax.shard_map(local, mesh=mesh, in_specs=in_specs, out_specs=out_specs, check_vma=False)
```

```python
import math

import jax
import jax.numpy as jnp
from jax import lax
from jax.experimental import pallas as pl
from jax.experimental.pallas import tpu as pltpu
from jax.sharding import PartitionSpec as P

LOG2E = 1.0 / math.log(2.0)
ROOT = math.sqrt(LOG2E)
CHUNK = 32
TAIL = 16
VMEM = pl.BlockSpec(memory_space=pltpu.VMEM)
SMEM = pl.BlockSpec(memory_space=pltpu.SMEM)
ANY = pl.BlockSpec(memory_space=pl.ANY)
PARAMS = pltpu.CompilerParams(vmem_limit_bytes=32 << 20)


def scaled(mon_ref, rating, base_ref, inverse_ref):
    blocks, width, scen = base_ref.shape
    for block in range(blocks):
        row = ROOT / rating[block : block + 1, :]
        inverse = jnp.transpose(jnp.broadcast_to(row, (scen, width)))
        rows = mon_ref[block * width : (block + 1) * width, :]
        inverse_ref[block] = inverse
        base_ref[block] = rows.astype(jnp.float32) * inverse


def prepare_kernel(
    mon_ref, rating_ref, info_ref, lodf_ref, shard_ref,
    base_ref, inverse_ref, packed_ref, lodf_out_ref, shard_out_ref
):
    scaled(mon_ref, rating_ref[...], base_ref, inverse_ref)
    rows, width = mon_ref.shape[0], rating_ref.shape[1]
    packed_ref[:rows, :] = mon_ref[...]
    parts, rest = [], rating_ref[...]
    for _ in range(3):
        part = rest.astype(jnp.bfloat16).astype(jnp.float32)
        parts.append(part)
        rest = rest - part
    parts.append(info_ref[...])
    blank = jnp.zeros((TAIL - 1 - 3 * rest.shape[0], width), jnp.float32)
    packed_ref[rows:, :] = jnp.concatenate(parts + [blank], axis=0).astype(packed_ref.dtype)
    lodf_out_ref[...] = lodf_ref[...]
    shard_out_ref[...] = shard_ref[...]


def tiles_kernel(slots, sources, ny, nz, wanted, added, *refs):
    place_ref = refs[0]
    info_refs = refs[1 : 1 + sources]
    refs = refs[1 + sources :]
    shard_refs, refs = refs[:nz], refs[nz:]
    lodf_refs, refs = refs[:sources], refs[sources:]
    own_base_ref, own_inverse_ref, weight_ref = refs[:3]
    refs = refs[3:]
    other_refs, refs = refs[: sources - 1], refs[sources - 1 :]
    before_refs, refs = refs[:added], refs[added:]
    grad_mon_ref, grad_out_ref, work_ref, ratio_ref, sums_ref, flow_ref, base_ref = refs[:7]
    inverse_ref, tile_buf, flow_buf, tile_sem, flow_sem = refs[7:]
    width = tile_buf.shape[-1]
    scen = base_ref.shape[-1]
    per_shard = shard_refs[0].shape[0]
    blocks = own_base_ref.shape[0]

    def find(source, made):
        info_ref = info_refs[source]

        def look(slot, made):
            block = info_ref[1 + slots + slot]
            owner = block // per_shard
            rel_z = lax.rem(owner // ny - place_ref[0] + nz, nz)
            inner = lax.rem(block, per_shard)
            in_wanted = jnp.logical_and(rel_z >= wanted[0], rel_z <= wanted[-1])
            here = jnp.logical_and(lax.rem(owner, ny) == place_ref[1], in_wanted)

            @pl.when(here)
            def fetch():
                work_ref[0, made] = source * blocks + info_ref[1 + slot]
                work_ref[1, made] = ((rel_z - wanted[0]) * per_shard + inner) * width
                pltpu.make_async_copy(
                    lodf_refs[source].at[slot], tile_buf.at[made], tile_sem.at[made]
                ).start()
                for index in wanted:

                    @pl.when(rel_z == index)
                    def start_flow():
                        pltpu.make_async_copy(
                            shard_refs[index].at[inner], flow_buf.at[made], flow_sem.at[made]
                        ).start()

            return made + here.astype(jnp.int32)

        return lax.fori_loop(0, info_ref[0], look, made)

    count = jnp.int32(0)
    for source in range(sources):
        count = find(source, count)
    base_ref[:blocks] = own_base_ref[...]
    inverse_ref[:blocks] = own_inverse_ref[...]
    if sources > 1:
        other_ref = other_refs[0]
        parts = other_ref[blocks * width : blocks * width + TAIL, :].astype(jnp.float32)
        rating = parts[:blocks] + parts[blocks : 2 * blocks] + parts[2 * blocks : 3 * blocks]
        scaled(other_ref, rating, base_ref.at[blocks:], inverse_ref.at[blocks:])
    grad_mon_ref[...] = before_refs[0][...] if added else jnp.zeros_like(grad_mon_ref)
    grad_out_ref[...] = jnp.zeros_like(grad_out_ref)
    weight = weight_ref[...]

    def one_tile(item, unused):
        mon_block = work_ref[0, item]
        out_row = work_ref[1, item]
        pltpu.make_async_copy(lodf_refs[0].at[0], tile_buf.at[item], tile_sem.at[item]).wait()
        pltpu.make_async_copy(shard_refs[0].at[0], flow_buf.at[item], flow_sem.at[item]).wait()
        ratio_ref[...] = tile_buf[item].astype(jnp.float32) * inverse_ref[mon_block]
        flow_ref[...] = flow_buf[item].astype(jnp.float32)
        sums_ref[...] = jnp.zeros_like(sums_ref)

        def one_chunk(chunk, unused):
            rows = pl.ds(pl.multiple_of(chunk * CHUNK, CHUNK), CHUNK)
            ratio = ratio_ref[rows, :]
            base = base_ref[mon_block, rows, :]
            total = jnp.zeros_like(base)
            for k in range(width):
                coupling = jnp.broadcast_to(ratio[:, k : k + 1], (CHUNK, scen))
                p = base + coupling * flow_ref[k : k + 1, :]
                t = jnp.exp2(p * p)
                z = t + math.e
                d = ((jnp.log2(z) - LOG2E) * p) * (t * pl.reciprocal(z, approx=True))
                total = total + d
                part = jnp.sum((coupling * d).reshape(CHUNK // 8, 8, scen), axis=0)
                sums_ref[8 * k : 8 * k + 8, :] += part
            scale = inverse_ref[mon_block, rows, :] * weight
            grad_mon_ref[mon_block, rows, :] += total * scale
            return unused

        lax.fori_loop(0, width // CHUNK, one_chunk, 0)
        gradient = sums_ref[pl.ds(0, width, stride=8), :]
        for row in range(1, 8):
            gradient = gradient + sums_ref[pl.ds(row, width, stride=8), :]
        at = pl.ds(pl.multiple_of(out_row, width), width)
        grad_out_ref[at, :] += gradient * weight
        return unused

    lax.fori_loop(0, count, one_tile, 0)


def prepare(mon_flow, rating, info, tiles, shard):
    width, scen = tiles.shape[-1], mon_flow.shape[1]
    rows = mon_flow.shape[0]
    by_block = jax.ShapeDtypeStruct((rows // width, width, scen), jnp.float32)
    info = jnp.pad(info.astype(jnp.float32), (0, width - info.shape[0]))
    return pl.pallas_call(
        prepare_kernel,
        out_shape=(
            by_block,
            by_block,
            jax.ShapeDtypeStruct((rows + TAIL, scen), mon_flow.dtype),
            jax.ShapeDtypeStruct(tiles.shape, tiles.dtype),
            jax.ShapeDtypeStruct(shard.shape, shard.dtype),
        ),
        in_specs=[VMEM] * 5,
        out_specs=(VMEM,) * 5,
        compiler_params=PARAMS,
        cost_estimate=pl.CostEstimate(flops=1 << 22, bytes_accessed=4 << 20, transcendentals=0),
        name="prepare",
    )(mon_flow, rating.reshape(-1, width), info[None], tiles, shard)


def run_tiles(place, infos, shards, ny, lodfs, prepared, weight, others, wanted, before=None):
    sources, nz = len(lodfs), len(shards)
    slots, width, _ = lodfs[0].shape
    base, inverse = prepared
    blocks, _, scen = base.shape
    items = sources * slots
    added = [] if before is None else [before]
    elements = items // 2 * width * width * scen

    def body(*refs):
        tiles_kernel(slots, sources, ny, nz, wanted, len(added), *refs)

    return pl.pallas_call(
        body,
        out_shape=(
            jax.ShapeDtypeStruct((sources * blocks, width, scen), jnp.float32),
            jax.ShapeDtypeStruct((len(wanted) * shards[0].shape[0] * width, scen), jnp.float32),
        ),
        in_specs=[SMEM] * (1 + sources)
        + [ANY] * (nz + sources)
        + [VMEM] * (3 + len(others) + len(added)),
        out_specs=(VMEM, VMEM),
        scratch_shapes=[
            pltpu.SMEM((2, items), jnp.int32),
            pltpu.VMEM((width, width), jnp.float32),
            pltpu.VMEM((8 * width, scen), jnp.float32),
            pltpu.VMEM((width, scen), jnp.float32),
            pltpu.VMEM((sources * blocks, width, scen), jnp.float32),
            pltpu.VMEM((sources * blocks, width, scen), jnp.float32),
            pltpu.VMEM((items, width, width), lodfs[0].dtype),
            pltpu.VMEM((items, width, scen), shards[0].dtype),
            pltpu.SemaphoreType.DMA((items,)),
            pltpu.SemaphoreType.DMA((items,)),
        ],
        compiler_params=PARAMS,
        cost_estimate=pl.CostEstimate(
            flops=14 * elements, bytes_accessed=64 << 20, transcendentals=2 * elements
        ),
        name="tiles",
    )(place, *infos, *shards, *lodfs, base, inverse, weight, *others, *added)


def pack_info(tile_mon, tile_out, tile_count):
    return jnp.concatenate([tile_count.reshape(-1), tile_mon.reshape(-1), tile_out.reshape(-1)])


def shifted(n_mon, ny, dy, dz):
    nz = n_mon // ny
    return [
        (z * ny + y, (z + dz) % nz * ny + (y + dy) % ny) for z in range(nz) for y in range(ny)
    ]


def local_pairs(n_mon, n_out, *args):
    ny, nz = 2, n_mon // 2
    mon_flow, out_flow, rating, weights, lodf, tile_mon, tile_out, tile_count = args
    width = lodf.shape[-1]
    rows, scen = mon_flow.shape
    beside = shifted(n_mon, ny, 1, 0)

    def across(part):
        return lax.ppermute(part, "mon", beside)

    own = out_flow[0].reshape(-1, width, scen)
    arrived = [lax.ppermute(own, "mon", shifted(n_mon, ny, 0, nz - r)) for r in range(1, nz)]
    info = pack_info(tile_mon, tile_out, tile_count)
    tiles = lodf[0, 0]
    other_tiles = across(tiles)
    base, inverse, packed, tiles, own = prepare(mon_flow, rating, info, tiles, own)
    other = across(packed)
    other_info = other[rows + 3 * (rows // width), : info.shape[0]].astype(jnp.int32)
    me = lax.axis_index("mon")
    place = jnp.stack([me // ny, me % ny]).astype(jnp.int32)
    common = (
        place, [info, other_info], [own] + arrived, ny, [tiles, other_tiles],
        (base, inverse), (weights * (4.0 / width / LOG2E**2)).reshape(1, -1), [other]
    )
    mon_part, out_part = run_tiles(*common, tuple(range(nz)))
    out_part = out_part.reshape(nz, -1, scen)
    come = [lax.ppermute(out_part[r], "mon", shifted(n_mon, ny, 0, r)) for r in range(1, nz)]
    mon_part = mon_part.reshape(2, n_out, -1, scen)
    pieces = mon_part[0] + across(mon_part[1])
    mine = lax.axis_index("out")
    grad_mon = lax.dynamic_index_in_dim(pieces, mine, 0, keepdims=False)
    grad_out = out_part[0]
    for part in come:
        grad_out = grad_out + part
    grad_mon, grad_out = lax.optimization_barrier((grad_mon, grad_out))
    for r in range(1, n_out):
        piece = lax.dynamic_index_in_dim(pieces, (mine + r) % n_out, 0, keepdims=False)
        grad_mon = grad_mon + lax.ppermute(
            piece, "out", [(j, (j + r) % n_out) for j in range(n_out)]
        )
    return (grad_mon, grad_out[None])


def local_any(n_mon, n_out, *args):
    mon_flow, out_flow, rating, weights, lodf, tile_mon, tile_out, tile_count = args
    width = lodf.shape[-1]
    scen = mon_flow.shape[1]
    gathered = lax.all_gather(out_flow, "mon", axis=1, tiled=True)[0]
    shard = out_flow[0].reshape(-1, scen)
    info = pack_info(tile_mon, tile_out, tile_count)
    base, inverse, _, tiles, _ = prepare(mon_flow, rating, info, lodf[0, 0], shard)
    mon_part, out_part = run_tiles(
        jnp.zeros((2,), jnp.int32), [info],
        [gathered.reshape(-1, width, scen)], 1, [tiles], (base, inverse),
        (weights * (4.0 / width / LOG2E**2)).reshape(1, -1), [], (0,)
    )
    grad_out = lax.psum_scatter(
        out_part.reshape(1, -1, scen), "mon", scatter_dimension=1, tiled=True
    )
    grad_mon = lax.psum_scatter(
        mon_part.reshape(mon_flow.shape), "out", scatter_dimension=0, tiled=True
    )
    return (grad_mon, grad_out)


def solution(mesh):
    n_mon, n_out = mesh.shape["mon"], mesh.shape["out"]
    chosen = local_pairs if n_mon == 8 else local_any

    def local(*args):
        return chosen(n_mon, n_out, *args)

    in_specs = (
        P("mon", None),
        P("out", "mon", None),
        P("mon"),
        P(),
        P("mon", "out", None, None, None),
        P("mon", "out", None),
        P("mon", "out", None),
        P("mon", "out"),
    )
    out_specs = (P(("mon", "out"), None), P("out", "mon", None))
    return jax.shard_map(local, mesh=mesh, in_specs=in_specs, out_specs=out_specs, check_vma=False)
```

```python
import math

import jax
import jax.numpy as jnp
from jax import lax
from jax.experimental import pallas as pl
from jax.experimental.pallas import tpu as pltpu
from jax.sharding import PartitionSpec as P

LOG2E = 1.0 / math.log(2.0)
ROOT = math.sqrt(LOG2E)
CHUNK = 32
TAIL = 16
VMEM = pl.BlockSpec(memory_space=pltpu.VMEM)
SMEM = pl.BlockSpec(memory_space=pltpu.SMEM)
ANY = pl.BlockSpec(memory_space=pl.ANY)
PARAMS = pltpu.CompilerParams(vmem_limit_bytes=32 << 20)


def scaled(mon_ref, rating, base_ref, inverse_ref):
    blocks, width, scen = base_ref.shape
    for block in range(blocks):
        row = ROOT / rating[block : block + 1, :]
        inverse = jnp.transpose(jnp.broadcast_to(row, (scen, width)))
        rows = mon_ref[block * width : (block + 1) * width, :]
        inverse_ref[block] = inverse
        base_ref[block] = rows.astype(jnp.float32) * inverse


def prepare_kernel(
    mon_ref, rating_ref, info_ref, lodf_ref, shard_ref,
    base_ref, inverse_ref, packed_ref, lodf_out_ref, shard_out_ref
):
    scaled(mon_ref, rating_ref[...], base_ref, inverse_ref)
    rows, width = mon_ref.shape[0], rating_ref.shape[1]
    packed_ref[:rows, :] = mon_ref[...]
    parts, rest = [], rating_ref[...]
    for _ in range(3):
        part = rest.astype(jnp.bfloat16).astype(jnp.float32)
        parts.append(part)
        rest = rest - part
    parts.append(info_ref[...])
    blank = jnp.zeros((TAIL - 1 - 3 * rest.shape[0], width), jnp.float32)
    packed_ref[rows:, :] = jnp.concatenate(parts + [blank], axis=0).astype(packed_ref.dtype)
    lodf_out_ref[...] = lodf_ref[...]
    shard_out_ref[...] = shard_ref[...]


def tiles_kernel(slots, sources, ny, nz, loaded, early, added, *refs):
    place_ref = refs[0]
    info_refs = refs[1 : 1 + sources]
    refs = refs[1 + sources :]
    shard_refs, refs = refs[:loaded], refs[loaded:]
    lodf_refs, refs = refs[:sources], refs[sources:]
    own_base_ref, own_inverse_ref, weight_ref = refs[:3]
    refs = refs[3:]
    other_refs, refs = refs[: sources - 1], refs[sources - 1 :]
    before_refs, refs = refs[: 2 * added], refs[2 * added :]
    grad_mon_ref, grad_out_ref, work_ref, ratio_ref, sums_ref, flow_ref, base_ref = refs[:7]
    inverse_ref, tile_buf, flow_buf, tile_sem, flow_sem = refs[7:]
    width = tile_buf.shape[-1]
    scen = base_ref.shape[-1]
    per_shard = shard_refs[0].shape[0]
    blocks = own_base_ref.shape[0]

    def find(source, made):
        info_ref = info_refs[source]

        def look(slot, made):
            block = info_ref[1 + slots + slot]
            owner = block // per_shard
            rel_z = lax.rem(owner // ny - place_ref[0] + nz, nz)
            inner = lax.rem(block, per_shard)
            here = lax.rem(owner, ny) == place_ref[1]
            if early:
                here = jnp.logical_and(here, rel_z == 0)
            elif added and source == 0:
                here = jnp.logical_and(here, rel_z != 0)

            @pl.when(here)
            def fetch():
                work_ref[0, made] = source * blocks + info_ref[1 + slot]
                work_ref[1, made] = (rel_z * per_shard + inner) * width
                pltpu.make_async_copy(
                    lodf_refs[source].at[slot], tile_buf.at[made], tile_sem.at[made]
                ).start()
                for index in range(loaded):

                    @pl.when(rel_z == index)
                    def start_flow():
                        pltpu.make_async_copy(
                            shard_refs[index].at[inner], flow_buf.at[made], flow_sem.at[made]
                        ).start()

            return made + here.astype(jnp.int32)

        return lax.fori_loop(0, info_ref[0], look, made)

    count = jnp.int32(0)
    for source in range(sources):
        count = find(source, count)
    base_ref[:blocks] = own_base_ref[...]
    inverse_ref[:blocks] = own_inverse_ref[...]
    if sources > 1:
        other_ref = other_refs[0]
        parts = other_ref[blocks * width : blocks * width + TAIL, :].astype(jnp.float32)
        rating = parts[:blocks] + parts[blocks : 2 * blocks] + parts[2 * blocks : 3 * blocks]
        scaled(other_ref, rating, base_ref.at[blocks:], inverse_ref.at[blocks:])
    for index, ref in enumerate((grad_mon_ref, grad_out_ref)):
        ready = 0
        if added:
            ready = before_refs[index].shape[0]
            ref[:ready] = before_refs[index][...]
        if ready < ref.shape[0]:
            ref[ready:] = jnp.zeros((ref.shape[0] - ready,) + ref.shape[1:], ref.dtype)
    weight = weight_ref[...]

    def one_tile(item, unused):
        mon_block = work_ref[0, item]
        out_row = work_ref[1, item]
        pltpu.make_async_copy(lodf_refs[0].at[0], tile_buf.at[item], tile_sem.at[item]).wait()
        pltpu.make_async_copy(shard_refs[0].at[0], flow_buf.at[item], flow_sem.at[item]).wait()
        ratio_ref[...] = tile_buf[item].astype(jnp.float32) * inverse_ref[mon_block]
        flow_ref[...] = flow_buf[item].astype(jnp.float32)
        sums_ref[...] = jnp.zeros_like(sums_ref)

        def one_chunk(chunk, unused):
            rows = pl.ds(pl.multiple_of(chunk * CHUNK, CHUNK), CHUNK)
            ratio = ratio_ref[rows, :]
            base = base_ref[mon_block, rows, :]
            total = jnp.zeros_like(base)
            for k in range(width):
                coupling = jnp.broadcast_to(ratio[:, k : k + 1], (CHUNK, scen))
                p = base + coupling * flow_ref[k : k + 1, :]
                t = jnp.exp2(p * p)
                z = t + math.e
                d = ((jnp.log2(z) - LOG2E) * p) * (t * pl.reciprocal(z, approx=True))
                total = total + d
                part = jnp.sum((coupling * d).reshape(CHUNK // 8, 8, scen), axis=0)
                sums_ref[8 * k : 8 * k + 8, :] += part
            scale = inverse_ref[mon_block, rows, :] * weight
            grad_mon_ref[mon_block, rows, :] += total * scale
            return unused

        lax.fori_loop(0, width // CHUNK, one_chunk, 0)
        gradient = sums_ref[pl.ds(0, width, stride=8), :]
        for row in range(1, 8):
            gradient = gradient + sums_ref[pl.ds(row, width, stride=8), :]
        at = pl.ds(pl.multiple_of(out_row, width), width)
        grad_out_ref[at, :] += gradient * weight
        return unused

    lax.fori_loop(0, count, one_tile, 0)


def prepare(mon_flow, rating, info, tiles, shard):
    width, scen = tiles.shape[-1], mon_flow.shape[1]
    rows = mon_flow.shape[0]
    by_block = jax.ShapeDtypeStruct((rows // width, width, scen), jnp.float32)
    info = jnp.pad(info.astype(jnp.float32), (0, width - info.shape[0]))
    return pl.pallas_call(
        prepare_kernel,
        out_shape=(
            by_block,
            by_block,
            jax.ShapeDtypeStruct((rows + TAIL, scen), mon_flow.dtype),
            jax.ShapeDtypeStruct(tiles.shape, tiles.dtype),
            jax.ShapeDtypeStruct(shard.shape, shard.dtype),
        ),
        in_specs=[VMEM] * 5,
        out_specs=(VMEM,) * 5,
        compiler_params=PARAMS,
        cost_estimate=pl.CostEstimate(flops=1 << 22, bytes_accessed=4 << 20, transcendentals=0),
        name="prepare",
    )(mon_flow, rating.reshape(-1, width), info[None], tiles, shard)


def run_tiles(place, infos, shards, ny, nz, lodfs, prepared, weight, others, before=()):
    sources, loaded = len(lodfs), len(shards)
    early = loaded < nz
    slots, width, _ = lodfs[0].shape
    base, inverse = prepared
    blocks, _, scen = base.shape
    items = sources * slots
    elements = (1 if early else items // 2) * width * width * scen

    def body(*refs):
        tiles_kernel(slots, sources, ny, nz, loaded, early, len(before) // 2, *refs)

    return pl.pallas_call(
        body,
        out_shape=(
            jax.ShapeDtypeStruct((sources * blocks, width, scen), jnp.float32),
            jax.ShapeDtypeStruct((loaded * shards[0].shape[0] * width, scen), jnp.float32),
        ),
        in_specs=[SMEM] * (1 + sources)
        + [ANY] * (loaded + sources)
        + [VMEM] * (3 + len(others) + len(before)),
        out_specs=(VMEM, VMEM),
        scratch_shapes=[
            pltpu.SMEM((2, items), jnp.int32),
            pltpu.VMEM((width, width), jnp.float32),
            pltpu.VMEM((8 * width, scen), jnp.float32),
            pltpu.VMEM((width, scen), jnp.float32),
            pltpu.VMEM((sources * blocks, width, scen), jnp.float32),
            pltpu.VMEM((sources * blocks, width, scen), jnp.float32),
            pltpu.VMEM((items, width, width), lodfs[0].dtype),
            pltpu.VMEM((items, width, scen), shards[0].dtype),
            pltpu.SemaphoreType.DMA((items,)),
            pltpu.SemaphoreType.DMA((items,)),
        ],
        compiler_params=PARAMS,
        cost_estimate=pl.CostEstimate(
            flops=14 * elements, bytes_accessed=(4 if early else 64) << 20, transcendentals=2 * elements
        ),
        name="tiles",
    )(place, *infos, *shards, *lodfs, base, inverse, weight, *others, *before)


def pack_info(tile_mon, tile_out, tile_count):
    return jnp.concatenate([tile_count.reshape(-1), tile_mon.reshape(-1), tile_out.reshape(-1)])


def shifted(n_mon, ny, dy, dz):
    nz = n_mon // ny
    return [
        (z * ny + y, (z + dz) % nz * ny + (y + dy) % ny) for z in range(nz) for y in range(ny)
    ]


def local_pairs(n_mon, n_out, *args):
    ny, nz = 2, n_mon // 2
    mon_flow, out_flow, rating, weights, lodf, tile_mon, tile_out, tile_count = args
    width = lodf.shape[-1]
    rows, scen = mon_flow.shape
    beside = shifted(n_mon, ny, 1, 0)

    def across(part):
        return lax.ppermute(part, "mon", beside)

    own = out_flow[0].reshape(-1, width, scen)
    arrived = [lax.ppermute(own, "mon", shifted(n_mon, ny, 0, nz - r)) for r in range(1, nz)]
    info = pack_info(tile_mon, tile_out, tile_count)
    tiles = lodf[0, 0]
    other_tiles = across(tiles)
    base, inverse, packed, tiles, own = prepare(mon_flow, rating, info, tiles, own)
    other = across(packed)
    other_info = other[rows + 3 * (rows // width), : info.shape[0]].astype(jnp.int32)
    me = lax.axis_index("mon")
    place = jnp.stack([me // ny, me % ny]).astype(jnp.int32)
    weight = (weights * (4.0 / width / LOG2E**2)).reshape(1, -1)
    prepared = base, inverse
    before = run_tiles(place, [info], [own], ny, nz, [tiles], prepared, weight, [])
    mon_part, out_part = run_tiles(
        place, [info, other_info], [own] + arrived, ny, nz, [tiles, other_tiles], prepared, weight,
        [other], before
    )
    out_part = out_part.reshape(nz, -1, scen)
    come = [lax.ppermute(out_part[r], "mon", shifted(n_mon, ny, 0, r)) for r in range(1, nz)]
    mon_part = mon_part.reshape(2, n_out, -1, scen)
    pieces = mon_part[0] + across(mon_part[1])
    mine = lax.axis_index("out")
    grad_mon = lax.dynamic_index_in_dim(pieces, mine, 0, keepdims=False)
    grad_out = out_part[0]
    for part in come:
        grad_out = grad_out + part
    grad_mon, grad_out = lax.optimization_barrier((grad_mon, grad_out))
    for r in range(1, n_out):
        piece = lax.dynamic_index_in_dim(pieces, (mine + r) % n_out, 0, keepdims=False)
        grad_mon = grad_mon + lax.ppermute(
            piece, "out", [(j, (j + r) % n_out) for j in range(n_out)]
        )
    return (grad_mon, grad_out[None])


def local_any(n_mon, n_out, *args):
    mon_flow, out_flow, rating, weights, lodf, tile_mon, tile_out, tile_count = args
    width = lodf.shape[-1]
    scen = mon_flow.shape[1]
    gathered = lax.all_gather(out_flow, "mon", axis=1, tiled=True)[0]
    shard = out_flow[0].reshape(-1, scen)
    info = pack_info(tile_mon, tile_out, tile_count)
    base, inverse, _, tiles, _ = prepare(mon_flow, rating, info, lodf[0, 0], shard)
    mon_part, out_part = run_tiles(
        jnp.zeros((2,), jnp.int32), [info],
        [gathered.reshape(-1, width, scen)], 1, 1, [tiles], (base, inverse),
        (weights * (4.0 / width / LOG2E**2)).reshape(1, -1), []
    )
    grad_out = lax.psum_scatter(
        out_part.reshape(1, -1, scen), "mon", scatter_dimension=1, tiled=True
    )
    grad_mon = lax.psum_scatter(
        mon_part.reshape(mon_flow.shape), "out", scatter_dimension=0, tiled=True
    )
    return (grad_mon, grad_out)


def solution(mesh):
    n_mon, n_out = mesh.shape["mon"], mesh.shape["out"]
    chosen = local_pairs if n_mon == 8 else local_any

    def local(*args):
        return chosen(n_mon, n_out, *args)

    in_specs = (
        P("mon", None),
        P("out", "mon", None),
        P("mon"),
        P(),
        P("mon", "out", None, None, None),
        P("mon", "out", None),
        P("mon", "out", None),
        P("mon", "out"),
    )
    out_specs = (P(("mon", "out"), None), P("out", "mon", None))
    return jax.shard_map(local, mesh=mesh, in_specs=in_specs, out_specs=out_specs, check_vma=False)
```

```python
import math

import jax
import jax.numpy as jnp
from jax import lax
from jax.experimental import pallas as pl
from jax.experimental.pallas import tpu as pltpu
from jax.sharding import PartitionSpec as P

LOG2E = 1.0 / math.log(2.0)
ROOT = math.sqrt(LOG2E)
CHUNK = 64
TAIL = 16
VMEM = pl.BlockSpec(memory_space=pltpu.VMEM)
SMEM = pl.BlockSpec(memory_space=pltpu.SMEM)
ANY = pl.BlockSpec(memory_space=pl.ANY)
PARAMS = pltpu.CompilerParams(vmem_limit_bytes=32 << 20)


def scaled(mon_ref, rating, base_ref, inverse_ref):
    blocks, width, scen = base_ref.shape
    for block in range(blocks):
        row = ROOT / rating[block : block + 1, :]
        inverse = jnp.transpose(jnp.broadcast_to(row, (scen, width)))
        rows = mon_ref[block * width : (block + 1) * width, :]
        inverse_ref[block] = inverse
        base_ref[block] = rows.astype(jnp.float32) * inverse


def prepare_kernel(
    mon_ref, rating_ref, info_ref, lodf_ref, shard_ref,
    base_ref, inverse_ref, packed_ref, lodf_out_ref, shard_out_ref
):
    scaled(mon_ref, rating_ref[...], base_ref, inverse_ref)
    rows, width = mon_ref.shape[0], rating_ref.shape[1]
    packed_ref[:rows, :] = mon_ref[...]
    parts, rest = [], rating_ref[...]
    for _ in range(3):
        part = rest.astype(jnp.bfloat16).astype(jnp.float32)
        parts.append(part)
        rest = rest - part
    parts.append(info_ref[...])
    blank = jnp.zeros((TAIL - 1 - 3 * rest.shape[0], width), jnp.float32)
    packed_ref[rows:, :] = jnp.concatenate(parts + [blank], axis=0).astype(packed_ref.dtype)
    lodf_out_ref[...] = lodf_ref[...]
    shard_out_ref[...] = shard_ref[...]


def tiles_kernel(slots, sources, ny, nz, loaded, early, added, *refs):
    place_ref = refs[0]
    info_refs = refs[1 : 1 + sources]
    refs = refs[1 + sources :]
    shard_refs, refs = refs[:loaded], refs[loaded:]
    lodf_refs, refs = refs[:sources], refs[sources:]
    own_base_ref, own_inverse_ref, weight_ref = refs[:3]
    refs = refs[3:]
    other_refs, refs = refs[: sources - 1], refs[sources - 1 :]
    before_refs, refs = refs[: 2 * added], refs[2 * added :]
    grad_mon_ref, grad_out_ref, work_ref, ratio_ref, sums_ref, flow_ref, base_ref = refs[:7]
    inverse_ref, tile_buf, flow_buf, tile_sem, flow_sem = refs[7:]
    width = tile_buf.shape[-1]
    scen = base_ref.shape[-1]
    per_shard = shard_refs[0].shape[0]
    blocks = own_base_ref.shape[0]

    def find(source, made):
        info_ref = info_refs[source]

        def look(slot, made):
            block = info_ref[1 + slots + slot]
            owner = block // per_shard
            rel_z = lax.rem(owner // ny - place_ref[0] + nz, nz)
            inner = lax.rem(block, per_shard)
            here = lax.rem(owner, ny) == place_ref[1]
            if early:
                here = jnp.logical_and(here, rel_z == 0)
            elif added and source == 0:
                here = jnp.logical_and(here, rel_z != 0)

            @pl.when(here)
            def fetch():
                work_ref[0, made] = source * blocks + info_ref[1 + slot]
                work_ref[1, made] = (rel_z * per_shard + inner) * width
                pltpu.make_async_copy(
                    lodf_refs[source].at[slot], tile_buf.at[made], tile_sem.at[made]
                ).start()
                for index in range(loaded):

                    @pl.when(rel_z == index)
                    def start_flow():
                        pltpu.make_async_copy(
                            shard_refs[index].at[inner], flow_buf.at[made], flow_sem.at[made]
                        ).start()

            return made + here.astype(jnp.int32)

        return lax.fori_loop(0, info_ref[0], look, made)

    count = jnp.int32(0)
    for source in range(sources):
        count = find(source, count)
    base_ref[:blocks] = own_base_ref[...]
    inverse_ref[:blocks] = own_inverse_ref[...]
    if sources > 1:
        other_ref = other_refs[0]
        parts = other_ref[blocks * width : blocks * width + TAIL, :].astype(jnp.float32)
        rating = parts[:blocks] + parts[blocks : 2 * blocks] + parts[2 * blocks : 3 * blocks]
        scaled(other_ref, rating, base_ref.at[blocks:], inverse_ref.at[blocks:])
    for index, ref in enumerate((grad_mon_ref, grad_out_ref)):
        ready = 0
        if added:
            ready = before_refs[index].shape[0]
            ref[:ready] = before_refs[index][...]
        if ready < ref.shape[0]:
            ref[ready:] = jnp.zeros((ref.shape[0] - ready,) + ref.shape[1:], ref.dtype)
    weight = weight_ref[...]

    def one_tile(item, unused):
        mon_block = work_ref[0, item]
        out_row = work_ref[1, item]
        pltpu.make_async_copy(lodf_refs[0].at[0], tile_buf.at[item], tile_sem.at[item]).wait()
        pltpu.make_async_copy(shard_refs[0].at[0], flow_buf.at[item], flow_sem.at[item]).wait()
        ratio_ref[...] = tile_buf[item].astype(jnp.float32) * inverse_ref[mon_block]
        flow_ref[...] = flow_buf[item].astype(jnp.float32)
        sums_ref[...] = jnp.zeros_like(sums_ref)

        def one_chunk(chunk, unused):
            rows = pl.ds(pl.multiple_of(chunk * CHUNK, CHUNK), CHUNK)
            ratio = ratio_ref[rows, :]
            base = base_ref[mon_block, rows, :]
            total = jnp.zeros_like(base)
            for k in range(width):
                coupling = jnp.broadcast_to(ratio[:, k : k + 1], (CHUNK, scen))
                p = base + coupling * flow_ref[k : k + 1, :]
                t = jnp.exp2(p * p)
                z = t + math.e
                d = ((jnp.log2(z) - LOG2E) * p) * (t * pl.reciprocal(z, approx=True))
                total = total + d
                part = jnp.sum((coupling * d).reshape(CHUNK // 8, 8, scen), axis=0)
                sums_ref[8 * k : 8 * k + 8, :] += part
            scale = inverse_ref[mon_block, rows, :] * weight
            grad_mon_ref[mon_block, rows, :] += total * scale
            return unused

        lax.fori_loop(0, width // CHUNK, one_chunk, 0)
        gradient = sums_ref[pl.ds(0, width, stride=8), :]
        for row in range(1, 8):
            gradient = gradient + sums_ref[pl.ds(row, width, stride=8), :]
        at = pl.ds(pl.multiple_of(out_row, width), width)
        grad_out_ref[at, :] += gradient * weight
        return unused

    lax.fori_loop(0, count, one_tile, 0)


def prepare(mon_flow, rating, info, tiles, shard):
    width, scen = tiles.shape[-1], mon_flow.shape[1]
    rows = mon_flow.shape[0]
    by_block = jax.ShapeDtypeStruct((rows // width, width, scen), jnp.float32)
    info = jnp.pad(info.astype(jnp.float32), (0, width - info.shape[0]))
    return pl.pallas_call(
        prepare_kernel,
        out_shape=(
            by_block,
            by_block,
            jax.ShapeDtypeStruct((rows + TAIL, scen), mon_flow.dtype),
            jax.ShapeDtypeStruct(tiles.shape, tiles.dtype),
            jax.ShapeDtypeStruct(shard.shape, shard.dtype),
        ),
        in_specs=[VMEM] * 5,
        out_specs=(VMEM,) * 5,
        compiler_params=PARAMS,
        cost_estimate=pl.CostEstimate(flops=1 << 22, bytes_accessed=4 << 20, transcendentals=0),
        name="prepare",
    )(mon_flow, rating.reshape(-1, width), info[None], tiles, shard)


def run_tiles(place, infos, shards, ny, nz, lodfs, prepared, weight, others, before=()):
    sources, loaded = len(lodfs), len(shards)
    early = loaded < nz
    slots, width, _ = lodfs[0].shape
    base, inverse = prepared
    blocks, _, scen = base.shape
    items = sources * slots
    elements = (1 if early else items // 2) * width * width * scen

    def body(*refs):
        tiles_kernel(slots, sources, ny, nz, loaded, early, len(before) // 2, *refs)

    return pl.pallas_call(
        body,
        out_shape=(
            jax.ShapeDtypeStruct((sources * blocks, width, scen), jnp.float32),
            jax.ShapeDtypeStruct((loaded * shards[0].shape[0] * width, scen), jnp.float32),
        ),
        in_specs=[SMEM] * (1 + sources)
        + [ANY] * (loaded + sources)
        + [VMEM] * (3 + len(others) + len(before)),
        out_specs=(VMEM, VMEM),
        scratch_shapes=[
            pltpu.SMEM((2, items), jnp.int32),
            pltpu.VMEM((width, width), jnp.float32),
            pltpu.VMEM((8 * width, scen), jnp.float32),
            pltpu.VMEM((width, scen), jnp.float32),
            pltpu.VMEM((sources * blocks, width, scen), jnp.float32),
            pltpu.VMEM((sources * blocks, width, scen), jnp.float32),
            pltpu.VMEM((items, width, width), lodfs[0].dtype),
            pltpu.VMEM((items, width, scen), shards[0].dtype),
            pltpu.SemaphoreType.DMA((items,)),
            pltpu.SemaphoreType.DMA((items,)),
        ],
        compiler_params=PARAMS,
        cost_estimate=pl.CostEstimate(
            flops=14 * elements, bytes_accessed=(4 if early else 64) << 20, transcendentals=2 * elements
        ),
        name="tiles",
    )(place, *infos, *shards, *lodfs, base, inverse, weight, *others, *before)


def pack_info(tile_mon, tile_out, tile_count):
    return jnp.concatenate([tile_count.reshape(-1), tile_mon.reshape(-1), tile_out.reshape(-1)])


def shifted(n_mon, ny, dy, dz):
    nz = n_mon // ny
    return [
        (z * ny + y, (z + dz) % nz * ny + (y + dy) % ny) for z in range(nz) for y in range(ny)
    ]


def local_pairs(n_mon, n_out, *args):
    ny, nz = 2, n_mon // 2
    mon_flow, out_flow, rating, weights, lodf, tile_mon, tile_out, tile_count = args
    width = lodf.shape[-1]
    rows, scen = mon_flow.shape
    beside = shifted(n_mon, ny, 1, 0)

    def across(part):
        return lax.ppermute(part, "mon", beside)

    own = out_flow[0].reshape(-1, width, scen)
    arrived = [lax.ppermute(own, "mon", shifted(n_mon, ny, 0, nz - r)) for r in range(1, nz)]
    info = pack_info(tile_mon, tile_out, tile_count)
    tiles = lodf[0, 0]
    other_tiles = across(tiles)
    base, inverse, packed, tiles, own = prepare(mon_flow, rating, info, tiles, own)
    other = across(packed)
    other_info = other[rows + 3 * (rows // width), : info.shape[0]].astype(jnp.int32)
    me = lax.axis_index("mon")
    place = jnp.stack([me // ny, me % ny]).astype(jnp.int32)
    weight = (weights * (4.0 / width / LOG2E**2)).reshape(1, -1)
    prepared = base, inverse
    before = run_tiles(place, [info], [own], ny, nz, [tiles], prepared, weight, [])
    mon_part, out_part = run_tiles(
        place, [info, other_info], [own] + arrived, ny, nz, [tiles, other_tiles], prepared, weight,
        [other], before
    )
    out_part = out_part.reshape(nz, -1, scen)
    come = [lax.ppermute(out_part[r], "mon", shifted(n_mon, ny, 0, r)) for r in range(1, nz)]
    mon_part = mon_part.reshape(2, n_out, -1, scen)
    pieces = mon_part[0] + across(mon_part[1])
    mine = lax.axis_index("out")
    grad_mon = lax.dynamic_index_in_dim(pieces, mine, 0, keepdims=False)
    grad_out = out_part[0]
    for part in come:
        grad_out = grad_out + part
    grad_mon, grad_out = lax.optimization_barrier((grad_mon, grad_out))
    for r in range(1, n_out):
        piece = lax.dynamic_index_in_dim(pieces, (mine + r) % n_out, 0, keepdims=False)
        grad_mon = grad_mon + lax.ppermute(
            piece, "out", [(j, (j + r) % n_out) for j in range(n_out)]
        )
    return (grad_mon, grad_out[None])


def local_any(n_mon, n_out, *args):
    mon_flow, out_flow, rating, weights, lodf, tile_mon, tile_out, tile_count = args
    width = lodf.shape[-1]
    scen = mon_flow.shape[1]
    gathered = lax.all_gather(out_flow, "mon", axis=1, tiled=True)[0]
    shard = out_flow[0].reshape(-1, scen)
    info = pack_info(tile_mon, tile_out, tile_count)
    base, inverse, _, tiles, _ = prepare(mon_flow, rating, info, lodf[0, 0], shard)
    mon_part, out_part = run_tiles(
        jnp.zeros((2,), jnp.int32), [info],
        [gathered.reshape(-1, width, scen)], 1, 1, [tiles], (base, inverse),
        (weights * (4.0 / width / LOG2E**2)).reshape(1, -1), []
    )
    grad_out = lax.psum_scatter(
        out_part.reshape(1, -1, scen), "mon", scatter_dimension=1, tiled=True
    )
    grad_mon = lax.psum_scatter(
        mon_part.reshape(mon_flow.shape), "out", scatter_dimension=0, tiled=True
    )
    return (grad_mon, grad_out)


def solution(mesh):
    n_mon, n_out = mesh.shape["mon"], mesh.shape["out"]
    chosen = local_pairs if n_mon == 8 else local_any

    def local(*args):
        return chosen(n_mon, n_out, *args)

    in_specs = (
        P("mon", None),
        P("out", "mon", None),
        P("mon"),
        P(),
        P("mon", "out", None, None, None),
        P("mon", "out", None),
        P("mon", "out", None),
        P("mon", "out"),
    )
    out_specs = (P(("mon", "out"), None), P("out", "mon", None))
    return jax.shard_map(local, mesh=mesh, in_specs=in_specs, out_specs=out_specs, check_vma=False)
```

```python
import math

import jax
import jax.numpy as jnp
from jax import lax
from jax.experimental import pallas as pl
from jax.experimental.pallas import tpu as pltpu
from jax.sharding import PartitionSpec as P

LOG2E = 1.0 / math.log(2.0)
ROOT = math.sqrt(LOG2E)
CHUNK = 64
TAIL = 16
VMEM = pl.BlockSpec(memory_space=pltpu.VMEM)
SMEM = pl.BlockSpec(memory_space=pltpu.SMEM)
ANY = pl.BlockSpec(memory_space=pl.ANY)
PARAMS = pltpu.CompilerParams(vmem_limit_bytes=32 << 20)


def scaled(mon_ref, rating, base_ref, inverse_ref):
    blocks, width, scen = base_ref.shape
    for block in range(blocks):
        row = ROOT / rating[block : block + 1, :]
        inverse = jnp.transpose(jnp.broadcast_to(row, (scen, width)))
        rows = mon_ref[block * width : (block + 1) * width, :]
        inverse_ref[block] = inverse
        base_ref[block] = rows.astype(jnp.float32) * inverse


def prepare_kernel(
    mon_ref, rating_ref, info_ref, lodf_ref, shard_ref,
    base_ref, inverse_ref, packed_ref, lodf_out_ref, shard_out_ref
):
    scaled(mon_ref, rating_ref[...], base_ref, inverse_ref)
    rows, width = mon_ref.shape[0], rating_ref.shape[1]
    packed_ref[:rows, :] = mon_ref[...]
    parts, rest = [], rating_ref[...]
    for _ in range(3):
        part = rest.astype(jnp.bfloat16).astype(jnp.float32)
        parts.append(part)
        rest = rest - part
    parts.append(info_ref[...])
    blank = jnp.zeros((TAIL - 1 - 3 * rest.shape[0], width), jnp.float32)
    packed_ref[rows:, :] = jnp.concatenate(parts + [blank], axis=0).astype(packed_ref.dtype)
    lodf_out_ref[...] = lodf_ref[...]
    shard_out_ref[...] = shard_ref[...]


def tiles_kernel(slots, sources, ny, nz, loaded, early, added, *refs):
    place_ref = refs[0]
    info_refs = refs[1 : 1 + sources]
    refs = refs[1 + sources :]
    shard_refs, refs = refs[:loaded], refs[loaded:]
    lodf_refs, refs = refs[:sources], refs[sources:]
    own_base_ref, own_inverse_ref, weight_ref = refs[:3]
    refs = refs[3:]
    other_refs, refs = refs[: sources - 1], refs[sources - 1 :]
    before_refs, refs = refs[: 2 * added], refs[2 * added :]
    grad_mon_ref, grad_out_ref, work_ref, ratio_ref, sums_ref, flow_ref, base_ref = refs[:7]
    inverse_ref, tile_buf, flow_buf, tile_sem, flow_sem = refs[7:]
    width = tile_buf.shape[-1]
    scen = base_ref.shape[-1]
    per_shard = shard_refs[0].shape[0]
    blocks = own_base_ref.shape[0]

    def find(source, made):
        info_ref = info_refs[source]

        def look(slot, made):
            block = info_ref[1 + slots + slot]
            owner = block // per_shard
            rel_z = lax.rem(owner // ny - place_ref[0] + nz, nz)
            inner = lax.rem(block, per_shard)
            here = lax.rem(owner, ny) == place_ref[1]
            if early:
                here = jnp.logical_and(here, rel_z == 0)
            elif added and source == 0:
                here = jnp.logical_and(here, rel_z != 0)

            @pl.when(here)
            def fetch():
                work_ref[0, made] = source * blocks + info_ref[1 + slot]
                work_ref[1, made] = (rel_z * per_shard + inner) * width
                pltpu.make_async_copy(
                    lodf_refs[source].at[slot], tile_buf.at[made], tile_sem.at[made]
                ).start()
                for index in range(loaded):

                    @pl.when(rel_z == index)
                    def start_flow():
                        pltpu.make_async_copy(
                            shard_refs[index].at[inner], flow_buf.at[made], flow_sem.at[made]
                        ).start()

            return made + here.astype(jnp.int32)

        return lax.fori_loop(0, info_ref[0], look, made)

    count = jnp.int32(0)
    for source in range(sources):
        count = find(source, count)
    base_ref[:blocks] = own_base_ref[...]
    inverse_ref[:blocks] = own_inverse_ref[...]
    if sources > 1:
        other_ref = other_refs[0]
        parts = other_ref[blocks * width : blocks * width + TAIL, :].astype(jnp.float32)
        rating = parts[:blocks] + parts[blocks : 2 * blocks] + parts[2 * blocks : 3 * blocks]
        scaled(other_ref, rating, base_ref.at[blocks:], inverse_ref.at[blocks:])
    for index, ref in enumerate((grad_mon_ref, grad_out_ref)):
        ready = 0
        if added:
            ready = before_refs[index].shape[0]
            ref[:ready] = before_refs[index][...]
        if ready < ref.shape[0]:
            ref[ready:] = jnp.zeros((ref.shape[0] - ready,) + ref.shape[1:], ref.dtype)
    weight = weight_ref[...]

    def one_tile(item, unused):
        mon_block = work_ref[0, item]
        out_row = work_ref[1, item]
        pltpu.make_async_copy(lodf_refs[0].at[0], tile_buf.at[item], tile_sem.at[item]).wait()
        pltpu.make_async_copy(shard_refs[0].at[0], flow_buf.at[item], flow_sem.at[item]).wait()
        ratio_ref[...] = tile_buf[item].astype(jnp.float32) * inverse_ref[mon_block]
        flow_ref[...] = flow_buf[item].astype(jnp.float32)
        for chunk in range(width // CHUNK):
            rows = slice(chunk * CHUNK, (chunk + 1) * CHUNK)
            ratio = ratio_ref[rows, :]
            base = base_ref[mon_block, rows, :]
            total = jnp.zeros_like(base)
            for k in range(width):
                coupling = jnp.broadcast_to(ratio[:, k : k + 1], (CHUNK, scen))
                p = base + coupling * flow_ref[k : k + 1, :]
                t = jnp.exp2(p * p)
                z = t + math.e
                d = ((jnp.log2(z) - LOG2E) * p) * (t * pl.reciprocal(z, approx=True))
                total = total + d
                part = jnp.sum((coupling * d).reshape(CHUNK // 8, 8, scen), axis=0)
                at = slice(8 * k, 8 * k + 8)
                sums_ref[at, :] = part if chunk == 0 else sums_ref[at, :] + part
            scale = inverse_ref[mon_block, rows, :] * weight
            grad_mon_ref[mon_block, rows, :] += total * scale
        gradient = sums_ref[pl.ds(0, width, stride=8), :]
        for row in range(1, 8):
            gradient = gradient + sums_ref[pl.ds(row, width, stride=8), :]
        at = pl.ds(pl.multiple_of(out_row, width), width)
        grad_out_ref[at, :] += gradient * weight
        return unused

    lax.fori_loop(0, count, one_tile, 0)


def prepare(mon_flow, rating, info, tiles, shard):
    width, scen = tiles.shape[-1], mon_flow.shape[1]
    rows = mon_flow.shape[0]
    by_block = jax.ShapeDtypeStruct((rows // width, width, scen), jnp.float32)
    info = jnp.pad(info.astype(jnp.float32), (0, width - info.shape[0]))
    return pl.pallas_call(
        prepare_kernel,
        out_shape=(
            by_block,
            by_block,
            jax.ShapeDtypeStruct((rows + TAIL, scen), mon_flow.dtype),
            jax.ShapeDtypeStruct(tiles.shape, tiles.dtype),
            jax.ShapeDtypeStruct(shard.shape, shard.dtype),
        ),
        in_specs=[VMEM] * 5,
        out_specs=(VMEM,) * 5,
        compiler_params=PARAMS,
        cost_estimate=pl.CostEstimate(flops=1 << 22, bytes_accessed=4 << 20, transcendentals=0),
        name="prepare",
    )(mon_flow, rating.reshape(-1, width), info[None], tiles, shard)


def run_tiles(place, infos, shards, ny, nz, lodfs, prepared, weight, others, before=()):
    sources, loaded = len(lodfs), len(shards)
    early = loaded < nz
    slots, width, _ = lodfs[0].shape
    base, inverse = prepared
    blocks, _, scen = base.shape
    items = sources * slots
    elements = (1 if early else items // 2) * width * width * scen

    def body(*refs):
        tiles_kernel(slots, sources, ny, nz, loaded, early, len(before) // 2, *refs)

    return pl.pallas_call(
        body,
        out_shape=(
            jax.ShapeDtypeStruct((sources * blocks, width, scen), jnp.float32),
            jax.ShapeDtypeStruct((loaded * shards[0].shape[0] * width, scen), jnp.float32),
        ),
        in_specs=[SMEM] * (1 + sources)
        + [ANY] * (loaded + sources)
        + [VMEM] * (3 + len(others) + len(before)),
        out_specs=(VMEM, VMEM),
        scratch_shapes=[
            pltpu.SMEM((2, items), jnp.int32),
            pltpu.VMEM((width, width), jnp.float32),
            pltpu.VMEM((8 * width, scen), jnp.float32),
            pltpu.VMEM((width, scen), jnp.float32),
            pltpu.VMEM((sources * blocks, width, scen), jnp.float32),
            pltpu.VMEM((sources * blocks, width, scen), jnp.float32),
            pltpu.VMEM((items, width, width), lodfs[0].dtype),
            pltpu.VMEM((items, width, scen), shards[0].dtype),
            pltpu.SemaphoreType.DMA((items,)),
            pltpu.SemaphoreType.DMA((items,)),
        ],
        compiler_params=PARAMS,
        cost_estimate=pl.CostEstimate(
            flops=14 * elements, bytes_accessed=(4 if early else 64) << 20, transcendentals=2 * elements
        ),
        name="tiles",
    )(place, *infos, *shards, *lodfs, base, inverse, weight, *others, *before)


def pack_info(tile_mon, tile_out, tile_count):
    return jnp.concatenate([tile_count.reshape(-1), tile_mon.reshape(-1), tile_out.reshape(-1)])


def shifted(n_mon, ny, dy, dz):
    nz = n_mon // ny
    return [
        (z * ny + y, (z + dz) % nz * ny + (y + dy) % ny) for z in range(nz) for y in range(ny)
    ]


def local_pairs(n_mon, n_out, *args):
    ny, nz = 2, n_mon // 2
    mon_flow, out_flow, rating, weights, lodf, tile_mon, tile_out, tile_count = args
    width = lodf.shape[-1]
    rows, scen = mon_flow.shape
    beside = shifted(n_mon, ny, 1, 0)

    def across(part):
        return lax.ppermute(part, "mon", beside)

    own = out_flow[0].reshape(-1, width, scen)
    arrived = [lax.ppermute(own, "mon", shifted(n_mon, ny, 0, nz - r)) for r in range(1, nz)]
    info = pack_info(tile_mon, tile_out, tile_count)
    tiles = lodf[0, 0]
    other_tiles = across(tiles)
    base, inverse, packed, tiles, own = prepare(mon_flow, rating, info, tiles, own)
    other = across(packed)
    other_info = other[rows + 3 * (rows // width), : info.shape[0]].astype(jnp.int32)
    me = lax.axis_index("mon")
    place = jnp.stack([me // ny, me % ny]).astype(jnp.int32)
    weight = (weights * (4.0 / width / LOG2E**2)).reshape(1, -1)
    prepared = base, inverse
    before = run_tiles(place, [info], [own], ny, nz, [tiles], prepared, weight, [])
    mon_part, out_part = run_tiles(
        place, [info, other_info], [own] + arrived, ny, nz, [tiles, other_tiles], prepared, weight,
        [other], before
    )
    out_part = out_part.reshape(nz, -1, scen)
    come = [lax.ppermute(out_part[r], "mon", shifted(n_mon, ny, 0, r)) for r in range(1, nz)]
    mon_part = mon_part.reshape(2, n_out, -1, scen)
    pieces = mon_part[0] + across(mon_part[1])
    mine = lax.axis_index("out")
    grad_mon = lax.dynamic_index_in_dim(pieces, mine, 0, keepdims=False)
    grad_out = out_part[0]
    for part in come:
        grad_out = grad_out + part
    grad_mon, grad_out = lax.optimization_barrier((grad_mon, grad_out))
    for r in range(1, n_out):
        piece = lax.dynamic_index_in_dim(pieces, (mine + r) % n_out, 0, keepdims=False)
        grad_mon = grad_mon + lax.ppermute(
            piece, "out", [(j, (j + r) % n_out) for j in range(n_out)]
        )
    return (grad_mon, grad_out[None])


def local_any(n_mon, n_out, *args):
    mon_flow, out_flow, rating, weights, lodf, tile_mon, tile_out, tile_count = args
    width = lodf.shape[-1]
    scen = mon_flow.shape[1]
    gathered = lax.all_gather(out_flow, "mon", axis=1, tiled=True)[0]
    shard = out_flow[0].reshape(-1, scen)
    info = pack_info(tile_mon, tile_out, tile_count)
    base, inverse, _, tiles, _ = prepare(mon_flow, rating, info, lodf[0, 0], shard)
    mon_part, out_part = run_tiles(
        jnp.zeros((2,), jnp.int32), [info],
        [gathered.reshape(-1, width, scen)], 1, 1, [tiles], (base, inverse),
        (weights * (4.0 / width / LOG2E**2)).reshape(1, -1), []
    )
    grad_out = lax.psum_scatter(
        out_part.reshape(1, -1, scen), "mon", scatter_dimension=1, tiled=True
    )
    grad_mon = lax.psum_scatter(
        mon_part.reshape(mon_flow.shape), "out", scatter_dimension=0, tiled=True
    )
    return (grad_mon, grad_out)


def solution(mesh):
    n_mon, n_out = mesh.shape["mon"], mesh.shape["out"]
    chosen = local_pairs if n_mon == 8 else local_any

    def local(*args):
        return chosen(n_mon, n_out, *args)

    in_specs = (
        P("mon", None),
        P("out", "mon", None),
        P("mon"),
        P(),
        P("mon", "out", None, None, None),
        P("mon", "out", None),
        P("mon", "out", None),
        P("mon", "out"),
    )
    out_specs = (P(("mon", "out"), None), P("out", "mon", None))
    return jax.shard_map(local, mesh=mesh, in_specs=in_specs, out_specs=out_specs, check_vma=False)
```

```python
import math

import jax
import jax.numpy as jnp
from jax import lax
from jax.experimental import pallas as pl
from jax.experimental.pallas import tpu as pltpu
from jax.sharding import PartitionSpec as P

LOG2E = 1.0 / math.log(2.0)
ROOT = math.sqrt(LOG2E)
CHUNK = 64
TAIL = 16
VMEM = pl.BlockSpec(memory_space=pltpu.VMEM)
SMEM = pl.BlockSpec(memory_space=pltpu.SMEM)
ANY = pl.BlockSpec(memory_space=pl.ANY)
PARAMS = pltpu.CompilerParams(vmem_limit_bytes=32 << 20)


def scaled(mon_ref, rating, base_ref, inverse_ref):
    blocks, width, scen = base_ref.shape
    for block in range(blocks):
        row = ROOT / rating[block : block + 1, :]
        inverse = jnp.transpose(jnp.broadcast_to(row, (scen, width)))
        rows = mon_ref[block * width : (block + 1) * width, :]
        inverse_ref[block] = inverse
        base_ref[block] = rows.astype(jnp.float32) * inverse


def prepare_kernel(
    mon_ref, rating_ref, info_ref, lodf_ref, shard_ref,
    base_ref, inverse_ref, packed_ref, lodf_out_ref, shard_out_ref
):
    scaled(mon_ref, rating_ref[...], base_ref, inverse_ref)
    rows, width = mon_ref.shape[0], rating_ref.shape[1]
    packed_ref[:rows, :] = mon_ref[...]
    parts, rest = [], rating_ref[...]
    for _ in range(3):
        part = rest.astype(jnp.bfloat16).astype(jnp.float32)
        parts.append(part)
        rest = rest - part
    parts.append(info_ref[...])
    blank = jnp.zeros((TAIL - 1 - 3 * rest.shape[0], width), jnp.float32)
    packed_ref[rows:, :] = jnp.concatenate(parts + [blank], axis=0).astype(packed_ref.dtype)
    lodf_out_ref[...] = lodf_ref[...]
    shard_out_ref[...] = shard_ref[...]


def tiles_kernel(slots, sources, ny, nz, loaded, early, added, *refs):
    place_ref = refs[0]
    info_refs = refs[1 : 1 + sources]
    refs = refs[1 + sources :]
    shard_refs, refs = refs[:loaded], refs[loaded:]
    lodf_refs, refs = refs[:sources], refs[sources:]
    own_base_ref, own_inverse_ref, weight_ref = refs[:3]
    refs = refs[3:]
    other_refs, refs = refs[: sources - 1], refs[sources - 1 :]
    before_refs, refs = refs[: 2 * added], refs[2 * added :]
    grad_mon_ref, grad_out_ref, work_ref, ratio_ref, sums_ref, flow_ref, base_ref = refs[:7]
    inverse_ref, tile_buf, flow_buf, tile_sem, flow_sem = refs[7:]
    width = tile_buf.shape[-1]
    scen = base_ref.shape[-1]
    per_shard = shard_refs[0].shape[0]
    blocks = own_base_ref.shape[0]

    def find(source, made):
        info_ref = info_refs[source]

        def look(slot, made):
            block = info_ref[1 + slots + slot]
            owner = block // per_shard
            apart = jnp.bitwise_xor(owner // ny, place_ref[0])
            rel_z = lax.rem(apart, 2) * (nz // 2) + apart // 2
            inner = lax.rem(block, per_shard)
            here = lax.rem(owner, ny) == place_ref[1]
            if early:
                here = jnp.logical_and(here, rel_z == 0)
            elif added and source == 0:
                here = jnp.logical_and(here, rel_z != 0)

            @pl.when(here)
            def fetch():
                work_ref[0, made] = source * blocks + info_ref[1 + slot]
                work_ref[1, made] = (rel_z * per_shard + inner) * width
                pltpu.make_async_copy(
                    lodf_refs[source].at[slot], tile_buf.at[made], tile_sem.at[made]
                ).start()
                for index in range(loaded):

                    @pl.when(rel_z == index)
                    def start_flow():
                        pltpu.make_async_copy(
                            shard_refs[index].at[inner], flow_buf.at[made], flow_sem.at[made]
                        ).start()

            return made + here.astype(jnp.int32)

        return lax.fori_loop(0, info_ref[0], look, made)

    count = jnp.int32(0)
    for source in range(sources):
        count = find(source, count)
    base_ref[:blocks] = own_base_ref[...]
    inverse_ref[:blocks] = own_inverse_ref[...]
    if sources > 1:
        other_ref = other_refs[0]
        parts = other_ref[blocks * width : blocks * width + TAIL, :].astype(jnp.float32)
        rating = parts[:blocks] + parts[blocks : 2 * blocks] + parts[2 * blocks : 3 * blocks]
        scaled(other_ref, rating, base_ref.at[blocks:], inverse_ref.at[blocks:])
    for index, ref in enumerate((grad_mon_ref, grad_out_ref)):
        ready = 0
        if added:
            ready = before_refs[index].shape[0]
            ref[:ready] = before_refs[index][...]
        if ready < ref.shape[0]:
            ref[ready:] = jnp.zeros((ref.shape[0] - ready,) + ref.shape[1:], ref.dtype)
    weight = weight_ref[...]

    def one_tile(item, unused):
        mon_block = work_ref[0, item]
        out_row = work_ref[1, item]
        pltpu.make_async_copy(lodf_refs[0].at[0], tile_buf.at[item], tile_sem.at[item]).wait()
        pltpu.make_async_copy(shard_refs[0].at[0], flow_buf.at[item], flow_sem.at[item]).wait()
        ratio_ref[...] = tile_buf[item].astype(jnp.float32) * inverse_ref[mon_block]
        flow_ref[...] = flow_buf[item].astype(jnp.float32)
        sums_ref[...] = jnp.zeros_like(sums_ref)

        def one_chunk(chunk, unused):
            rows = pl.ds(pl.multiple_of(chunk * CHUNK, CHUNK), CHUNK)
            ratio = ratio_ref[rows, :]
            base = base_ref[mon_block, rows, :]
            total = jnp.zeros_like(base)
            for k in range(width):
                coupling = jnp.broadcast_to(ratio[:, k : k + 1], (CHUNK, scen))
                p = base + coupling * flow_ref[k : k + 1, :]
                t = jnp.exp2(p * p)
                z = t + math.e
                d = ((jnp.log2(z) - LOG2E) * p) * (t * pl.reciprocal(z, approx=True))
                total = total + d
                part = jnp.sum((coupling * d).reshape(CHUNK // 8, 8, scen), axis=0)
                sums_ref[8 * k : 8 * k + 8, :] += part
            scale = inverse_ref[mon_block, rows, :] * weight
            grad_mon_ref[mon_block, rows, :] += total * scale
            return unused

        lax.fori_loop(0, width // CHUNK, one_chunk, 0)
        gradient = sums_ref[pl.ds(0, width, stride=8), :]
        for row in range(1, 8):
            gradient = gradient + sums_ref[pl.ds(row, width, stride=8), :]
        at = pl.ds(pl.multiple_of(out_row, width), width)
        grad_out_ref[at, :] += gradient * weight
        return unused

    lax.fori_loop(0, count, one_tile, 0)


def prepare(mon_flow, rating, info, tiles, shard):
    width, scen = tiles.shape[-1], mon_flow.shape[1]
    rows = mon_flow.shape[0]
    by_block = jax.ShapeDtypeStruct((rows // width, width, scen), jnp.float32)
    info = jnp.pad(info.astype(jnp.float32), (0, width - info.shape[0]))
    return pl.pallas_call(
        prepare_kernel,
        out_shape=(
            by_block,
            by_block,
            jax.ShapeDtypeStruct((rows + TAIL, scen), mon_flow.dtype),
            jax.ShapeDtypeStruct(tiles.shape, tiles.dtype),
            jax.ShapeDtypeStruct(shard.shape, shard.dtype),
        ),
        in_specs=[VMEM] * 5,
        out_specs=(VMEM,) * 5,
        compiler_params=PARAMS,
        cost_estimate=pl.CostEstimate(flops=1 << 22, bytes_accessed=4 << 20, transcendentals=0),
        name="prepare",
    )(mon_flow, rating.reshape(-1, width), info[None], tiles, shard)


def run_tiles(place, infos, shards, ny, nz, lodfs, prepared, weight, others, before=()):
    sources, loaded = len(lodfs), len(shards)
    early = loaded < nz
    slots, width, _ = lodfs[0].shape
    base, inverse = prepared
    blocks, _, scen = base.shape
    items = sources * slots
    elements = (1 if early else items // 2) * width * width * scen

    def body(*refs):
        tiles_kernel(slots, sources, ny, nz, loaded, early, len(before) // 2, *refs)

    return pl.pallas_call(
        body,
        out_shape=(
            jax.ShapeDtypeStruct((sources * blocks, width, scen), jnp.float32),
            jax.ShapeDtypeStruct((loaded * shards[0].shape[0] * width, scen), jnp.float32),
        ),
        in_specs=[SMEM] * (1 + sources)
        + [ANY] * (loaded + sources)
        + [VMEM] * (3 + len(others) + len(before)),
        out_specs=(VMEM, VMEM),
        scratch_shapes=[
            pltpu.SMEM((2, items), jnp.int32),
            pltpu.VMEM((width, width), jnp.float32),
            pltpu.VMEM((8 * width, scen), jnp.float32),
            pltpu.VMEM((width, scen), jnp.float32),
            pltpu.VMEM((sources * blocks, width, scen), jnp.float32),
            pltpu.VMEM((sources * blocks, width, scen), jnp.float32),
            pltpu.VMEM((items, width, width), lodfs[0].dtype),
            pltpu.VMEM((items, width, scen), shards[0].dtype),
            pltpu.SemaphoreType.DMA((items,)),
            pltpu.SemaphoreType.DMA((items,)),
        ],
        compiler_params=PARAMS,
        cost_estimate=pl.CostEstimate(
            flops=14 * elements, bytes_accessed=(4 if early else 64) << 20, transcendentals=2 * elements
        ),
        name="tiles",
    )(place, *infos, *shards, *lodfs, base, inverse, weight, *others, *before)


def pack_info(tile_mon, tile_out, tile_count):
    return jnp.concatenate([tile_count.reshape(-1), tile_mon.reshape(-1), tile_out.reshape(-1)])


def crossed(n_mon, ny, dy, dz):
    return [(i, (i // ny ^ dz) * ny + (i % ny ^ dy)) for i in range(n_mon)]


def local_pairs(n_mon, n_out, *args):
    ny, nz = 2, n_mon // 2
    mon_flow, out_flow, rating, weights, lodf, tile_mon, tile_out, tile_count = args
    width = lodf.shape[-1]
    rows, scen = mon_flow.shape
    beside = crossed(n_mon, ny, 1, 0)

    def across(part):
        return lax.ppermute(part, "mon", beside)

    own = out_flow[0].reshape(-1, width, scen)
    apart = [*range(0, nz, 2), *range(1, nz, 2)]
    arrived = [lax.ppermute(own, "mon", crossed(n_mon, ny, 0, r)) for r in apart[1:]]
    info = pack_info(tile_mon, tile_out, tile_count)
    tiles = lodf[0, 0]
    other_tiles = across(tiles)
    base, inverse, packed, tiles, own = prepare(mon_flow, rating, info, tiles, own)
    other = across(packed)
    other_info = other[rows + 3 * (rows // width), : info.shape[0]].astype(jnp.int32)
    me = lax.axis_index("mon")
    place = jnp.stack([me // ny, me % ny]).astype(jnp.int32)
    weight = (weights * (4.0 / width / LOG2E**2)).reshape(1, -1)
    prepared = base, inverse
    before = run_tiles(place, [info], [own], ny, nz, [tiles], prepared, weight, [])
    mon_part, out_part = run_tiles(
        place, [info, other_info], [own] + arrived, ny, nz, [tiles, other_tiles], prepared, weight,
        [other], before
    )
    out_part = out_part.reshape(nz, -1, scen)
    half = nz // 2
    pair = out_part[:half] + lax.ppermute(out_part[half:], "mon", crossed(n_mon, ny, 0, 1))
    come = lax.ppermute(pair[1], "mon", crossed(n_mon, ny, 0, 2))
    mon_part = mon_part.reshape(2, n_out, -1, scen)
    pieces = mon_part[0] + across(mon_part[1])
    mine = lax.axis_index("out")
    grad_mon = lax.dynamic_index_in_dim(pieces, mine, 0, keepdims=False)
    grad_out = pair[0] + come
    grad_mon, grad_out = lax.optimization_barrier((grad_mon, grad_out))
    for r in range(1, n_out):
        piece = lax.dynamic_index_in_dim(pieces, (mine + r) % n_out, 0, keepdims=False)
        grad_mon = grad_mon + lax.ppermute(
            piece, "out", [(j, (j + r) % n_out) for j in range(n_out)]
        )
    return (grad_mon, grad_out[None])


def local_any(n_mon, n_out, *args):
    mon_flow, out_flow, rating, weights, lodf, tile_mon, tile_out, tile_count = args
    width = lodf.shape[-1]
    scen = mon_flow.shape[1]
    gathered = lax.all_gather(out_flow, "mon", axis=1, tiled=True)[0]
    shard = out_flow[0].reshape(-1, scen)
    info = pack_info(tile_mon, tile_out, tile_count)
    base, inverse, _, tiles, _ = prepare(mon_flow, rating, info, lodf[0, 0], shard)
    mon_part, out_part = run_tiles(
        jnp.zeros((2,), jnp.int32), [info],
        [gathered.reshape(-1, width, scen)], 1, 1, [tiles], (base, inverse),
        (weights * (4.0 / width / LOG2E**2)).reshape(1, -1), []
    )
    grad_out = lax.psum_scatter(
        out_part.reshape(1, -1, scen), "mon", scatter_dimension=1, tiled=True
    )
    grad_mon = lax.psum_scatter(
        mon_part.reshape(mon_flow.shape), "out", scatter_dimension=0, tiled=True
    )
    return (grad_mon, grad_out)


def solution(mesh):
    n_mon, n_out = mesh.shape["mon"], mesh.shape["out"]
    chosen = local_pairs if n_mon == 8 else local_any

    def local(*args):
        return chosen(n_mon, n_out, *args)

    in_specs = (
        P("mon", None),
        P("out", "mon", None),
        P("mon"),
        P(),
        P("mon", "out", None, None, None),
        P("mon", "out", None),
        P("mon", "out", None),
        P("mon", "out"),
    )
    out_specs = (P(("mon", "out"), None), P("out", "mon", None))
    return jax.shard_map(local, mesh=mesh, in_specs=in_specs, out_specs=out_specs, check_vma=False)
```

```python
import math

import jax
import jax.numpy as jnp
from jax import lax
from jax.experimental import pallas as pl
from jax.experimental.pallas import tpu as pltpu
from jax.sharding import PartitionSpec as P

LOG2E = 1.0 / math.log(2.0)
ROOT = math.sqrt(LOG2E)
CHUNK = 64
TAIL = 16
VMEM = pl.BlockSpec(memory_space=pltpu.VMEM)
SMEM = pl.BlockSpec(memory_space=pltpu.SMEM)
ANY = pl.BlockSpec(memory_space=pl.ANY)
PARAMS = pltpu.CompilerParams(vmem_limit_bytes=32 << 20)


def scaled(mon_ref, rating, base_ref, inverse_ref):
    blocks, width, scen = base_ref.shape
    for block in range(blocks):
        row = ROOT / rating[block : block + 1, :]
        inverse = jnp.transpose(jnp.broadcast_to(row, (scen, width)))
        rows = mon_ref[block * width : (block + 1) * width, :]
        inverse_ref[block] = inverse
        base_ref[block] = rows.astype(jnp.float32) * inverse


def prepare_kernel(
    mon_ref, rating_ref, info_ref, lodf_ref, shard_ref,
    base_ref, inverse_ref, packed_ref, lodf_out_ref, shard_out_ref
):
    scaled(mon_ref, rating_ref[...], base_ref, inverse_ref)
    rows, width = mon_ref.shape[0], rating_ref.shape[1]
    packed_ref[:rows, :] = mon_ref[...]
    parts, rest = [], rating_ref[...]
    for _ in range(3):
        part = rest.astype(jnp.bfloat16).astype(jnp.float32)
        parts.append(part)
        rest = rest - part
    parts.append(info_ref[...])
    blank = jnp.zeros((TAIL - 1 - 3 * rest.shape[0], width), jnp.float32)
    packed_ref[rows:, :] = jnp.concatenate(parts + [blank], axis=0).astype(packed_ref.dtype)
    lodf_out_ref[...] = lodf_ref[...]
    shard_out_ref[...] = shard_ref[...]


def tiles_kernel(slots, sources, ny, nz, loaded, early, added, *refs):
    place_ref = refs[0]
    info_refs = refs[1 : 1 + sources]
    refs = refs[1 + sources :]
    shard_refs, refs = refs[:loaded], refs[loaded:]
    lodf_refs, refs = refs[:sources], refs[sources:]
    own_base_ref, own_inverse_ref, weight_ref = refs[:3]
    refs = refs[3:]
    other_refs, refs = refs[: sources - 1], refs[sources - 1 :]
    before_refs, refs = refs[: 2 * added], refs[2 * added :]
    grad_mon_ref, grad_out_ref, work_ref, ratio_ref, sums_ref, flow_ref, base_ref = refs[:7]
    inverse_ref, tile_buf, flow_buf, tile_sem, flow_sem = refs[7:]
    width = tile_buf.shape[-1]
    scen = base_ref.shape[-1]
    per_shard = shard_refs[0].shape[0]
    blocks = own_base_ref.shape[0]

    def find(source, made):
        info_ref = info_refs[source]

        def look(slot, made):
            block = info_ref[1 + slots + slot]
            owner = block // per_shard
            apart = jnp.bitwise_xor(owner // ny, place_ref[0])
            rel_z = lax.rem(apart, 2) * (nz // 2) + apart // 2
            inner = lax.rem(block, per_shard)
            here = lax.rem(owner, ny) == place_ref[1]
            if early:
                here = jnp.logical_and(here, rel_z == 0)
            elif added and source == 0:
                here = jnp.logical_and(here, rel_z != 0)

            @pl.when(here)
            def fetch():
                work_ref[0, made] = source * blocks + info_ref[1 + slot]
                work_ref[1, made] = (rel_z * per_shard + inner) * width
                pltpu.make_async_copy(
                    lodf_refs[source].at[slot], tile_buf.at[made], tile_sem.at[made]
                ).start()
                for index in range(loaded):

                    @pl.when(rel_z == index)
                    def start_flow():
                        pltpu.make_async_copy(
                            shard_refs[index].at[inner], flow_buf.at[made], flow_sem.at[made]
                        ).start()

            return made + here.astype(jnp.int32)

        return lax.fori_loop(0, info_ref[0], look, made)

    count = jnp.int32(0)
    for source in range(sources):
        count = find(source, count)
    base_ref[:blocks] = own_base_ref[...]
    inverse_ref[:blocks] = own_inverse_ref[...]
    if sources > 1:
        other_ref = other_refs[0]
        parts = other_ref[blocks * width : blocks * width + TAIL, :].astype(jnp.float32)
        rating = parts[:blocks] + parts[blocks : 2 * blocks] + parts[2 * blocks : 3 * blocks]
        scaled(other_ref, rating, base_ref.at[blocks:], inverse_ref.at[blocks:])
    for index, ref in enumerate((grad_mon_ref, grad_out_ref)):
        ready = 0
        if added:
            ready = before_refs[index].shape[0]
            ref[:ready] = before_refs[index][...]
        if ready < ref.shape[0]:
            ref[ready:] = jnp.zeros((ref.shape[0] - ready,) + ref.shape[1:], ref.dtype)
    weight = weight_ref[...]

    def one_tile(item, unused):
        mon_block = work_ref[0, item]
        out_row = work_ref[1, item]
        pltpu.make_async_copy(lodf_refs[0].at[0], tile_buf.at[item], tile_sem.at[item]).wait()
        pltpu.make_async_copy(shard_refs[0].at[0], flow_buf.at[item], flow_sem.at[item]).wait()
        ratio_ref[...] = tile_buf[item].astype(jnp.float32) * inverse_ref[mon_block]
        flow_ref[...] = flow_buf[item].astype(jnp.float32)
        sums_ref[...] = jnp.zeros_like(sums_ref)

        def one_chunk(chunk, unused):
            rows = pl.ds(pl.multiple_of(chunk * CHUNK, CHUNK), CHUNK)
            ratio = ratio_ref[rows, :]
            base = base_ref[mon_block, rows, :]
            total = jnp.zeros_like(base)
            for k in range(width):
                coupling = jnp.broadcast_to(ratio[:, k : k + 1], (CHUNK, scen))
                p = base + coupling * flow_ref[k : k + 1, :]
                t = jnp.exp2(p * p)
                z = t + math.e
                d = ((jnp.log2(z) - LOG2E) * p) * (t * pl.reciprocal(z, approx=True))
                total = total + d
                part = jnp.sum((coupling * d).reshape(CHUNK // 8, 8, scen), axis=0)
                sums_ref[8 * k : 8 * k + 8, :] += part
            scale = inverse_ref[mon_block, rows, :] * weight
            grad_mon_ref[mon_block, rows, :] += total * scale
            return unused

        lax.fori_loop(0, width // CHUNK, one_chunk, 0)
        gradient = sums_ref[pl.ds(0, width, stride=8), :]
        for row in range(1, 8):
            gradient = gradient + sums_ref[pl.ds(row, width, stride=8), :]
        at = pl.ds(pl.multiple_of(out_row, width), width)
        grad_out_ref[at, :] += gradient * weight
        return unused

    lax.fori_loop(0, count, one_tile, 0)


def prepare(mon_flow, rating, info, tiles, shard):
    width, scen = tiles.shape[-1], mon_flow.shape[1]
    rows = mon_flow.shape[0]
    by_block = jax.ShapeDtypeStruct((rows // width, width, scen), jnp.float32)
    info = jnp.pad(info.astype(jnp.float32), (0, width - info.shape[0]))
    return pl.pallas_call(
        prepare_kernel,
        out_shape=(
            by_block,
            by_block,
            jax.ShapeDtypeStruct((rows + TAIL, scen), mon_flow.dtype),
            jax.ShapeDtypeStruct(tiles.shape, tiles.dtype),
            jax.ShapeDtypeStruct(shard.shape, shard.dtype),
        ),
        in_specs=[VMEM] * 5,
        out_specs=(VMEM,) * 5,
        compiler_params=PARAMS,
        cost_estimate=pl.CostEstimate(flops=1 << 22, bytes_accessed=4 << 20, transcendentals=0),
        name="prepare",
    )(mon_flow, rating.reshape(-1, width), info[None], tiles, shard)


def run_tiles(place, infos, shards, ny, nz, lodfs, prepared, weight, others, before=()):
    sources, loaded = len(lodfs), len(shards)
    early = loaded < nz
    slots, width, _ = lodfs[0].shape
    base, inverse = prepared
    blocks, _, scen = base.shape
    items = sources * slots
    elements = (1 if early else items // 2) * width * width * scen

    def body(*refs):
        tiles_kernel(slots, sources, ny, nz, loaded, early, len(before) // 2, *refs)

    return pl.pallas_call(
        body,
        out_shape=(
            jax.ShapeDtypeStruct((sources * blocks, width, scen), jnp.float32),
            jax.ShapeDtypeStruct((loaded * shards[0].shape[0] * width, scen), jnp.float32),
        ),
        in_specs=[SMEM] * (1 + sources)
        + [ANY] * (loaded + sources)
        + [VMEM] * (3 + len(others) + len(before)),
        out_specs=(VMEM, VMEM),
        scratch_shapes=[
            pltpu.SMEM((2, items), jnp.int32),
            pltpu.VMEM((width, width), jnp.float32),
            pltpu.VMEM((8 * width, scen), jnp.float32),
            pltpu.VMEM((width, scen), jnp.float32),
            pltpu.VMEM((sources * blocks, width, scen), jnp.float32),
            pltpu.VMEM((sources * blocks, width, scen), jnp.float32),
            pltpu.VMEM((items, width, width), lodfs[0].dtype),
            pltpu.VMEM((items, width, scen), shards[0].dtype),
            pltpu.SemaphoreType.DMA((items,)),
            pltpu.SemaphoreType.DMA((items,)),
        ],
        compiler_params=PARAMS,
        cost_estimate=pl.CostEstimate(
            flops=14 * elements, bytes_accessed=(4 if early else 64) << 20, transcendentals=2 * elements
        ),
        name="tiles",
    )(place, *infos, *shards, *lodfs, base, inverse, weight, *others, *before)


def pack_info(tile_mon, tile_out, tile_count):
    return jnp.concatenate([tile_count.reshape(-1), tile_mon.reshape(-1), tile_out.reshape(-1)])


def crossed(n_mon, ny, dy, dz):
    return [(i, (i // ny ^ dz) * ny + (i % ny ^ dy)) for i in range(n_mon)]


def local_pairs(n_mon, n_out, *args):
    ny, nz = 2, n_mon // 2
    mon_flow, out_flow, rating, weights, lodf, tile_mon, tile_out, tile_count = args
    width = lodf.shape[-1]
    rows, scen = mon_flow.shape
    beside = crossed(n_mon, ny, 1, 0)

    def across(part):
        return lax.ppermute(part, "mon", beside)

    own = out_flow[0].reshape(-1, width, scen)
    apart = [*range(0, nz, 2), *range(1, nz, 2)]
    arrived = [lax.ppermute(own, "mon", crossed(n_mon, ny, 0, r)) for r in apart[1:]]
    info = pack_info(tile_mon, tile_out, tile_count)
    tiles = lodf[0, 0]
    other_tiles = across(tiles)
    base, inverse, packed, tiles, own = prepare(mon_flow, rating, info, tiles, own)
    other = across(packed)
    other_info = other[rows + 3 * (rows // width), : info.shape[0]].astype(jnp.int32)
    me = lax.axis_index("mon")
    place = jnp.stack([me // ny, me % ny]).astype(jnp.int32)
    weight = (weights * (4.0 / width / LOG2E**2)).reshape(1, -1)
    prepared = base, inverse
    before = run_tiles(place, [info], [own], ny, nz, [tiles], prepared, weight, [])
    mon_part, out_part = run_tiles(
        place, [info, other_info], [own] + arrived, ny, nz, [tiles, other_tiles], prepared, weight,
        [other], before
    )
    out_part = out_part.reshape(nz, -1, scen)
    come = [
        lax.ppermute(out_part[place], "mon", crossed(n_mon, ny, 0, apart[place]))
        for place in range(1, nz)
    ]
    mon_part = mon_part.reshape(2, n_out, -1, scen)
    pieces = mon_part[0] + across(mon_part[1])
    mine = lax.axis_index("out")
    grad_mon = lax.dynamic_index_in_dim(pieces, mine, 0, keepdims=False)
    grad_out = out_part[0]
    for part in come:
        grad_out = grad_out + part
    grad_mon, grad_out = lax.optimization_barrier((grad_mon, grad_out))
    for r in range(1, n_out):
        piece = lax.dynamic_index_in_dim(pieces, (mine + r) % n_out, 0, keepdims=False)
        grad_mon = grad_mon + lax.ppermute(
            piece, "out", [(j, (j + r) % n_out) for j in range(n_out)]
        )
    return (grad_mon, grad_out[None])


def local_any(n_mon, n_out, *args):
    mon_flow, out_flow, rating, weights, lodf, tile_mon, tile_out, tile_count = args
    width = lodf.shape[-1]
    scen = mon_flow.shape[1]
    gathered = lax.all_gather(out_flow, "mon", axis=1, tiled=True)[0]
    shard = out_flow[0].reshape(-1, scen)
    info = pack_info(tile_mon, tile_out, tile_count)
    base, inverse, _, tiles, _ = prepare(mon_flow, rating, info, lodf[0, 0], shard)
    mon_part, out_part = run_tiles(
        jnp.zeros((2,), jnp.int32), [info],
        [gathered.reshape(-1, width, scen)], 1, 1, [tiles], (base, inverse),
        (weights * (4.0 / width / LOG2E**2)).reshape(1, -1), []
    )
    grad_out = lax.psum_scatter(
        out_part.reshape(1, -1, scen), "mon", scatter_dimension=1, tiled=True
    )
    grad_mon = lax.psum_scatter(
        mon_part.reshape(mon_flow.shape), "out", scatter_dimension=0, tiled=True
    )
    return (grad_mon, grad_out)


def solution(mesh):
    n_mon, n_out = mesh.shape["mon"], mesh.shape["out"]
    chosen = local_pairs if n_mon == 8 else local_any

    def local(*args):
        return chosen(n_mon, n_out, *args)

    in_specs = (
        P("mon", None),
        P("out", "mon", None),
        P("mon"),
        P(),
        P("mon", "out", None, None, None),
        P("mon", "out", None),
        P("mon", "out", None),
        P("mon", "out"),
    )
    out_specs = (P(("mon", "out"), None), P("out", "mon", None))
    return jax.shard_map(local, mesh=mesh, in_specs=in_specs, out_specs=out_specs, check_vma=False)
```

```python
import math

import jax
import jax.numpy as jnp
from jax import lax
from jax.experimental import pallas as pl
from jax.experimental.pallas import tpu as pltpu
from jax.sharding import PartitionSpec as P

LOG2E = 1.0 / math.log(2.0)
ROOT = math.sqrt(LOG2E)
CHUNK = 64
TAIL = 16
VMEM = pl.BlockSpec(memory_space=pltpu.VMEM)
SMEM = pl.BlockSpec(memory_space=pltpu.SMEM)
ANY = pl.BlockSpec(memory_space=pl.ANY)
PARAMS = pltpu.CompilerParams(vmem_limit_bytes=32 << 20)


def scaled(mon_ref, rating, base_ref, inverse_ref):
    blocks, width, scen = base_ref.shape
    for block in range(blocks):
        row = ROOT / rating[block : block + 1, :]
        inverse = jnp.transpose(jnp.broadcast_to(row, (scen, width)))
        rows = mon_ref[block * width : (block + 1) * width, :]
        inverse_ref[block] = inverse
        base_ref[block] = rows.astype(jnp.float32) * inverse


def prepare_kernel(
    mon_ref, rating_ref, info_ref, lodf_ref, shard_ref,
    base_ref, inverse_ref, packed_ref, lodf_out_ref, shard_out_ref
):
    scaled(mon_ref, rating_ref[...], base_ref, inverse_ref)
    rows, width = mon_ref.shape[0], rating_ref.shape[1]
    packed_ref[:rows, :] = mon_ref[...]
    parts, rest = [], rating_ref[...]
    for _ in range(3):
        part = rest.astype(jnp.bfloat16).astype(jnp.float32)
        parts.append(part)
        rest = rest - part
    parts.append(info_ref[...])
    blank = jnp.zeros((TAIL - 1 - 3 * rest.shape[0], width), jnp.float32)
    packed_ref[rows:, :] = jnp.concatenate(parts + [blank], axis=0).astype(packed_ref.dtype)
    lodf_out_ref[...] = lodf_ref[...]
    shard_out_ref[...] = shard_ref[...]


def tiles_kernel(slots, sources, ny, nz, loaded, early, added, *refs):
    place_ref = refs[0]
    info_refs = refs[1 : 1 + sources]
    refs = refs[1 + sources :]
    shard_refs, refs = refs[:loaded], refs[loaded:]
    lodf_refs, refs = refs[:sources], refs[sources:]
    own_base_ref, own_inverse_ref, weight_ref = refs[:3]
    refs = refs[3:]
    other_refs, refs = refs[: sources - 1], refs[sources - 1 :]
    before_refs, refs = refs[: 2 * added], refs[2 * added :]
    grad_mon_ref, grad_out_ref, work_ref, ratio_ref, sums_ref, flow_ref, base_ref = refs[:7]
    inverse_ref, tile_buf, flow_buf, tile_sem, flow_sem = refs[7:]
    width = tile_buf.shape[-1]
    height = CHUNK // 2 if early else CHUNK
    scen = base_ref.shape[-1]
    per_shard = shard_refs[0].shape[0]
    blocks = own_base_ref.shape[0]

    def find(source, made):
        info_ref = info_refs[source]

        def look(slot, made):
            block = info_ref[1 + slots + slot]
            owner = block // per_shard
            apart = jnp.bitwise_xor(owner // ny, place_ref[0])
            rel_z = lax.rem(apart, 2) * (nz // 2) + apart // 2
            inner = lax.rem(block, per_shard)
            here = lax.rem(owner, ny) == place_ref[1]
            if early:
                here = jnp.logical_and(here, rel_z == 0)
            elif added and source == 0:
                here = jnp.logical_and(here, rel_z != 0)

            @pl.when(here)
            def fetch():
                work_ref[0, made] = source * blocks + info_ref[1 + slot]
                work_ref[1, made] = (rel_z * per_shard + inner) * width
                pltpu.make_async_copy(
                    lodf_refs[source].at[slot], tile_buf.at[made], tile_sem.at[made]
                ).start()
                for index in range(loaded):

                    @pl.when(rel_z == index)
                    def start_flow():
                        pltpu.make_async_copy(
                            shard_refs[index].at[inner], flow_buf.at[made], flow_sem.at[made]
                        ).start()

            return made + here.astype(jnp.int32)

        return lax.fori_loop(0, info_ref[0], look, made)

    count = jnp.int32(0)
    for source in range(sources):
        count = find(source, count)
    base_ref[:blocks] = own_base_ref[...]
    inverse_ref[:blocks] = own_inverse_ref[...]
    if sources > 1:
        other_ref = other_refs[0]
        parts = other_ref[blocks * width : blocks * width + TAIL, :].astype(jnp.float32)
        rating = parts[:blocks] + parts[blocks : 2 * blocks] + parts[2 * blocks : 3 * blocks]
        scaled(other_ref, rating, base_ref.at[blocks:], inverse_ref.at[blocks:])
    for index, ref in enumerate((grad_mon_ref, grad_out_ref)):
        ready = 0
        if added:
            ready = before_refs[index].shape[0]
            ref[:ready] = before_refs[index][...]
        if ready < ref.shape[0]:
            ref[ready:] = jnp.zeros((ref.shape[0] - ready,) + ref.shape[1:], ref.dtype)
    weight = weight_ref[...]

    def one_tile(item, unused):
        mon_block = work_ref[0, item]
        out_row = work_ref[1, item]
        pltpu.make_async_copy(lodf_refs[0].at[0], tile_buf.at[item], tile_sem.at[item]).wait()
        pltpu.make_async_copy(shard_refs[0].at[0], flow_buf.at[item], flow_sem.at[item]).wait()
        ratio_ref[...] = tile_buf[item].astype(jnp.float32) * inverse_ref[mon_block]
        flow_ref[...] = flow_buf[item].astype(jnp.float32)
        sums_ref[...] = jnp.zeros_like(sums_ref)

        def one_chunk(chunk, unused):
            rows = pl.ds(pl.multiple_of(chunk * height, height), height)
            ratio = ratio_ref[rows, :]
            base = base_ref[mon_block, rows, :]
            total = jnp.zeros_like(base)
            for k in range(width):
                coupling = jnp.broadcast_to(ratio[:, k : k + 1], (height, scen))
                p = base + coupling * flow_ref[k : k + 1, :]
                t = jnp.exp2(p * p)
                z = t + math.e
                d = ((jnp.log2(z) - LOG2E) * p) * (t * pl.reciprocal(z, approx=True))
                total = total + d
                part = jnp.sum((coupling * d).reshape(height // 8, 8, scen), axis=0)
                sums_ref[8 * k : 8 * k + 8, :] += part
            scale = inverse_ref[mon_block, rows, :] * weight
            grad_mon_ref[mon_block, rows, :] += total * scale
            return unused

        lax.fori_loop(0, width // height, one_chunk, 0)
        gradient = sums_ref[pl.ds(0, width, stride=8), :]
        for row in range(1, 8):
            gradient = gradient + sums_ref[pl.ds(row, width, stride=8), :]
        at = pl.ds(pl.multiple_of(out_row, width), width)
        grad_out_ref[at, :] += gradient * weight
        return unused

    lax.fori_loop(0, count, one_tile, 0)


def prepare(mon_flow, rating, info, tiles, shard):
    width, scen = tiles.shape[-1], mon_flow.shape[1]
    rows = mon_flow.shape[0]
    by_block = jax.ShapeDtypeStruct((rows // width, width, scen), jnp.float32)
    info = jnp.pad(info.astype(jnp.float32), (0, width - info.shape[0]))
    return pl.pallas_call(
        prepare_kernel,
        out_shape=(
            by_block,
            by_block,
            jax.ShapeDtypeStruct((rows + TAIL, scen), mon_flow.dtype),
            jax.ShapeDtypeStruct(tiles.shape, tiles.dtype),
            jax.ShapeDtypeStruct(shard.shape, shard.dtype),
        ),
        in_specs=[VMEM] * 5,
        out_specs=(VMEM,) * 5,
        compiler_params=PARAMS,
        cost_estimate=pl.CostEstimate(flops=1 << 22, bytes_accessed=4 << 20, transcendentals=0),
        name="prepare",
    )(mon_flow, rating.reshape(-1, width), info[None], tiles, shard)


def run_tiles(place, infos, shards, ny, nz, lodfs, prepared, weight, others, before=()):
    sources, loaded = len(lodfs), len(shards)
    early = loaded < nz
    slots, width, _ = lodfs[0].shape
    base, inverse = prepared
    blocks, _, scen = base.shape
    items = sources * slots
    elements = (1 if early else items // 2) * width * width * scen

    def body(*refs):
        tiles_kernel(slots, sources, ny, nz, loaded, early, len(before) // 2, *refs)

    return pl.pallas_call(
        body,
        out_shape=(
            jax.ShapeDtypeStruct((sources * blocks, width, scen), jnp.float32),
            jax.ShapeDtypeStruct((loaded * shards[0].shape[0] * width, scen), jnp.float32),
        ),
        in_specs=[SMEM] * (1 + sources)
        + [ANY] * (loaded + sources)
        + [VMEM] * (3 + len(others) + len(before)),
        out_specs=(VMEM, VMEM),
        scratch_shapes=[
            pltpu.SMEM((2, items), jnp.int32),
            pltpu.VMEM((width, width), jnp.float32),
            pltpu.VMEM((8 * width, scen), jnp.float32),
            pltpu.VMEM((width, scen), jnp.float32),
            pltpu.VMEM((sources * blocks, width, scen), jnp.float32),
            pltpu.VMEM((sources * blocks, width, scen), jnp.float32),
            pltpu.VMEM((items, width, width), lodfs[0].dtype),
            pltpu.VMEM((items, width, scen), shards[0].dtype),
            pltpu.SemaphoreType.DMA((items,)),
            pltpu.SemaphoreType.DMA((items,)),
        ],
        compiler_params=PARAMS,
        cost_estimate=pl.CostEstimate(
            flops=14 * elements, bytes_accessed=(4 if early else 64) << 20, transcendentals=2 * elements
        ),
        name="tiles",
    )(place, *infos, *shards, *lodfs, base, inverse, weight, *others, *before)


def pack_info(tile_mon, tile_out, tile_count):
    return jnp.concatenate([tile_count.reshape(-1), tile_mon.reshape(-1), tile_out.reshape(-1)])


def crossed(n_mon, ny, dy, dz):
    return [(i, (i // ny ^ dz) * ny + (i % ny ^ dy)) for i in range(n_mon)]


def local_pairs(n_mon, n_out, *args):
    ny, nz = 2, n_mon // 2
    mon_flow, out_flow, rating, weights, lodf, tile_mon, tile_out, tile_count = args
    width = lodf.shape[-1]
    rows, scen = mon_flow.shape
    beside = crossed(n_mon, ny, 1, 0)

    def across(part):
        return lax.ppermute(part, "mon", beside)

    own = out_flow[0].reshape(-1, width, scen)
    apart = [*range(0, nz, 2), *range(1, nz, 2)]
    arrived = [lax.ppermute(own, "mon", crossed(n_mon, ny, 0, r)) for r in apart[1:]]
    info = pack_info(tile_mon, tile_out, tile_count)
    tiles = lodf[0, 0]
    other_tiles = across(tiles)
    base, inverse, packed, tiles, own = prepare(mon_flow, rating, info, tiles, own)
    other = across(packed)
    other_info = other[rows + 3 * (rows // width), : info.shape[0]].astype(jnp.int32)
    me = lax.axis_index("mon")
    place = jnp.stack([me // ny, me % ny]).astype(jnp.int32)
    weight = (weights * (4.0 / width / LOG2E**2)).reshape(1, -1)
    prepared = base, inverse
    before = run_tiles(place, [info], [own], ny, nz, [tiles], prepared, weight, [])
    mon_part, out_part = run_tiles(
        place, [info, other_info], [own] + arrived, ny, nz, [tiles, other_tiles], prepared, weight,
        [other], before
    )
    out_part = out_part.reshape(nz, -1, scen)
    come = [
        lax.ppermute(out_part[place], "mon", crossed(n_mon, ny, 0, apart[place]))
        for place in range(1, nz)
    ]
    mon_part = mon_part.reshape(2, n_out, -1, scen)
    pieces = mon_part[0] + across(mon_part[1])
    mine = lax.axis_index("out")
    grad_mon = lax.dynamic_index_in_dim(pieces, mine, 0, keepdims=False)
    grad_out = out_part[0]
    for part in come:
        grad_out = grad_out + part
    grad_mon, grad_out = lax.optimization_barrier((grad_mon, grad_out))
    for r in range(1, n_out):
        piece = lax.dynamic_index_in_dim(pieces, (mine + r) % n_out, 0, keepdims=False)
        grad_mon = grad_mon + lax.ppermute(
            piece, "out", [(j, (j + r) % n_out) for j in range(n_out)]
        )
    return (grad_mon, grad_out[None])


def local_any(n_mon, n_out, *args):
    mon_flow, out_flow, rating, weights, lodf, tile_mon, tile_out, tile_count = args
    width = lodf.shape[-1]
    scen = mon_flow.shape[1]
    gathered = lax.all_gather(out_flow, "mon", axis=1, tiled=True)[0]
    shard = out_flow[0].reshape(-1, scen)
    info = pack_info(tile_mon, tile_out, tile_count)
    base, inverse, _, tiles, _ = prepare(mon_flow, rating, info, lodf[0, 0], shard)
    mon_part, out_part = run_tiles(
        jnp.zeros((2,), jnp.int32), [info],
        [gathered.reshape(-1, width, scen)], 1, 1, [tiles], (base, inverse),
        (weights * (4.0 / width / LOG2E**2)).reshape(1, -1), []
    )
    grad_out = lax.psum_scatter(
        out_part.reshape(1, -1, scen), "mon", scatter_dimension=1, tiled=True
    )
    grad_mon = lax.psum_scatter(
        mon_part.reshape(mon_flow.shape), "out", scatter_dimension=0, tiled=True
    )
    return (grad_mon, grad_out)


def solution(mesh):
    n_mon, n_out = mesh.shape["mon"], mesh.shape["out"]
    chosen = local_pairs if n_mon == 8 else local_any

    def local(*args):
        return chosen(n_mon, n_out, *args)

    in_specs = (
        P("mon", None),
        P("out", "mon", None),
        P("mon"),
        P(),
        P("mon", "out", None, None, None),
        P("mon", "out", None),
        P("mon", "out", None),
        P("mon", "out"),
    )
    out_specs = (P(("mon", "out"), None), P("out", "mon", None))
    return jax.shard_map(local, mesh=mesh, in_specs=in_specs, out_specs=out_specs, check_vma=False)
```
